128 devices in a mesh: tm: 16 (over y_lo, z, core), rows: 8 (over y_hi, x).
Axes of the slice: x: 4, y: 4 (y_hi: 2, y_lo: 2; y = y_hi * 2 + y_lo), z: 4, core: 2. Of those that a mesh axis runs over, the one named last changes fastest.
Arguments:
- activations: bfloat16 [128, 32, 32, 384], P('tm', 'rows'), may hold values from -27 to 27
- frame_counts: int32 [16], replicated, may hold values from 1 to 8, as said below
- norm_gain: float32 [384], replicated, may hold values from 0.5 to 1.5
- norm_bias: float32 [384], replicated, may hold values from -3 to 3
- conv_weight: bfloat16 [10368, 384], replicated, may hold values from -0.0625 to 0.0625
- cotangent: bfloat16 [128, 32, 32, 384], P('tm', 'rows'), may hold values from -6 to 6
Outputs:
- block_out: bfloat16 [128, 32, 32, 384], P('tm', 'rows')
- input_grad: float32 [128, 32, 32, 384], P('tm', 'rows')
- weight_grad: float32 [10368, 384], P(('tm', 'rows'))
The draws below stay inside these ranges and needn't reach their ends.
Inputs may be any that keep to these rules, and one draw needn't show every extreme that they name: `frame_counts`: entry 0 is 1; every other entry is 4 or 8, and 8 occurs; the entries sum to 89.
All inputs are finite; a program needn't handle non-finite values.
Results may differ from the reference program's by a relative error of at most 0.0028.
Values may be sent and summed in bfloat16 or wider, within the bound.
No kernel may reach another device: no remote copies, remote signals or barrier semaphores. Data moves between devices by JAX's collectives and lax.ppermute only.
A program may use at most 256 MiB of HBM per device.

```python
import math
import jax
import jax.numpy as jnp
from jax import lax

C = 384
GROUPS = 32
CAP = 8
W = 32
GRP = 22
FRAMES = 89
SLOTS = 128
H = 32
N_TM = 16


def draw_activations(key, part):
    key = jax.random.fold_in(key, 11)
    sub_keys = jax.random.split(key, 3)
    full_shape = (SLOTS, H, W, C)
    rough_part = jnp.clip(jax.random.normal(sub_keys[0], full_shape, jnp.float32), -4.0, 4.0)
    offset = 0.5 * jnp.clip(jax.random.normal(sub_keys[1], (SLOTS, 1, 1, C), jnp.float32), -4.0, 4.0)
    row_scale = 1.0 + 2.0 * jnp.arange(H, dtype=jnp.float32)[None, :, None, None] / max(H - 1, 1)
    frame_scale = jnp.exp(jax.random.uniform(sub_keys[2], (SLOTS, 1, 1, 1), jnp.float32, -0.7, 0.7))
    return (rough_part * row_scale * frame_scale + offset).astype(jnp.bfloat16)


def draw_frame_counts(key, part):
    key = jax.random.fold_in(key, 12)
    ranking = jax.random.permutation(key, N_TM - 1)
    surplus = GRP - (N_TM - 1)
    group_num = 1 + (ranking < surplus).astype(jnp.int32)
    return jnp.concatenate([jnp.ones((1,), jnp.int32), 4 * group_num]).astype(jnp.int32)


def steps_of(stream_key, dims, pieces, least, largest):
    loudness, own = 1.0, jax.random.fold_in(stream_key, 6)
    for axis_at, parts in pieces:
        draws = jnp.exp(jax.random.uniform(jax.random.fold_in(own, axis_at), (parts,), jnp.float32, least / len(pieces), largest / len(pieces)))
        loudness = loudness * jnp.repeat(draws, dims[axis_at] // parts).reshape([-1 if axis == axis_at else 1 for axis in range(len(dims))])
    return loudness


def bell_draw(rng, extent, deviation, limit, cuts=(), kind=jnp.bfloat16):
    drawn = deviation * jax.random.normal(rng, extent, jnp.float32)
    if cuts:
        drawn = drawn * steps_of(rng, extent, cuts, -0.22, 0.18)
    return jnp.clip(drawn, -limit, limit).astype(kind)


def setup_inputs(seed: int = 0) -> dict:
    key_of = jax.random.split(jax.random.key(seed), 7)
    return {
        "activations": draw_activations(jax.random.fold_in(key_of[6], 71), 0),
        "frame_counts": draw_frame_counts(jax.random.fold_in(key_of[6], 71), 0),
        "norm_gain": jnp.clip(1.0 + 0.1 * jax.random.normal(key_of[2], (C,), jnp.float32), 0.5, 1.5),
        "norm_bias": bell_draw(key_of[3], (C,), 0.5, 3.0, (), jnp.float32),
        "conv_weight": bell_draw(key_of[4], (27 * C, C), (27 * C) ** -0.5, 0.0625),
        "cotangent": bell_draw(key_of[5], (SLOTS, H, W, C), 1.0, 6.0, ((0, 16), (1, 8))),
    }


EPS = 1e-05

def clip_layout(frame_counts):
    starts = jnp.cumsum(frame_counts) - frame_counts
    slot_ids = jnp.arange(SLOTS, dtype=jnp.int32)
    owner_ids = slot_ids // CAP
    local_ids = slot_ids % CAP
    is_valid = local_ids < frame_counts[owner_ids]
    return jnp.where(is_valid, starts[owner_ids] + local_ids, FRAMES).astype(jnp.int32)

def to_clip(values_in, position):
    canvas = jnp.zeros((FRAMES + 1,) + values_in.shape[1:], values_in.dtype)
    return canvas.at[position].set(values_in)[:FRAMES]

def to_slots(values_in, position):
    padded = jnp.concatenate([values_in, jnp.zeros((1,) + values_in.shape[1:], values_in.dtype)], axis=0)
    return padded[position]

def tap_sum(padded, kernel, frames, flipped):
    running = jnp.zeros((frames * H * W, C), jnp.float32)
    for tap_id in range(27):
        t_off, r_off, w_off = (tap_id // 9, tap_id // 3 % 3, tap_id % 3)
        tap_block = kernel[tap_id * C:(tap_id + 1) * C]
        if flipped:
            tap_piece = padded[2 - t_off:2 - t_off + frames, 2 - r_off:2 - r_off + H, 2 - w_off:2 - w_off + W]
            running = running + lax.dot_general(tap_piece.reshape(-1, C), tap_block, (((1,), (1,)), ((), ())), preferred_element_type=jnp.float32)
        else:
            tap_piece = padded[t_off:t_off + frames, r_off:r_off + H, w_off:w_off + W]
            running = running + jnp.dot(tap_piece.reshape(-1, C), tap_block, preferred_element_type=jnp.float32)
    return running

def reference(activations, frame_counts, norm_gain, norm_bias, conv_weight, cotangent):
    position = clip_layout(frame_counts)
    clip = to_clip(activations, position).astype(jnp.float32)
    cot_clip = to_clip(cotangent, position)
    grouped_shape = (FRAMES, H, W, GROUPS, C // GROUPS)
    cell_count = H * W * (C // GROUPS)
    grouped = clip.reshape(grouped_shape)
    group_mean = lax.optimization_barrier(jnp.sum(grouped, axis=(1, 2, 4))) / cell_count
    square = lax.optimization_barrier(jnp.sum(grouped * grouped, axis=(1, 2, 4))) / cell_count
    inv_std = lax.rsqrt(square - group_mean * group_mean + EPS)
    centred = (grouped - group_mean[:, None, None, :, None]) * inv_std[:, None, None, :, None]
    centred = centred.reshape(clip.shape)
    pre_act = centred * norm_gain + norm_bias
    hidden = jax.nn.silu(pre_act).astype(jnp.bfloat16)
    padded = jnp.pad(hidden, ((2, 0), (1, 1), (1, 1), (0, 0)))
    conv_out = tap_sum(padded, conv_weight, FRAMES, False).reshape(clip.shape)
    block_out = (clip + conv_out).astype(jnp.bfloat16)
    grad_pad = jnp.pad(cot_clip, ((0, 2), (1, 1), (1, 1), (0, 0)))
    hidden_grad = tap_sum(grad_pad, conv_weight, FRAMES, True).reshape(clip.shape)
    gate_sig = jax.nn.sigmoid(pre_act)
    pre_grad = hidden_grad * gate_sig * (1.0 + pre_act * (1.0 - gate_sig)) * norm_gain
    first_avg = lax.optimization_barrier(jnp.sum(pre_grad.reshape(grouped_shape), axis=(1, 2, 4))) / cell_count
    second_avg = lax.optimization_barrier(jnp.sum((pre_grad * centred).reshape(grouped_shape), axis=(1, 2, 4))) / cell_count
    centred_grad = pre_grad.reshape(grouped_shape) - first_avg[:, None, None, :, None] - centred.reshape(grouped_shape) * second_avg[:, None, None, :, None]
    input_grad = cot_clip.astype(jnp.float32) + (centred_grad * inv_std[:, None, None, :, None]).reshape(clip.shape)
    grad_scale = 1.0 / math.sqrt(FRAMES * H * W)
    flat_grads = cot_clip.reshape(-1, C)
    blocks = []
    for tap_id in range(27):
        t_off, r_off, w_off = (tap_id // 9, tap_id // 3 % 3, tap_id % 3)
        tap_piece = padded[t_off:t_off + FRAMES, r_off:r_off + H, w_off:w_off + W].reshape(-1, C)
        blocks.append(lax.dot_general(tap_piece, flat_grads, (((0,), (0,)), ((), ())), preferred_element_type=jnp.float32) * grad_scale)
    weight_grad = jnp.concatenate(blocks, axis=0)
    return (to_slots(block_out, position), to_slots(input_grad, position), weight_grad)
```

```python
import functools
import math

import jax
import jax.numpy as jnp
from jax import lax
from jax.experimental import pallas as pl
from jax.experimental.pallas import tpu as pltpu
from jax.sharding import Mesh
from jax.sharding import PartitionSpec as P

GROUPS = 32
EPS = 1e-05
CHAN = 384
HALF = CHAN // 2
SLOTS = 8
ROWS = 4
COLS = 32
CELLS = ROWS * COLS
POS = SLOTS * CELLS
WIDE = 3 * CHAN
PIECE = 81
SENT = 88
CHIPS = 64

TM = ("ylo", "z", "core")
ROW_AXES = ("yhi", "x")
CHIP_AXES = ("ylo", "z", "yhi", "x")
ALL_AXES = TM + ROW_AXES

bf16 = jnp.bfloat16
f32 = jnp.float32
VMEM_LIMIT = pltpu.CompilerParams(vmem_limit_bytes=60 * 1024 * 1024)


def from_left(values):
    col = lax.broadcasted_iota(jnp.int32, values.shape, 0) % COLS
    return jnp.where(col == 0, 0.0, pltpu.roll(values, 1, 0))


def from_right(values):
    col = lax.broadcasted_iota(jnp.int32, values.shape, 0) % COLS
    return jnp.where(col == COLS - 1, 0.0, pltpu.roll(values, values.shape[0] - 1, 0))


def tap_products(x_ref, w_ref, acc, back):
    step = pl.program_id(0)
    weights = w_ref[...]
    pieces = []
    for b in range(3):
        at = (2 - step, 2 - b) if back else (step, b)
        pieces.append(x_ref[pl.ds(at[0], SLOTS), pl.ds(at[1], ROWS)].reshape(POS, CHAN))
    left = jnp.concatenate(pieces, axis=1)
    if back:
        right = jnp.concatenate([weights[b * WIDE : (b + 1) * WIDE] for b in range(3)], axis=1)
        dims = (((1,), (1,)), ((), ()))
    else:
        right = jnp.concatenate(
            [
                jnp.concatenate(
                    [weights[(b * 3 + c) * CHAN : (b * 3 + c + 1) * CHAN] for c in range(3)], axis=1
                )
                for b in range(3)
            ],
            axis=0,
        )
        dims = (((1,), (0,)), ((), ()))
    product = lax.dot_general(left, right, dims, preferred_element_type=f32)

    @pl.when(step == 0)
    def _():
        acc[...] = product

    @pl.when(step > 0)
    def _():
        acc[...] += product


def forward_kernel(count_ref, x_ref, w_ref, act_ref, out_ref, acc):
    tap_products(x_ref, w_ref, acc, False)

    @pl.when(pl.program_id(0) == 2)
    def _():
        for frame in range(SLOTS):
            rows = slice(frame * CELLS, (frame + 1) * CELLS)
            conv = (
                acc[rows, CHAN : 2 * CHAN]
                + from_left(acc[rows, :CHAN])
                + from_right(acc[rows, 2 * CHAN :])
            )
            total = act_ref[rows].astype(f32) + conv
            out_ref[rows] = jnp.where(frame < count_ref[0], total, 0.0).astype(bf16)


def backward_kernel(
    x_ref, w_ref, act_ref, mean_ref, inv_ref, gain_ref, bias_ref, out_ref, first_ref, second_ref, acc
):
    tap_products(x_ref, w_ref, acc, True)

    @pl.when(pl.program_id(0) == 2)
    def _():
        gain = gain_ref[...]
        bias = bias_ref[...]
        for frame in range(SLOTS):
            rows = slice(frame * CELLS, (frame + 1) * CELLS)
            grad = (
                acc[rows, CHAN : 2 * CHAN]
                + from_right(acc[rows, :CHAN])
                + from_left(acc[rows, 2 * CHAN :])
            )
            centred = (act_ref[rows].astype(f32) - mean_ref[frame : frame + 1]) * inv_ref[
                frame : frame + 1
            ]
            pre_act = centred * gain + bias
            gate = jax.nn.sigmoid(pre_act)
            pre_grad = grad * gate * (1.0 + pre_act * (1.0 - gate)) * gain
            out_ref[rows] = pre_grad
            first_ref[frame : frame + 1] = jnp.sum(pre_grad, axis=0, keepdims=True)
            second_ref[frame : frame + 1] = jnp.sum(pre_grad * centred, axis=0, keepdims=True)


def weight_kernel(h0_ref, h1_ref, c0_ref, c1_ref, out_ref, turned, sums):
    step = pl.program_id(0)

    @pl.when(step == 0)
    def _():
        for half, h_ref in enumerate((h0_ref, h1_ref)):

            def turn(m, carry, h_ref=h_ref, half=half):
                values = h_ref[pl.ds(pl.multiple_of(m * 256, 256), 256)].astype(f32)
                cols = pl.ds(pl.multiple_of(half * POS + m * 256, 256), 256)
                for c, moved in enumerate((from_left(values), values, from_right(values))):
                    turned[c * CHAN : (c + 1) * CHAN, cols] = moved.T.astype(bf16)
                return carry

            lax.fori_loop(0, POS // 256, turn, 0)

    a, b = step // 3, step % 3
    right = jnp.concatenate(
        [
            ref[pl.ds(2 - a, SLOTS), pl.ds(2 - b, ROWS)].reshape(POS, HALF)
            for ref in (c0_ref, c1_ref)
        ],
        axis=0,
    )
    sums[pl.ds(pl.multiple_of(step * WIDE, WIDE), WIDE)] = jnp.dot(
        turned[...], right, preferred_element_type=f32
    )

    @pl.when(step == 8)
    def _():
        def pack(j, carry):
            row = j % 8
            first = (j // 8) * 16 + row
            for core in range(2):
                start = pl.multiple_of(PIECE * (first + 8 * core) - row, 8)
                out_ref[j, :, core * HALF : (core + 1) * HALF] = sums[pl.ds(start, SENT)].astype(
                    bf16
                )
            return carry

        lax.fori_loop(0, CHIPS, pack, 0)


def whole(shape):
    return pl.BlockSpec(shape, lambda step: (0,) * len(shape))


def cost(flops, moved):
    return pl.CostEstimate(flops=flops, bytes_accessed=moved, transcendentals=0)


FLOPS = 2 * POS * 27 * CHAN * CHAN
TAPS_SPEC = pl.BlockSpec((3 * WIDE, CHAN), lambda step: (step, 0))


def forward_conv(count, extended, weights, act):
    return pl.pallas_call(
        forward_kernel,
        out_shape=jax.ShapeDtypeStruct((POS, CHAN), bf16),
        grid=(3,),
        in_specs=[
            pl.BlockSpec(memory_space=pltpu.SMEM),
            whole(extended.shape),
            TAPS_SPEC,
            whole(act.shape),
        ],
        out_specs=whole((POS, CHAN)),
        scratch_shapes=[pltpu.VMEM((POS, WIDE), f32)],
        compiler_params=VMEM_LIMIT,
        cost_estimate=cost(FLOPS, 12 << 20),
        name="forward_conv",
    )(count, extended, weights, act)


def backward_conv(extended, weights, act, mean, inv, gain, bias):
    return pl.pallas_call(
        backward_kernel,
        out_shape=(
            jax.ShapeDtypeStruct((POS, CHAN), f32),
            jax.ShapeDtypeStruct((SLOTS, CHAN), f32),
            jax.ShapeDtypeStruct((SLOTS, CHAN), f32),
        ),
        grid=(3,),
        in_specs=[
            whole(extended.shape),
            TAPS_SPEC,
            whole(act.shape),
            whole(mean.shape),
            whole(inv.shape),
            whole(gain.shape),
            whole(bias.shape),
        ],
        out_specs=(whole((POS, CHAN)), whole((SLOTS, CHAN)), whole((SLOTS, CHAN))),
        scratch_shapes=[pltpu.VMEM((POS, WIDE), f32)],
        compiler_params=VMEM_LIMIT,
        cost_estimate=cost(FLOPS, 12 << 20),
        name="backward_conv",
    )(extended, weights, act, mean, inv, gain, bias)


def weight_terms(hidden, other_hidden, cots, other_cots):
    return pl.pallas_call(
        weight_kernel,
        out_shape=jax.ShapeDtypeStruct((CHIPS, SENT, CHAN), bf16),
        grid=(9,),
        in_specs=[
            whole(hidden.shape),
            whole(other_hidden.shape),
            whole(cots.shape),
            whole(other_cots.shape),
        ],
        out_specs=whole((CHIPS, SENT, CHAN)),
        scratch_shapes=[
            pltpu.VMEM((WIDE, 2 * POS), bf16),
            pltpu.VMEM((9 * WIDE, HALF), f32),
        ],
        compiler_params=VMEM_LIMIT,
        cost_estimate=cost(FLOPS, 12 << 20),
        name="weight_terms",
    )(hidden, other_hidden, cots, other_cots)


def shift(values, axes, count, step):
    pairs = [(i, i + step) for i in range(count) if 0 <= i + step < count]
    return lax.ppermute(values, axes, pairs)


def swap_cores(values):
    return lax.ppermute(values, "core", [(0, 1), (1, 0)])


def with_rows(block):
    low = shift(block[:, ROWS - 1 :], ROW_AXES, 8, 1)
    high = shift(block[:, :1], ROW_AXES, 8, -1)
    return jnp.concatenate([low, block, high], axis=1)


def over_rows(first, second):
    grouped = jnp.concatenate([first, second], axis=0).reshape(2 * SLOTS, GROUPS, CHAN // GROUPS)
    sums = jnp.sum(grouped, axis=2)
    spread = jnp.broadcast_to(sums[None], (8,) + sums.shape)
    total = jnp.sum(lax.all_to_all(spread, ROW_AXES, 0, 0), axis=0)
    return total[:SLOTS], total[SLOTS:]


def per_channel(grouped):
    return jnp.repeat(grouped, CHAN // GROUPS, axis=1)


def on_device(activations, frame_counts, norm_gain, norm_bias, conv_weight, cotangent):
    tm_place = lax.axis_index(TM)
    core = lax.axis_index("core")
    row_place = lax.axis_index(ROW_AXES)
    count = frame_counts[tm_place]
    live = (jnp.arange(SLOTS) < count)[:, None, None, None]
    cell_count = 8 * CELLS * (CHAN // GROUPS)
    act = activations.reshape(POS, CHAN)
    zero_pair = jnp.zeros((2, ROWS, COLS, CHAN), bf16)

    values = activations.astype(f32)
    first_sum, second_sum = over_rows(
        jnp.sum(values, axis=(1, 2)), jnp.sum(values * values, axis=(1, 2))
    )

    grads = jnp.where(live, cotangent, jnp.zeros_like(cotangent))
    next_head = shift(grads[:2], TM, 16, -1)
    future = lax.dynamic_update_slice_in_dim(
        jnp.concatenate([grads, zero_pair], 0), next_head, count, 0
    )
    cots = with_rows(future)
    cots_here = lax.dynamic_slice_in_dim(cots, core * HALF, HALF, 3)
    cots_there = swap_cores(lax.dynamic_slice_in_dim(cots, (1 - core) * HALF, HALF, 3))

    group_mean = first_sum / cell_count
    inv_std = lax.rsqrt(second_sum / cell_count - group_mean * group_mean + EPS)
    mean = per_channel(group_mean)
    inv = per_channel(inv_std)
    centred = (values - mean[:, None, None, :]) * inv[:, None, None, :]
    pre_act = centred * norm_gain + norm_bias
    hidden = jnp.where(live, jax.nn.silu(pre_act), 0.0).astype(bf16)

    terms = weight_terms(
        hidden.reshape(POS, CHAN),
        swap_cores(hidden).reshape(POS, CHAN),
        cots_here,
        cots_there,
    )
    arrived = lax.all_to_all(terms, CHIP_AXES, 0, 0)

    pre_grad, first_grad, second_grad = backward_conv(
        cots, conv_weight, act, mean, inv, norm_gain[None], norm_bias[None]
    )
    first_grad, second_grad = over_rows(first_grad, second_grad)
    first_avg = per_channel(first_grad / cell_count)[:, None, None, :]
    second_avg = per_channel(second_grad / cell_count)[:, None, None, :]
    norm_part = inv[:, None, None, :] * (
        pre_grad.reshape(activations.shape) - first_avg - centred * second_avg
    )
    input_grad = jnp.where(live, grads.astype(f32) + norm_part, 0.0)

    last_pair = lax.dynamic_slice_in_dim(jnp.concatenate([zero_pair, hidden], 0), count, 2, 0)
    extended = with_rows(jnp.concatenate([shift(last_pair, TM, 16, 1), hidden], 0))
    block_out = forward_conv(count[None], extended, conv_weight, act).reshape(activations.shape)

    frame_total = 1 + 4 * ((16 - 1) * 3 // 2)
    grad_scale = 1.0 / math.sqrt(frame_total * 8 * ROWS * COLS)
    total = jnp.sum(arrived.astype(f32), axis=0) * grad_scale
    total = lax.dynamic_slice_in_dim(total, row_place, PIECE, 0)
    parts = (total[:, :HALF], total[:, HALF:])
    kept = jnp.where(core == 0, parts[0], parts[1])
    got = swap_cores(jnp.where(core == 0, parts[1], parts[0]))
    weight_grad = jnp.where(
        core == 0, jnp.concatenate([kept, got], 1), jnp.concatenate([got, kept], 1)
    )
    return block_out, input_grad, weight_grad


def solution(mesh):
    fine = Mesh(mesh.devices.reshape(2, 4, 2, 2, 4), ALL_AXES)
    placed = P(TM, ROW_AXES, None, None)
    return jax.shard_map(
        on_device,
        mesh=fine,
        in_specs=(placed, P(), P(), P(), P(), placed),
        out_specs=(placed, placed, P(ALL_AXES, None)),
        check_vma=False,
    )
```

```python
import functools
import math

import jax
import jax.numpy as jnp
from jax import lax
from jax.experimental import pallas as pl
from jax.experimental.pallas import tpu as pltpu
from jax.sharding import Mesh
from jax.sharding import PartitionSpec as P

GROUPS = 32
EPS = 1e-05
CHAN = 384
HALF = CHAN // 2
SLOTS = 8
ROWS = 4
COLS = 32
CELLS = ROWS * COLS
POS = SLOTS * CELLS
WIDE = 3 * CHAN
PIECE = 81
SENT = 88
CHIPS = 64
LANES = 128
TILE = 256

TM = ("ylo", "z", "core")
ROW_AXES = ("yhi", "x")
CHIP_AXES = ("ylo", "z", "yhi", "x")
ALL_AXES = TM + ROW_AXES

bf16 = jnp.bfloat16
f32 = jnp.float32
VMEM_LIMIT = pltpu.CompilerParams(vmem_limit_bytes=60 * 1024 * 1024)


def from_left(values):
    col = lax.broadcasted_iota(jnp.int32, values.shape, 0) % COLS
    return jnp.where(col == 0, 0.0, pltpu.roll(values, 1, 0))


def from_right(values):
    col = lax.broadcasted_iota(jnp.int32, values.shape, 0) % COLS
    return jnp.where(col == COLS - 1, 0.0, pltpu.roll(values, values.shape[0] - 1, 0))


def tap_products(x_ref, w_ref, acc, back):
    step = pl.program_id(0)
    weights = w_ref[...]
    pieces = []
    for b in range(3):
        at = (2 - step, 2 - b) if back else (step, b)
        pieces.append(x_ref[pl.ds(at[0], SLOTS), pl.ds(at[1], ROWS)].reshape(POS, CHAN))
    left = jnp.concatenate(pieces, axis=1)
    if back:
        right = jnp.concatenate([weights[b * WIDE : (b + 1) * WIDE] for b in range(3)], axis=1)
        dims = (((1,), (1,)), ((), ()))
    else:
        right = jnp.concatenate(
            [
                jnp.concatenate(
                    [weights[(b * 3 + c) * CHAN : (b * 3 + c + 1) * CHAN] for c in range(3)], axis=1
                )
                for b in range(3)
            ],
            axis=0,
        )
        dims = (((1,), (0,)), ((), ()))
    product = lax.dot_general(left, right, dims, preferred_element_type=f32)

    @pl.when(step == 0)
    def _():
        acc[...] = product

    @pl.when(step > 0)
    def _():
        acc[...] += product


def forward_kernel(count_ref, x_ref, w_ref, act_ref, out_ref, acc):
    tap_products(x_ref, w_ref, acc, False)

    @pl.when(pl.program_id(0) == 2)
    def _():
        for frame in range(SLOTS):
            rows = slice(frame * CELLS, (frame + 1) * CELLS)
            conv = (
                acc[rows, CHAN : 2 * CHAN]
                + from_left(acc[rows, :CHAN])
                + from_right(acc[rows, 2 * CHAN :])
            )
            total = act_ref[rows].astype(f32) + conv
            out_ref[rows] = jnp.where(frame < count_ref[0], total, 0.0).astype(bf16)


def backward_kernel(
    x_ref, w_ref, act_ref, mean_ref, inv_ref, gain_ref, bias_ref, out_ref, first_ref, second_ref, acc
):
    tap_products(x_ref, w_ref, acc, True)

    @pl.when(pl.program_id(0) == 2)
    def _():
        gain = gain_ref[...]
        bias = bias_ref[...]
        for frame in range(SLOTS):
            rows = slice(frame * CELLS, (frame + 1) * CELLS)
            grad = (
                acc[rows, CHAN : 2 * CHAN]
                + from_right(acc[rows, :CHAN])
                + from_left(acc[rows, 2 * CHAN :])
            )
            centred = (act_ref[rows].astype(f32) - mean_ref[frame : frame + 1]) * inv_ref[
                frame : frame + 1
            ]
            pre_act = centred * gain + bias
            gate = jax.nn.sigmoid(pre_act)
            pre_grad = grad * gate * (1.0 + pre_act * (1.0 - gate)) * gain
            out_ref[rows] = pre_grad
            first_ref[frame : frame + 1] = jnp.sum(pre_grad, axis=0, keepdims=True)
            second_ref[frame : frame + 1] = jnp.sum(pre_grad * centred, axis=0, keepdims=True)


def weight_kernel(h0_ref, h1_ref, c0_ref, c1_ref, out_ref, turned, sums):
    step = pl.program_id(0)

    @pl.when(step == 0)
    def _():
        for half, h_ref in enumerate((h0_ref, h1_ref)):

            def turn(m, carry, h_ref=h_ref, half=half):
                values = h_ref[pl.ds(pl.multiple_of(m * 256, 256), 256)].astype(f32)
                cols = pl.ds(pl.multiple_of(half * POS + m * 256, 256), 256)
                for c, moved in enumerate((from_left(values), values, from_right(values))):
                    turned[c * CHAN : (c + 1) * CHAN, cols] = moved.T.astype(bf16)
                return carry

            lax.fori_loop(0, POS // 256, turn, 0)

    right = jnp.concatenate(
        [
            jnp.concatenate(
                [
                    ref[pl.ds(2 - step, SLOTS), pl.ds(2 - b, ROWS)].reshape(POS, TILE)
                    for ref in (c0_ref, c1_ref)
                ],
                axis=0,
            )
            for b in range(3)
        ],
        axis=1,
    )
    product = jnp.dot(turned[...], right, preferred_element_type=f32)
    for b in range(3):
        rows = pl.ds(pl.multiple_of((step * 3 + b) * WIDE, WIDE), WIDE)
        sums[rows] = product[:, b * TILE : (b + 1) * TILE]

    @pl.when(step == 2)
    def _():
        upper = lax.broadcasted_iota(jnp.int32, (SENT, LANES), 1) >= LANES // 2

        def pack(m, carry):
            for row in range(8):
                starts = [pl.multiple_of(m * 1296 + row * 80 + core * 648, 8) for core in range(2)]
                first, second = (sums[pl.ds(start, SENT)] for start in starts)
                block = jnp.concatenate(
                    [
                        first[:, :LANES],
                        second[:, :LANES],
                        jnp.where(upper, second[:, LANES:], first[:, LANES:]),
                    ],
                    axis=1,
                )
                out_ref[m * 8 + row] = block.astype(bf16)
            return carry

        lax.fori_loop(0, CHIPS // 8, pack, 0)


def whole(shape):
    return pl.BlockSpec(shape, lambda step: (0,) * len(shape))


def cost(flops, moved):
    return pl.CostEstimate(flops=flops, bytes_accessed=moved, transcendentals=0)


FLOPS = 2 * POS * 27 * CHAN * CHAN
TAPS_SPEC = pl.BlockSpec((3 * WIDE, CHAN), lambda step: (step, 0))


def forward_conv(count, extended, weights, act):
    return pl.pallas_call(
        forward_kernel,
        out_shape=jax.ShapeDtypeStruct((POS, CHAN), bf16),
        grid=(3,),
        in_specs=[
            pl.BlockSpec(memory_space=pltpu.SMEM),
            whole(extended.shape),
            TAPS_SPEC,
            whole(act.shape),
        ],
        out_specs=whole((POS, CHAN)),
        scratch_shapes=[pltpu.VMEM((POS, WIDE), f32)],
        compiler_params=VMEM_LIMIT,
        cost_estimate=cost(FLOPS, 12 << 20),
        name="forward_conv",
    )(count, extended, weights, act)


def backward_conv(extended, weights, act, mean, inv, gain, bias):
    return pl.pallas_call(
        backward_kernel,
        out_shape=(
            jax.ShapeDtypeStruct((POS, CHAN), f32),
            jax.ShapeDtypeStruct((SLOTS, CHAN), f32),
            jax.ShapeDtypeStruct((SLOTS, CHAN), f32),
        ),
        grid=(3,),
        in_specs=[
            whole(extended.shape),
            TAPS_SPEC,
            whole(act.shape),
            whole(mean.shape),
            whole(inv.shape),
            whole(gain.shape),
            whole(bias.shape),
        ],
        out_specs=(whole((POS, CHAN)), whole((SLOTS, CHAN)), whole((SLOTS, CHAN))),
        scratch_shapes=[pltpu.VMEM((POS, WIDE), f32)],
        compiler_params=VMEM_LIMIT,
        cost_estimate=cost(FLOPS, 12 << 20),
        name="backward_conv",
    )(extended, weights, act, mean, inv, gain, bias)


def weight_terms(hidden, other_hidden, cots, other_cots):
    return pl.pallas_call(
        weight_kernel,
        out_shape=jax.ShapeDtypeStruct((CHIPS, SENT, CHAN), bf16),
        grid=(3,),
        in_specs=[
            whole(hidden.shape),
            whole(other_hidden.shape),
            whole(cots.shape),
            whole(other_cots.shape),
        ],
        out_specs=whole((CHIPS, SENT, CHAN)),
        scratch_shapes=[
            pltpu.VMEM((WIDE, 2 * POS), bf16),
            pltpu.VMEM((9 * WIDE, TILE), f32),
        ],
        compiler_params=VMEM_LIMIT,
        cost_estimate=cost(FLOPS, 12 << 20),
        name="weight_terms",
    )(hidden, other_hidden, cots, other_cots)


def shift(values, axes, count, step):
    pairs = [(i, i + step) for i in range(count) if 0 <= i + step < count]
    return lax.ppermute(values, axes, pairs)


def swap_cores(values):
    return lax.ppermute(values, "core", [(0, 1), (1, 0)])


def edge_rows(block):
    low = shift(block[:, ROWS - 1 :], ROW_AXES, 8, 1)
    high = shift(block[:, :1], ROW_AXES, 8, -1)
    return low, high


def half_columns(cots, second):
    halves = [
        jnp.concatenate([cots[..., at : at + HALF], cots[..., at + LANES : at + HALF]], axis=3)
        for at in (0, HALF)
    ]
    return jnp.where(second, halves[1], halves[0])


def per_group(first, second):
    grouped = jnp.concatenate([first, second], axis=0).reshape(2 * SLOTS, GROUPS, CHAN // GROUPS)
    return jnp.sum(grouped, axis=2)


def over_rows(sums):
    spread = jnp.broadcast_to(sums[None], (8,) + sums.shape)
    total = jnp.sum(lax.all_to_all(spread, ROW_AXES, 0, 0), axis=0)
    return total[:SLOTS], total[SLOTS:]


def per_channel(grouped):
    return jnp.repeat(grouped, CHAN // GROUPS, axis=1)


def on_device(activations, frame_counts, norm_gain, norm_bias, conv_weight, cotangent):
    core = lax.axis_index("core")
    cell_count = 8 * CELLS * (CHAN // GROUPS)
    act = activations.reshape(POS, CHAN)
    zero_pair = jnp.zeros((2, ROWS, COLS, CHAN), bf16)

    values = activations.astype(f32)
    sums = per_group(jnp.sum(values, axis=(1, 2)), jnp.sum(values * values, axis=(1, 2)))
    first_sum, second_sum = over_rows(sums)

    cotangent, frame_counts, _ = lax.optimization_barrier((cotangent, frame_counts, sums))
    count = frame_counts[lax.axis_index(TM)]
    live = (jnp.arange(SLOTS) < count)[:, None, None, None]
    grads = jnp.where(live, cotangent, jnp.zeros_like(cotangent))
    next_head = shift(grads[:2], TM, 16, -1)
    future = lax.dynamic_update_slice_in_dim(
        jnp.concatenate([grads, zero_pair], 0), next_head, count, 0
    )
    low, high = edge_rows(future)
    cots = jnp.concatenate([low, future, high], axis=1)
    cots_here = half_columns(cots, core == 1)
    cots_there = swap_cores(half_columns(cots, core == 0))

    group_mean = first_sum / cell_count
    inv_std = lax.rsqrt(second_sum / cell_count - group_mean * group_mean + EPS)
    mean = per_channel(group_mean)
    inv = per_channel(inv_std)
    centred = (values - mean[:, None, None, :]) * inv[:, None, None, :]
    pre_act = centred * norm_gain + norm_bias
    hidden = jnp.where(live, jax.nn.silu(pre_act), 0.0).astype(bf16)
    hidden_there = swap_cores(hidden)
    last_pair = lax.dynamic_slice_in_dim(jnp.concatenate([zero_pair, hidden], 0), count, 2, 0)
    frames = jnp.concatenate([shift(last_pair, TM, 16, 1), hidden], 0)
    low, high = edge_rows(frames)

    terms = weight_terms(
        hidden.reshape(POS, CHAN), hidden_there.reshape(POS, CHAN), cots_here, cots_there
    )
    terms, low, high = lax.optimization_barrier((terms, low, high))
    arrived = lax.all_to_all(terms, CHIP_AXES, 0, 0)

    cots, _ = lax.optimization_barrier((cots, terms))
    pre_grad, first_grad, second_grad = backward_conv(
        cots, conv_weight, act, mean, inv, norm_gain[None], norm_bias[None]
    )
    first_grad, second_grad = over_rows(per_group(first_grad, second_grad))
    first_avg = per_channel(first_grad / cell_count)[:, None, None, :]
    second_avg = per_channel(second_grad / cell_count)[:, None, None, :]
    norm_part = inv[:, None, None, :] * (
        pre_grad.reshape(activations.shape) - first_avg - centred * second_avg
    )
    input_grad = jnp.where(live, grads.astype(f32) + norm_part, 0.0)

    extended = jnp.concatenate([low, frames, high], axis=1)
    block_out = forward_conv(count[None], extended, conv_weight, act).reshape(activations.shape)

    frame_total = 1 + 4 * ((16 - 1) * 3 // 2)
    grad_scale = 1.0 / math.sqrt(frame_total * 8 * ROWS * COLS)
    total = jnp.sum(arrived.astype(f32), axis=0) * grad_scale
    total = lax.dynamic_slice_in_dim(total, lax.axis_index(ROW_AXES), PIECE, 0)
    parts = [
        jnp.concatenate(
            [
                total[:, k * LANES : (k + 1) * LANES],
                total[:, 2 * LANES + k * 64 : 2 * LANES + (k + 1) * 64],
            ],
            axis=1,
        )
        for k in range(2)
    ]
    kept = jnp.where(core == 0, parts[0], parts[1])
    got = swap_cores(jnp.where(core == 0, parts[1], parts[0]))
    weight_grad = jnp.where(
        core == 0, jnp.concatenate([kept, got], 1), jnp.concatenate([got, kept], 1)
    )
    return block_out, input_grad, weight_grad


def solution(mesh):
    fine = Mesh(mesh.devices.reshape(2, 4, 2, 2, 4), ALL_AXES)
    placed = P(TM, ROW_AXES, None, None)
    return jax.shard_map(
        on_device,
        mesh=fine,
        in_specs=(placed, P(), P(), P(), P(), placed),
        out_specs=(placed, placed, P(ALL_AXES, None)),
        check_vma=False,
    )
```

```python
import functools
import math

import jax
import jax.numpy as jnp
from jax import lax
from jax.experimental import pallas as pl
from jax.experimental.pallas import tpu as pltpu
from jax.sharding import Mesh
from jax.sharding import PartitionSpec as P

GROUPS = 32
EPS = 1e-05
CHAN = 384
HALF = CHAN // 2
SLOTS = 8
ROWS = 4
COLS = 32
CELLS = ROWS * COLS
POS = SLOTS * CELLS
WIDE = 3 * CHAN
PIECE = 81
CHIPS = 64
LANES = 128
TILE = 256

TM = ("ylo", "z", "core")
ROW_AXES = ("yhi", "x")
CHIP_AXES = ("ylo", "z", "yhi", "x")
ALL_AXES = TM + ROW_AXES

bf16 = jnp.bfloat16
f32 = jnp.float32
VMEM_LIMIT = pltpu.CompilerParams(vmem_limit_bytes=60 * 1024 * 1024)


def from_left(values):
    col = lax.broadcasted_iota(jnp.int32, values.shape, 0) % COLS
    return jnp.where(col == 0, 0.0, pltpu.roll(values, 1, 0))


def from_right(values):
    col = lax.broadcasted_iota(jnp.int32, values.shape, 0) % COLS
    return jnp.where(col == COLS - 1, 0.0, pltpu.roll(values, values.shape[0] - 1, 0))


def tap_products(x_ref, w_ref, acc, back):
    step = pl.program_id(0)
    weights = w_ref[...]
    pieces = []
    for b in range(3):
        at = (2 - step, 2 - b) if back else (step, b)
        pieces.append(x_ref[pl.ds(at[0], SLOTS), pl.ds(at[1], ROWS)].reshape(POS, CHAN))
    left = jnp.concatenate(pieces, axis=1)
    if back:
        right = jnp.concatenate([weights[b * WIDE : (b + 1) * WIDE] for b in range(3)], axis=1)
        dims = (((1,), (1,)), ((), ()))
    else:
        right = jnp.concatenate(
            [
                jnp.concatenate(
                    [weights[(b * 3 + c) * CHAN : (b * 3 + c + 1) * CHAN] for c in range(3)], axis=1
                )
                for b in range(3)
            ],
            axis=0,
        )
        dims = (((1,), (0,)), ((), ()))
    product = lax.dot_general(left, right, dims, preferred_element_type=f32)

    @pl.when(step == 0)
    def _():
        acc[...] = product

    @pl.when(step > 0)
    def _():
        acc[...] += product


def forward_kernel(count_ref, x_ref, w_ref, act_ref, out_ref, acc):
    tap_products(x_ref, w_ref, acc, False)

    @pl.when(pl.program_id(0) == 2)
    def _():
        for frame in range(SLOTS):
            rows = slice(frame * CELLS, (frame + 1) * CELLS)
            conv = (
                acc[rows, CHAN : 2 * CHAN]
                + from_left(acc[rows, :CHAN])
                + from_right(acc[rows, 2 * CHAN :])
            )
            total = act_ref[rows].astype(f32) + conv
            out_ref[rows] = jnp.where(frame < count_ref[0], total, 0.0).astype(bf16)


def backward_kernel(
    x_ref, w_ref, act_ref, mean_ref, inv_ref, gain_ref, bias_ref, out_ref, first_ref, second_ref, acc
):
    tap_products(x_ref, w_ref, acc, True)

    @pl.when(pl.program_id(0) == 2)
    def _():
        gain = gain_ref[...]
        bias = bias_ref[...]
        for frame in range(SLOTS):
            rows = slice(frame * CELLS, (frame + 1) * CELLS)
            grad = (
                acc[rows, CHAN : 2 * CHAN]
                + from_right(acc[rows, :CHAN])
                + from_left(acc[rows, 2 * CHAN :])
            )
            centred = (act_ref[rows].astype(f32) - mean_ref[frame : frame + 1]) * inv_ref[
                frame : frame + 1
            ]
            pre_act = centred * gain + bias
            gate = jax.nn.sigmoid(pre_act)
            pre_grad = grad * gate * (1.0 + pre_act * (1.0 - gate)) * gain
            out_ref[rows] = pre_grad
            first_ref[frame : frame + 1] = jnp.sum(pre_grad, axis=0, keepdims=True)
            second_ref[frame : frame + 1] = jnp.sum(pre_grad * centred, axis=0, keepdims=True)


READY = ((0, 2), (2, 5), (5, 8))


def weight_kernel(h0_ref, h1_ref, c0_ref, c1_ref, out_ref, turned, sums, packed, sems):
    for half, h_ref in enumerate((h0_ref, h1_ref)):

        def turn(m, carry, h_ref=h_ref, half=half):
            values = h_ref[pl.ds(pl.multiple_of(m * 256, 256), 256)].astype(f32)
            cols = pl.ds(pl.multiple_of(half * POS + m * 256, 256), 256)
            for c, moved in enumerate((from_left(values), values, from_right(values))):
                turned[c * CHAN : (c + 1) * CHAN, cols] = moved.T.astype(bf16)
            return carry

        lax.fori_loop(0, POS // 256, turn, 0)

    upper = lax.broadcasted_iota(jnp.int32, (PIECE, LANES), 1) >= LANES // 2
    copies = []
    for a in range(3):
        right = jnp.concatenate(
            [
                jnp.concatenate(
                    [
                        ref[2 - a : 2 - a + SLOTS, 2 - b : 2 - b + ROWS].reshape(POS, TILE)
                        for ref in (c0_ref, c1_ref)
                    ],
                    axis=0,
                )
                for b in range(3)
            ],
            axis=1,
        )
        product = jnp.dot(turned[...], right, preferred_element_type=f32)
        for b in range(3):
            at = (a * 3 + b) * WIDE
            sums[at : at + WIDE] = product[:, b * TILE : (b + 1) * TILE]
        for chip in range(8 * READY[a][0], 8 * READY[a][1]):
            start = 1296 * (chip // 8) + PIECE * (chip % 8)
            first, second = sums[start : start + PIECE], sums[start + 648 : start + 648 + PIECE]
            block = jnp.concatenate(
                [
                    first[:, :LANES],
                    second[:, :LANES],
                    jnp.where(upper, second[:, LANES:], first[:, LANES:]),
                ],
                axis=0,
            )
            packed[chip] = block.astype(bf16)
        chips = pl.ds(8 * READY[a][0], 8 * (READY[a][1] - READY[a][0]))
        copies.append(pltpu.make_async_copy(packed.at[chips], out_ref.at[chips], sems.at[a]))
        copies[-1].start()
    for copy in copies:
        copy.wait()


def whole(shape):
    return pl.BlockSpec(shape, lambda step: (0,) * len(shape))


def cost(flops, moved):
    return pl.CostEstimate(flops=flops, bytes_accessed=moved, transcendentals=0)


FLOPS = 2 * POS * 27 * CHAN * CHAN
TAPS_SPEC = pl.BlockSpec((3 * WIDE, CHAN), lambda step: (step, 0))


def forward_conv(count, extended, weights, act):
    return pl.pallas_call(
        forward_kernel,
        out_shape=jax.ShapeDtypeStruct((POS, CHAN), bf16),
        grid=(3,),
        in_specs=[
            pl.BlockSpec(memory_space=pltpu.SMEM),
            whole(extended.shape),
            TAPS_SPEC,
            whole(act.shape),
        ],
        out_specs=whole((POS, CHAN)),
        scratch_shapes=[pltpu.VMEM((POS, WIDE), f32)],
        compiler_params=VMEM_LIMIT,
        cost_estimate=cost(FLOPS, 12 << 20),
        name="forward_conv",
    )(count, extended, weights, act)


def backward_conv(extended, weights, act, mean, inv, gain, bias):
    return pl.pallas_call(
        backward_kernel,
        out_shape=(
            jax.ShapeDtypeStruct((POS, CHAN), f32),
            jax.ShapeDtypeStruct((SLOTS, CHAN), f32),
            jax.ShapeDtypeStruct((SLOTS, CHAN), f32),
        ),
        grid=(3,),
        in_specs=[
            whole(extended.shape),
            TAPS_SPEC,
            whole(act.shape),
            whole(mean.shape),
            whole(inv.shape),
            whole(gain.shape),
            whole(bias.shape),
        ],
        out_specs=(whole((POS, CHAN)), whole((SLOTS, CHAN)), whole((SLOTS, CHAN))),
        scratch_shapes=[pltpu.VMEM((POS, WIDE), f32)],
        compiler_params=VMEM_LIMIT,
        cost_estimate=cost(FLOPS, 12 << 20),
        name="backward_conv",
    )(extended, weights, act, mean, inv, gain, bias)


def weight_terms(hidden, other_hidden, cots, other_cots):
    return pl.pallas_call(
        weight_kernel,
        out_shape=jax.ShapeDtypeStruct((CHIPS, 3 * PIECE, LANES), bf16),
        in_specs=[pl.BlockSpec(memory_space=pltpu.VMEM)] * 4,
        out_specs=pl.BlockSpec(memory_space=pl.ANY),
        scratch_shapes=[
            pltpu.VMEM((WIDE, 2 * POS), bf16),
            pltpu.VMEM((9 * WIDE, TILE), f32),
            pltpu.VMEM((CHIPS, 3 * PIECE, LANES), bf16),
            pltpu.SemaphoreType.DMA((3,)),
        ],
        compiler_params=VMEM_LIMIT,
        cost_estimate=cost(FLOPS, 12 << 20),
        name="weight_terms",
    )(hidden, other_hidden, cots, other_cots)


def shift(values, axes, count, step):
    pairs = [(i, i + step) for i in range(count) if 0 <= i + step < count]
    return lax.ppermute(values, axes, pairs)


def swap_cores(values):
    return lax.ppermute(values, "core", [(0, 1), (1, 0)])


def edge_rows(block):
    low = shift(block[:, ROWS - 1 :], ROW_AXES, 8, 1)
    high = shift(block[:, :1], ROW_AXES, 8, -1)
    return low, high


def half_columns(cots, second):
    halves = [
        jnp.concatenate([cots[..., at : at + HALF], cots[..., at + LANES : at + HALF]], axis=3)
        for at in (0, HALF)
    ]
    return jnp.where(second, halves[1], halves[0])


def per_group(first, second):
    grouped = jnp.concatenate([first, second], axis=0).reshape(2 * SLOTS, GROUPS, CHAN // GROUPS)
    return jnp.sum(grouped, axis=2)


def by_butterfly(sums):
    for axis, pairs in (
        ("x", ((0, 1), (1, 0), (2, 3), (3, 2))),
        ("x", ((0, 2), (1, 3), (2, 0), (3, 1))),
        ("yhi", ((0, 1), (1, 0))),
    ):
        sums = sums + lax.ppermute(sums, axis, pairs)
    return sums


def at_once(sums):
    total = sums
    for step in range(1, 8):
        total = total + lax.ppermute(sums, ROW_AXES, [(i, (i + step) % 8) for i in range(8)])
    return total


def per_channel(grouped):
    return jnp.repeat(grouped, CHAN // GROUPS, axis=1)


def on_device(activations, frame_counts, norm_gain, norm_bias, conv_weight, cotangent):
    core = lax.axis_index("core")
    cell_count = 8 * CELLS * (CHAN // GROUPS)
    act = activations.reshape(POS, CHAN)

    values = activations.astype(f32)
    sums = per_group(jnp.sum(values, axis=(1, 2)), jnp.sum(values * values, axis=(1, 2)))
    sums = by_butterfly(sums)

    count = frame_counts[lax.axis_index(TM)]
    live = (jnp.arange(SLOTS) < count)[:, None, None, None]
    grads = jnp.where(live, cotangent, jnp.zeros_like(cotangent))
    low, high = edge_rows(jnp.concatenate([activations, grads], 0))
    wide_grads = jnp.concatenate([low[SLOTS:], grads, high[SLOTS:]], axis=1)
    next_head = shift(wide_grads[:2], TM, 16, -1)
    cots = lax.dynamic_update_slice_in_dim(
        jnp.concatenate([wide_grads, jnp.zeros((2, ROWS + 2, COLS, CHAN), bf16)], 0),
        next_head,
        count,
        0,
    )
    cots_here = half_columns(cots, core == 1)
    cots_there = swap_cores(half_columns(cots, core == 0))

    group_mean = sums[:SLOTS] / cell_count
    inv_std = lax.rsqrt(sums[SLOTS:] / cell_count - group_mean * group_mean + EPS)
    mean = per_channel(group_mean)
    inv = per_channel(inv_std)

    def normed(rows):
        return (rows.astype(f32) - mean[:, None, None, :]) * inv[:, None, None, :]

    def activated(rows, keep):
        pre_act = normed(rows) * norm_gain + norm_bias
        return jnp.where(keep, jax.nn.silu(pre_act), 0.0).astype(bf16)

    hidden = activated(activations, live)
    hidden_there = swap_cores(hidden)
    row_place = lax.axis_index(ROW_AXES)
    wide_hidden = jnp.concatenate(
        [
            activated(low[:SLOTS], live & (row_place > 0)),
            hidden,
            activated(high[:SLOTS], live & (row_place < 7)),
        ],
        axis=1,
    )
    before = jnp.zeros((2, ROWS + 2, COLS, CHAN), bf16)
    last_pair = lax.dynamic_slice_in_dim(jnp.concatenate([before, wide_hidden], 0), count, 2, 0)
    before = shift(last_pair, TM, 16, 1)

    terms = weight_terms(
        hidden.reshape(POS, CHAN), hidden_there.reshape(POS, CHAN), cots_here, cots_there
    )
    terms, before = lax.optimization_barrier((terms, before))
    arrived = lax.all_to_all(terms, CHIP_AXES, 0, 0)

    cots, _ = lax.optimization_barrier((cots, terms))
    pre_grad, first_grad, second_grad = backward_conv(
        cots, conv_weight, act, mean, inv, norm_gain[None], norm_bias[None]
    )
    sums = at_once(per_group(first_grad, second_grad))
    first_avg = per_channel(sums[:SLOTS] / cell_count)[:, None, None, :]
    second_avg = per_channel(sums[SLOTS:] / cell_count)[:, None, None, :]
    norm_part = inv[:, None, None, :] * (
        pre_grad.reshape(activations.shape) - first_avg - normed(activations) * second_avg
    )
    input_grad = jnp.where(live, grads.astype(f32) + norm_part, 0.0)

    extended = jnp.concatenate([before, wide_hidden], axis=0)
    block_out = forward_conv(count[None], extended, conv_weight, act).reshape(activations.shape)

    frame_total = 1 + 4 * ((16 - 1) * 3 // 2)
    grad_scale = 1.0 / math.sqrt(frame_total * 8 * ROWS * COLS)
    total = jnp.sum(arrived.astype(f32), axis=0) * grad_scale
    shared = total[2 * PIECE :]
    parts = [
        jnp.concatenate(
            [total[k * PIECE : (k + 1) * PIECE], shared[:, k * 64 : (k + 1) * 64]], axis=1
        )
        for k in range(2)
    ]
    kept = jnp.where(core == 0, parts[0], parts[1])
    got = swap_cores(jnp.where(core == 0, parts[1], parts[0]))
    weight_grad = jnp.where(
        core == 0, jnp.concatenate([kept, got], 1), jnp.concatenate([got, kept], 1)
    )
    return block_out, input_grad, weight_grad


def solution(mesh):
    fine = Mesh(mesh.devices.reshape(2, 4, 2, 2, 4), ALL_AXES)
    placed = P(TM, ROW_AXES, None, None)
    return jax.shard_map(
        on_device,
        mesh=fine,
        in_specs=(placed, P(), P(), P(), P(), placed),
        out_specs=(placed, placed, P(ALL_AXES, None)),
        check_vma=False,
    )
```

```python
import functools
import math

import jax
import jax.numpy as jnp
from jax import lax
from jax.experimental import pallas as pl
from jax.experimental.pallas import tpu as pltpu
from jax.sharding import Mesh
from jax.sharding import PartitionSpec as P

GROUPS = 32
EPS = 1e-05
CHAN = 384
HALF = CHAN // 2
SLOTS = 8
ROWS = 4
COLS = 32
CELLS = ROWS * COLS
POS = SLOTS * CELLS
WIDE = 3 * CHAN
PIECE = 81
CHIPS = 64
LANES = 128
TILE = 256

TM = ("ylo", "z", "core")
ROW_AXES = ("yhi", "x")
CHIP_AXES = ("ylo", "z", "yhi", "x")
ALL_AXES = TM + ROW_AXES

bf16 = jnp.bfloat16
f32 = jnp.float32
VMEM_LIMIT = pltpu.CompilerParams(vmem_limit_bytes=60 * 1024 * 1024)


def from_left(values):
    col = lax.broadcasted_iota(jnp.int32, values.shape, 0) % COLS
    return jnp.where(col == 0, 0.0, pltpu.roll(values, 1, 0))


def from_right(values):
    col = lax.broadcasted_iota(jnp.int32, values.shape, 0) % COLS
    return jnp.where(col == COLS - 1, 0.0, pltpu.roll(values, values.shape[0] - 1, 0))


def tap_products(x_ref, w_ref, acc, back):
    step = pl.program_id(0)
    weights = w_ref[...]
    pieces = []
    for b in range(3):
        at = (2 - step, 2 - b) if back else (step, b)
        pieces.append(x_ref[pl.ds(at[0], SLOTS), pl.ds(at[1], ROWS)].reshape(POS, CHAN))
    left = jnp.concatenate(pieces, axis=1)
    if back:
        right = jnp.concatenate([weights[b * WIDE : (b + 1) * WIDE] for b in range(3)], axis=1)
        dims = (((1,), (1,)), ((), ()))
    else:
        right = jnp.concatenate(
            [
                jnp.concatenate(
                    [weights[(b * 3 + c) * CHAN : (b * 3 + c + 1) * CHAN] for c in range(3)], axis=1
                )
                for b in range(3)
            ],
            axis=0,
        )
        dims = (((1,), (0,)), ((), ()))
    product = lax.dot_general(left, right, dims, preferred_element_type=f32)

    @pl.when(step == 0)
    def _():
        acc[...] = product

    @pl.when(step > 0)
    def _():
        acc[...] += product


def forward_kernel(count_ref, x_ref, w_ref, act_ref, out_ref, acc):
    tap_products(x_ref, w_ref, acc, False)

    @pl.when(pl.program_id(0) == 2)
    def _():
        for frame in range(SLOTS):
            rows = slice(frame * CELLS, (frame + 1) * CELLS)
            conv = (
                acc[rows, CHAN : 2 * CHAN]
                + from_left(acc[rows, :CHAN])
                + from_right(acc[rows, 2 * CHAN :])
            )
            total = act_ref[rows].astype(f32) + conv
            out_ref[rows] = jnp.where(frame < count_ref[0], total, 0.0).astype(bf16)


def backward_kernel(
    x_ref, w_ref, act_ref, mean_ref, inv_ref, gain_ref, bias_ref, out_ref, first_ref, second_ref, acc
):
    tap_products(x_ref, w_ref, acc, True)

    @pl.when(pl.program_id(0) == 2)
    def _():
        gain = gain_ref[...]
        bias = bias_ref[...]
        for frame in range(SLOTS):
            rows = slice(frame * CELLS, (frame + 1) * CELLS)
            grad = (
                acc[rows, CHAN : 2 * CHAN]
                + from_right(acc[rows, :CHAN])
                + from_left(acc[rows, 2 * CHAN :])
            )
            centred = (act_ref[rows].astype(f32) - mean_ref[frame : frame + 1]) * inv_ref[
                frame : frame + 1
            ]
            pre_act = centred * gain + bias
            gate = jax.nn.sigmoid(pre_act)
            pre_grad = grad * gate * (1.0 + pre_act * (1.0 - gate)) * gain
            out_ref[rows] = pre_grad
            first_ref[frame : frame + 1] = jnp.sum(pre_grad, axis=0, keepdims=True)
            second_ref[frame : frame + 1] = jnp.sum(pre_grad * centred, axis=0, keepdims=True)


READY = ((0, 2), (2, 5), (5, 8))


def weight_kernel(h0_ref, h1_ref, c0_ref, c1_ref, out_ref, turned, sums, packed, sems):
    for half, h_ref in enumerate((h0_ref, h1_ref)):

        def turn(m, carry, h_ref=h_ref, half=half):
            values = h_ref[pl.ds(pl.multiple_of(m * 256, 256), 256)].astype(f32)
            cols = pl.ds(pl.multiple_of(half * POS + m * 256, 256), 256)
            for c, moved in enumerate((from_left(values), values, from_right(values))):
                turned[c * CHAN : (c + 1) * CHAN, cols] = moved.T.astype(bf16)
            return carry

        lax.fori_loop(0, POS // 256, turn, 0)

    upper = lax.broadcasted_iota(jnp.int32, (PIECE, LANES), 1) >= LANES // 2
    copies = []
    for a in range(3):
        right = jnp.concatenate(
            [
                jnp.concatenate(
                    [
                        ref[2 - a : 2 - a + SLOTS, 2 - b : 2 - b + ROWS].reshape(POS, TILE)
                        for ref in (c0_ref, c1_ref)
                    ],
                    axis=0,
                )
                for b in range(3)
            ],
            axis=1,
        )
        product = jnp.dot(turned[...], right, preferred_element_type=f32)
        for b in range(3):
            at = (a * 3 + b) * WIDE
            sums[at : at + WIDE] = product[:, b * TILE : (b + 1) * TILE]
        for chip in range(8 * READY[a][0], 8 * READY[a][1]):
            start = 1296 * (chip // 8) + PIECE * (chip % 8)
            first, second = sums[start : start + PIECE], sums[start + 648 : start + 648 + PIECE]
            block = jnp.concatenate(
                [
                    first[:, :LANES],
                    second[:, :LANES],
                    jnp.where(upper, second[:, LANES:], first[:, LANES:]),
                ],
                axis=0,
            )
            packed[chip] = block.astype(bf16)
        chips = pl.ds(8 * READY[a][0], 8 * (READY[a][1] - READY[a][0]))
        copies.append(pltpu.make_async_copy(packed.at[chips], out_ref.at[chips], sems.at[a]))
        copies[-1].start()
    for copy in copies:
        copy.wait()


def whole(shape):
    return pl.BlockSpec(shape, lambda step: (0,) * len(shape))


def cost(flops, moved):
    return pl.CostEstimate(flops=flops, bytes_accessed=moved, transcendentals=0)


FLOPS = 2 * POS * 27 * CHAN * CHAN
TAPS_SPEC = pl.BlockSpec((3 * WIDE, CHAN), lambda step: (step, 0))


def forward_conv(count, extended, weights, act):
    return pl.pallas_call(
        forward_kernel,
        out_shape=jax.ShapeDtypeStruct((POS, CHAN), bf16),
        grid=(3,),
        in_specs=[
            pl.BlockSpec(memory_space=pltpu.SMEM),
            whole(extended.shape),
            TAPS_SPEC,
            whole(act.shape),
        ],
        out_specs=whole((POS, CHAN)),
        scratch_shapes=[pltpu.VMEM((POS, WIDE), f32)],
        compiler_params=VMEM_LIMIT,
        cost_estimate=cost(FLOPS, 12 << 20),
        name="forward_conv",
    )(count, extended, weights, act)


def backward_conv(extended, weights, act, mean, inv, gain, bias):
    return pl.pallas_call(
        backward_kernel,
        out_shape=(
            jax.ShapeDtypeStruct((POS, CHAN), f32),
            jax.ShapeDtypeStruct((SLOTS, CHAN), f32),
            jax.ShapeDtypeStruct((SLOTS, CHAN), f32),
        ),
        grid=(3,),
        in_specs=[
            whole(extended.shape),
            TAPS_SPEC,
            whole(act.shape),
            whole(mean.shape),
            whole(inv.shape),
            whole(gain.shape),
            whole(bias.shape),
        ],
        out_specs=(whole((POS, CHAN)), whole((SLOTS, CHAN)), whole((SLOTS, CHAN))),
        scratch_shapes=[pltpu.VMEM((POS, WIDE), f32)],
        compiler_params=VMEM_LIMIT,
        cost_estimate=cost(FLOPS, 12 << 20),
        name="backward_conv",
    )(extended, weights, act, mean, inv, gain, bias)


def weight_terms(hidden, other_hidden, cots, other_cots):
    return pl.pallas_call(
        weight_kernel,
        out_shape=jax.ShapeDtypeStruct((CHIPS, 3 * PIECE, LANES), bf16),
        in_specs=[pl.BlockSpec(memory_space=pltpu.VMEM)] * 4,
        out_specs=pl.BlockSpec(memory_space=pl.ANY),
        scratch_shapes=[
            pltpu.VMEM((WIDE, 2 * POS), bf16),
            pltpu.VMEM((9 * WIDE, TILE), f32),
            pltpu.VMEM((CHIPS, 3 * PIECE, LANES), bf16),
            pltpu.SemaphoreType.DMA((3,)),
        ],
        compiler_params=VMEM_LIMIT,
        cost_estimate=cost(FLOPS, 12 << 20),
        name="weight_terms",
    )(hidden, other_hidden, cots, other_cots)


def shift(values, axes, count, step):
    pairs = [(i, i + step) for i in range(count) if 0 <= i + step < count]
    return lax.ppermute(values, axes, pairs)


def swap_cores(values):
    return lax.ppermute(values, "core", [(0, 1), (1, 0)])


def edge_rows(block):
    low = shift(block[:, ROWS - 1 :], ROW_AXES, 8, 1)
    high = shift(block[:, :1], ROW_AXES, 8, -1)
    return low, high


def half_columns(cots, second):
    halves = [
        jnp.concatenate([cots[..., at : at + HALF], cots[..., at + LANES : at + HALF]], axis=3)
        for at in (0, HALF)
    ]
    return jnp.where(second, halves[1], halves[0])


def per_group(first, second):
    grouped = jnp.concatenate([first, second], axis=0).reshape(2 * SLOTS, GROUPS, CHAN // GROUPS)
    return jnp.sum(grouped, axis=2)


def add_pairs(sums, axis, pairs):
    return sums + lax.ppermute(sums, axis, pairs + [(b, a) for a, b in pairs])


def per_channel(grouped):
    return jnp.repeat(grouped, CHAN // GROUPS, axis=1)


def on_device(activations, frame_counts, norm_gain, norm_bias, conv_weight, cotangent):
    core = lax.axis_index("core")
    cell_count = 8 * CELLS * (CHAN // GROUPS)
    act = activations.reshape(POS, CHAN)

    values = activations.astype(f32)
    sums = per_group(jnp.sum(values, axis=(1, 2)), jnp.sum(values * values, axis=(1, 2)))
    low, high = edge_rows(cotangent)
    sums = add_pairs(sums, "x", [(0, 1), (2, 3)])
    sums = add_pairs(sums, "x", [(0, 2), (1, 3)])
    sums, low, high, late = lax.optimization_barrier((sums, low, high, activations))
    act_low, act_high = edge_rows(late)
    sums = add_pairs(sums, "yhi", [(0, 1)])
    sums, act_low, act_high = lax.optimization_barrier((sums, act_low, act_high))

    count = frame_counts[lax.axis_index(TM)]
    live = (jnp.arange(SLOTS) < count)[:, None, None, None]
    wide_grads = jnp.concatenate([low, cotangent, high], axis=1)
    wide_grads = jnp.where(live, wide_grads, jnp.zeros_like(wide_grads))
    grads = wide_grads[:, 1 : 1 + ROWS]
    next_head = shift(wide_grads[:2], TM, 16, -1)
    cots = lax.dynamic_update_slice_in_dim(
        jnp.concatenate([wide_grads, jnp.zeros((2, ROWS + 2, COLS, CHAN), bf16)], 0),
        next_head,
        count,
        0,
    )
    cots_here = half_columns(cots, core == 1)
    cots_there = swap_cores(half_columns(cots, core == 0))

    group_mean = sums[:SLOTS] / cell_count
    inv_std = lax.rsqrt(sums[SLOTS:] / cell_count - group_mean * group_mean + EPS)
    mean = per_channel(group_mean)
    inv = per_channel(inv_std)

    def normed(rows):
        return (rows.astype(f32) - mean[:, None, None, :]) * inv[:, None, None, :]

    def activated(rows, keep):
        pre_act = normed(rows) * norm_gain + norm_bias
        return jnp.where(keep, jax.nn.silu(pre_act), 0.0).astype(bf16)

    hidden = activated(activations, live)
    hidden_there = swap_cores(hidden)
    row_place = lax.axis_index(ROW_AXES)
    wide_hidden = jnp.concatenate(
        [
            activated(act_low, live & (row_place > 0)),
            hidden,
            activated(act_high, live & (row_place < 7)),
        ],
        axis=1,
    )
    before = jnp.zeros((2, ROWS + 2, COLS, CHAN), bf16)
    last_pair = lax.dynamic_slice_in_dim(jnp.concatenate([before, wide_hidden], 0), count, 2, 0)
    before = shift(last_pair, TM, 16, 1)

    terms = weight_terms(
        hidden.reshape(POS, CHAN), hidden_there.reshape(POS, CHAN), cots_here, cots_there
    )
    terms, before = lax.optimization_barrier((terms, before))
    arrived = lax.all_to_all(terms, CHIP_AXES, 0, 0)

    cots, _ = lax.optimization_barrier((cots, terms))
    pre_grad, first_grad, second_grad = backward_conv(
        cots, conv_weight, act, mean, inv, norm_gain[None], norm_bias[None]
    )
    sums = per_group(first_grad, second_grad)
    parts = [lax.ppermute(sums, "x", [(i, (i + k) % 4) for i in range(4)]) for k in range(1, 4)]

    extended = jnp.concatenate([before, wide_hidden], axis=0)
    block_out = forward_conv(count[None], extended, conv_weight, act)
    block_out, parts = lax.optimization_barrier((block_out, parts))
    block_out = block_out.reshape(activations.shape)

    sums = add_pairs(sums + parts[0] + parts[1] + parts[2], "yhi", [(0, 1)])
    first_avg = per_channel(sums[:SLOTS] / cell_count)[:, None, None, :]
    second_avg = per_channel(sums[SLOTS:] / cell_count)[:, None, None, :]
    norm_part = inv[:, None, None, :] * (
        pre_grad.reshape(activations.shape) - first_avg - normed(activations) * second_avg
    )
    input_grad = jnp.where(live, grads.astype(f32) + norm_part, 0.0)

    frame_total = 1 + 4 * ((16 - 1) * 3 // 2)
    grad_scale = 1.0 / math.sqrt(frame_total * 8 * ROWS * COLS)
    total = jnp.sum(arrived.astype(f32), axis=0) * grad_scale
    shared = total[2 * PIECE :]
    parts = [
        jnp.concatenate(
            [total[k * PIECE : (k + 1) * PIECE], shared[:, k * 64 : (k + 1) * 64]], axis=1
        )
        for k in range(2)
    ]
    kept = jnp.where(core == 0, parts[0], parts[1])
    got = swap_cores(jnp.where(core == 0, parts[1], parts[0]))
    weight_grad = jnp.where(
        core == 0, jnp.concatenate([kept, got], 1), jnp.concatenate([got, kept], 1)
    )
    return block_out, input_grad, weight_grad


def solution(mesh):
    fine = Mesh(mesh.devices.reshape(2, 4, 2, 2, 4), ALL_AXES)
    placed = P(TM, ROW_AXES, None, None)
    return jax.shard_map(
        on_device,
        mesh=fine,
        in_specs=(placed, P(), P(), P(), P(), placed),
        out_specs=(placed, placed, P(ALL_AXES, None)),
        check_vma=False,
    )
```

```python
import functools
import math

import jax
import jax.numpy as jnp
from jax import lax
from jax.experimental import pallas as pl
from jax.experimental.pallas import tpu as pltpu
from jax.sharding import Mesh
from jax.sharding import PartitionSpec as P

GROUPS = 32
EPS = 1e-05
CHAN = 384
HALF = CHAN // 2
SLOTS = 8
ROWS = 4
COLS = 32
CELLS = ROWS * COLS
POS = SLOTS * CELLS
WIDE = 3 * CHAN
PIECE = 81
CHIPS = 64
LANES = 128
TILE = 256

TM = ("ylo", "z", "core")
ROW_AXES = ("yhi", "x")
CHIP_AXES = ("ylo", "z", "yhi", "x")
ALL_AXES = TM + ROW_AXES

bf16 = jnp.bfloat16
f32 = jnp.float32
VMEM_LIMIT = pltpu.CompilerParams(vmem_limit_bytes=60 * 1024 * 1024)


def from_left(values):
    col = lax.broadcasted_iota(jnp.int32, values.shape, 0) % COLS
    return jnp.where(col == 0, 0.0, pltpu.roll(values, 1, 0))


def from_right(values):
    col = lax.broadcasted_iota(jnp.int32, values.shape, 0) % COLS
    return jnp.where(col == COLS - 1, 0.0, pltpu.roll(values, values.shape[0] - 1, 0))


def tap_products(x_ref, w_ref, acc, back):
    step = pl.program_id(0)
    weights = w_ref[...]
    pieces = []
    for b in range(3):
        at = (2 - step, 2 - b) if back else (step, b)
        pieces.append(x_ref[pl.ds(at[0], SLOTS), pl.ds(at[1], ROWS)].reshape(POS, CHAN))
    left = jnp.concatenate(pieces, axis=1)
    if back:
        right = jnp.concatenate([weights[b * WIDE : (b + 1) * WIDE] for b in range(3)], axis=1)
        dims = (((1,), (1,)), ((), ()))
    else:
        right = jnp.concatenate(
            [
                jnp.concatenate(
                    [weights[(b * 3 + c) * CHAN : (b * 3 + c + 1) * CHAN] for c in range(3)], axis=1
                )
                for b in range(3)
            ],
            axis=0,
        )
        dims = (((1,), (0,)), ((), ()))
    product = lax.dot_general(left, right, dims, preferred_element_type=f32)

    @pl.when(step == 0)
    def _():
        acc[...] = product

    @pl.when(step > 0)
    def _():
        acc[...] += product


def forward_kernel(count_ref, x_ref, w_ref, act_ref, out_ref, acc):
    tap_products(x_ref, w_ref, acc, False)

    @pl.when(pl.program_id(0) == 2)
    def _():
        for frame in range(SLOTS):
            rows = slice(frame * CELLS, (frame + 1) * CELLS)
            conv = (
                acc[rows, CHAN : 2 * CHAN]
                + from_left(acc[rows, :CHAN])
                + from_right(acc[rows, 2 * CHAN :])
            )
            total = act_ref[rows].astype(f32) + conv
            out_ref[rows] = jnp.where(frame < count_ref[0], total, 0.0).astype(bf16)


def backward_kernel(
    x_ref, w_ref, act_ref, mean_ref, inv_ref, gain_ref, bias_ref, out_ref, first_ref, second_ref, acc
):
    tap_products(x_ref, w_ref, acc, True)

    @pl.when(pl.program_id(0) == 2)
    def _():
        gain = gain_ref[...]
        bias = bias_ref[...]
        for frame in range(SLOTS):
            rows = slice(frame * CELLS, (frame + 1) * CELLS)
            grad = (
                acc[rows, CHAN : 2 * CHAN]
                + from_right(acc[rows, :CHAN])
                + from_left(acc[rows, 2 * CHAN :])
            )
            centred = (act_ref[rows].astype(f32) - mean_ref[frame : frame + 1]) * inv_ref[
                frame : frame + 1
            ]
            pre_act = centred * gain + bias
            gate = jax.nn.sigmoid(pre_act)
            pre_grad = grad * gate * (1.0 + pre_act * (1.0 - gate)) * gain
            out_ref[rows] = pre_grad
            first_ref[frame : frame + 1] = jnp.sum(pre_grad, axis=0, keepdims=True)
            second_ref[frame : frame + 1] = jnp.sum(pre_grad * centred, axis=0, keepdims=True)


READY = ((0, 2), (2, 5), (5, 8))


def weight_kernel(h0_ref, h1_ref, c0_ref, c1_ref, out_ref, turned, sums, packed, sems):
    for half, h_ref in enumerate((h0_ref, h1_ref)):

        def turn(m, carry, h_ref=h_ref, half=half):
            values = h_ref[pl.ds(pl.multiple_of(m * 256, 256), 256)].astype(f32)
            cols = pl.ds(pl.multiple_of(half * POS + m * 256, 256), 256)
            for c, moved in enumerate((from_left(values), values, from_right(values))):
                turned[c * CHAN : (c + 1) * CHAN, cols] = moved.T.astype(bf16)
            return carry

        lax.fori_loop(0, POS // 256, turn, 0)

    upper = lax.broadcasted_iota(jnp.int32, (PIECE, LANES), 1) >= LANES // 2
    copies = []
    for a in range(3):
        right = jnp.concatenate(
            [
                jnp.concatenate(
                    [
                        ref[2 - a : 2 - a + SLOTS, 2 - b : 2 - b + ROWS].reshape(POS, TILE)
                        for ref in (c0_ref, c1_ref)
                    ],
                    axis=0,
                )
                for b in range(3)
            ],
            axis=1,
        )
        product = jnp.dot(turned[...], right, preferred_element_type=f32)
        for b in range(3):
            at = (a * 3 + b) * WIDE
            sums[at : at + WIDE] = product[:, b * TILE : (b + 1) * TILE]
        for chip in range(8 * READY[a][0], 8 * READY[a][1]):
            start = 1296 * (chip // 8) + PIECE * (chip % 8)
            first, second = sums[start : start + PIECE], sums[start + 648 : start + 648 + PIECE]
            block = jnp.concatenate(
                [
                    first[:, :LANES],
                    second[:, :LANES],
                    jnp.where(upper, second[:, LANES:], first[:, LANES:]),
                ],
                axis=0,
            )
            packed[chip] = block.astype(bf16)
        chips = pl.ds(8 * READY[a][0], 8 * (READY[a][1] - READY[a][0]))
        copies.append(pltpu.make_async_copy(packed.at[chips], out_ref.at[chips], sems.at[a]))
        copies[-1].start()
    for copy in copies:
        copy.wait()


def whole(shape):
    return pl.BlockSpec(shape, lambda step: (0,) * len(shape))


def cost(flops, moved):
    return pl.CostEstimate(flops=flops, bytes_accessed=moved, transcendentals=0)


FLOPS = 2 * POS * 27 * CHAN * CHAN
TAPS_SPEC = pl.BlockSpec((3 * WIDE, CHAN), lambda step: (step, 0))


def forward_conv(count, extended, weights, act):
    return pl.pallas_call(
        forward_kernel,
        out_shape=jax.ShapeDtypeStruct((POS, CHAN), bf16),
        grid=(3,),
        in_specs=[
            pl.BlockSpec(memory_space=pltpu.SMEM),
            whole(extended.shape),
            TAPS_SPEC,
            whole(act.shape),
        ],
        out_specs=whole((POS, CHAN)),
        scratch_shapes=[pltpu.VMEM((POS, WIDE), f32)],
        compiler_params=VMEM_LIMIT,
        cost_estimate=cost(FLOPS, 12 << 20),
        name="forward_conv",
    )(count, extended, weights, act)


def backward_conv(extended, weights, act, mean, inv, gain, bias):
    return pl.pallas_call(
        backward_kernel,
        out_shape=(
            jax.ShapeDtypeStruct((POS, CHAN), f32),
            jax.ShapeDtypeStruct((SLOTS, CHAN), f32),
            jax.ShapeDtypeStruct((SLOTS, CHAN), f32),
        ),
        grid=(3,),
        in_specs=[
            whole(extended.shape),
            TAPS_SPEC,
            whole(act.shape),
            whole(mean.shape),
            whole(inv.shape),
            whole(gain.shape),
            whole(bias.shape),
        ],
        out_specs=(whole((POS, CHAN)), whole((SLOTS, CHAN)), whole((SLOTS, CHAN))),
        scratch_shapes=[pltpu.VMEM((POS, WIDE), f32)],
        compiler_params=VMEM_LIMIT,
        cost_estimate=cost(FLOPS, 12 << 20),
        name="backward_conv",
    )(extended, weights, act, mean, inv, gain, bias)


def weight_terms(hidden, other_hidden, cots, other_cots):
    return pl.pallas_call(
        weight_kernel,
        out_shape=jax.ShapeDtypeStruct((CHIPS, 3 * PIECE, LANES), bf16),
        in_specs=[pl.BlockSpec(memory_space=pltpu.VMEM)] * 4,
        out_specs=pl.BlockSpec(memory_space=pl.ANY),
        scratch_shapes=[
            pltpu.VMEM((WIDE, 2 * POS), bf16),
            pltpu.VMEM((9 * WIDE, TILE), f32),
            pltpu.VMEM((CHIPS, 3 * PIECE, LANES), bf16),
            pltpu.SemaphoreType.DMA((3,)),
        ],
        compiler_params=VMEM_LIMIT,
        cost_estimate=cost(FLOPS, 12 << 20),
        name="weight_terms",
    )(hidden, other_hidden, cots, other_cots)


def shift(values, axes, count, step):
    pairs = [(i, i + step) for i in range(count) if 0 <= i + step < count]
    return lax.ppermute(values, axes, pairs)


def swap_cores(values):
    return lax.ppermute(values, "core", [(0, 1), (1, 0)])


def edge_rows(block):
    low = shift(block[:, ROWS - 1 :], ROW_AXES, 8, 1)
    high = shift(block[:, :1], ROW_AXES, 8, -1)
    return low, high


def half_columns(cots, second):
    halves = [
        jnp.concatenate([cots[..., at : at + HALF], cots[..., at + LANES : at + HALF]], axis=3)
        for at in (0, HALF)
    ]
    return jnp.where(second, halves[1], halves[0])


def per_group(first, second):
    grouped = jnp.concatenate([first, second], axis=0).reshape(2 * SLOTS, GROUPS, CHAN // GROUPS)
    return jnp.sum(grouped, axis=2)


def over_rows(sums):
    spread = jnp.broadcast_to(sums[None], (8,) + sums.shape)
    return jnp.sum(lax.all_to_all(spread, ROW_AXES, 0, 0), axis=0)


def add_pairs(sums, axis, pairs):
    return sums + lax.ppermute(sums, axis, pairs + [(b, a) for a, b in pairs])


def per_channel(grouped):
    return jnp.repeat(grouped, CHAN // GROUPS, axis=1)


def on_device(activations, frame_counts, norm_gain, norm_bias, conv_weight, cotangent):
    core = lax.axis_index("core")
    cell_count = 8 * CELLS * (CHAN // GROUPS)
    act = activations.reshape(POS, CHAN)

    values = activations.astype(f32)
    sums = per_group(jnp.sum(values, axis=(1, 2)), jnp.sum(values * values, axis=(1, 2)))
    sums = over_rows(sums)
    next_head = shift(cotangent[:2], TM, 16, -1)
    sums, next_head, cotangent = lax.optimization_barrier((sums, next_head, cotangent))

    count = frame_counts[lax.axis_index(TM)]
    live = (jnp.arange(SLOTS) < count)[:, None, None, None]
    grads = jnp.where(live, cotangent, jnp.zeros_like(cotangent))
    pair = jnp.zeros((2, ROWS, COLS, CHAN), bf16)
    future = lax.dynamic_update_slice_in_dim(
        jnp.concatenate([grads, pair], 0), next_head, count, 0
    )
    low, high = edge_rows(future)

    group_mean = sums[:SLOTS] / cell_count
    inv_std = lax.rsqrt(sums[SLOTS:] / cell_count - group_mean * group_mean + EPS)
    mean = per_channel(group_mean)
    inv = per_channel(inv_std)

    def normed(rows):
        return (rows.astype(f32) - mean[:, None, None, :]) * inv[:, None, None, :]

    def activated(rows, keep):
        pre_act = normed(rows) * norm_gain + norm_bias
        return jnp.where(keep, jax.nn.silu(pre_act), 0.0).astype(bf16)

    hidden = activated(activations, live)
    hidden_there = swap_cores(hidden)
    last_pair = lax.dynamic_slice_in_dim(jnp.concatenate([pair, hidden], 0), count, 2, 0)
    before = shift(last_pair, TM, 16, 1)
    low, high, before, hidden = lax.optimization_barrier((low, high, before, hidden))
    cots = jnp.concatenate([low, future, high], axis=1)
    cots_here = half_columns(cots, core == 1)
    cots_there = swap_cores(half_columns(cots, core == 0))
    frames = jnp.concatenate([before, hidden], 0)
    low, high = edge_rows(frames)

    terms = weight_terms(
        hidden.reshape(POS, CHAN), hidden_there.reshape(POS, CHAN), cots_here, cots_there
    )
    terms, low, high = lax.optimization_barrier((terms, low, high))
    arrived = lax.all_to_all(terms, CHIP_AXES, 0, 0)

    cots, _ = lax.optimization_barrier((cots, terms))
    pre_grad, first_grad, second_grad = backward_conv(
        cots, conv_weight, act, mean, inv, norm_gain[None], norm_bias[None]
    )
    sums = per_group(first_grad, second_grad)
    parts = [lax.ppermute(sums, "x", [(i, (i + k) % 4) for i in range(4)]) for k in range(1, 4)]

    extended = jnp.concatenate([low, frames, high], axis=1)
    block_out = forward_conv(count[None], extended, conv_weight, act)
    block_out, parts, arrived = lax.optimization_barrier((block_out, parts, arrived))
    block_out = block_out.reshape(activations.shape)

    sums = add_pairs(sums + parts[0] + parts[1] + parts[2], "yhi", [(0, 1)])
    first_avg = per_channel(sums[:SLOTS] / cell_count)[:, None, None, :]
    second_avg = per_channel(sums[SLOTS:] / cell_count)[:, None, None, :]
    norm_part = inv[:, None, None, :] * (
        pre_grad.reshape(activations.shape) - first_avg - normed(activations) * second_avg
    )
    input_grad = jnp.where(live, grads.astype(f32) + norm_part, 0.0)

    frame_total = 1 + 4 * ((16 - 1) * 3 // 2)
    grad_scale = 1.0 / math.sqrt(frame_total * 8 * ROWS * COLS)
    total = jnp.sum(arrived.astype(f32), axis=0) * grad_scale
    shared = total[2 * PIECE :]
    parts = [
        jnp.concatenate(
            [total[k * PIECE : (k + 1) * PIECE], shared[:, k * 64 : (k + 1) * 64]], axis=1
        )
        for k in range(2)
    ]
    kept = jnp.where(core == 0, parts[0], parts[1])
    got = swap_cores(jnp.where(core == 0, parts[1], parts[0]))
    weight_grad = jnp.where(
        core == 0, jnp.concatenate([kept, got], 1), jnp.concatenate([got, kept], 1)
    )
    return block_out, input_grad, weight_grad


def solution(mesh):
    fine = Mesh(mesh.devices.reshape(2, 4, 2, 2, 4), ALL_AXES)
    placed = P(TM, ROW_AXES, None, None)
    return jax.shard_map(
        on_device,
        mesh=fine,
        in_specs=(placed, P(), P(), P(), P(), placed),
        out_specs=(placed, placed, P(ALL_AXES, None)),
        check_vma=False,
    )
```

```python
import functools
import math

import jax
import jax.numpy as jnp
from jax import lax
from jax.experimental import pallas as pl
from jax.experimental.pallas import tpu as pltpu
from jax.sharding import Mesh
from jax.sharding import PartitionSpec as P

GROUPS = 32
EPS = 1e-05
CHAN = 384
HALF = CHAN // 2
SLOTS = 8
ROWS = 4
COLS = 32
CELLS = ROWS * COLS
POS = SLOTS * CELLS
WIDE = 3 * CHAN
PIECE = 81
CHIPS = 64
LANES = 128
TILE = 256

TM = ("ylo", "z", "core")
ROW_AXES = ("yhi", "x")
CHIP_AXES = ("ylo", "z", "yhi", "x")
ALL_AXES = TM + ROW_AXES

bf16 = jnp.bfloat16
f32 = jnp.float32
VMEM_LIMIT = pltpu.CompilerParams(vmem_limit_bytes=60 * 1024 * 1024)


def from_left(values):
    col = lax.broadcasted_iota(jnp.int32, values.shape, 0) % COLS
    return jnp.where(col == 0, 0.0, pltpu.roll(values, 1, 0))


def from_right(values):
    col = lax.broadcasted_iota(jnp.int32, values.shape, 0) % COLS
    return jnp.where(col == COLS - 1, 0.0, pltpu.roll(values, values.shape[0] - 1, 0))


def tap_products(x_ref, w_ref, acc, back):
    step = pl.program_id(0)
    weights = w_ref[...]
    pieces = []
    for b in range(3):
        at = (2 - step, 2 - b) if back else (step, b)
        pieces.append(x_ref[pl.ds(at[0], SLOTS), pl.ds(at[1], ROWS)].reshape(POS, CHAN))
    left = jnp.concatenate(pieces, axis=1)
    if back:
        right = jnp.concatenate([weights[b * WIDE : (b + 1) * WIDE] for b in range(3)], axis=1)
        dims = (((1,), (1,)), ((), ()))
    else:
        right = jnp.concatenate(
            [
                jnp.concatenate(
                    [weights[(b * 3 + c) * CHAN : (b * 3 + c + 1) * CHAN] for c in range(3)], axis=1
                )
                for b in range(3)
            ],
            axis=0,
        )
        dims = (((1,), (0,)), ((), ()))
    product = lax.dot_general(left, right, dims, preferred_element_type=f32)

    @pl.when(step == 0)
    def _():
        acc[...] = product

    @pl.when(step > 0)
    def _():
        acc[...] += product


def forward_kernel(count_ref, x_ref, w_ref, act_ref, out_ref, acc):
    tap_products(x_ref, w_ref, acc, False)

    @pl.when(pl.program_id(0) == 2)
    def _():
        for frame in range(SLOTS):
            rows = slice(frame * CELLS, (frame + 1) * CELLS)
            conv = (
                acc[rows, CHAN : 2 * CHAN]
                + from_left(acc[rows, :CHAN])
                + from_right(acc[rows, 2 * CHAN :])
            )
            total = act_ref[rows].astype(f32) + conv
            out_ref[rows] = jnp.where(frame < count_ref[0], total, 0.0).astype(bf16)


def backward_kernel(
    x_ref, w_ref, act_ref, mean_ref, inv_ref, gain_ref, bias_ref, out_ref, first_ref, second_ref, acc
):
    tap_products(x_ref, w_ref, acc, True)

    @pl.when(pl.program_id(0) == 2)
    def _():
        gain = gain_ref[...]
        bias = bias_ref[...]
        for frame in range(SLOTS):
            rows = slice(frame * CELLS, (frame + 1) * CELLS)
            grad = (
                acc[rows, CHAN : 2 * CHAN]
                + from_right(acc[rows, :CHAN])
                + from_left(acc[rows, 2 * CHAN :])
            )
            centred = (act_ref[rows].astype(f32) - mean_ref[frame : frame + 1]) * inv_ref[
                frame : frame + 1
            ]
            pre_act = centred * gain + bias
            gate = jax.nn.sigmoid(pre_act)
            pre_grad = grad * gate * (1.0 + pre_act * (1.0 - gate)) * gain
            out_ref[rows] = pre_grad
            first_ref[frame : frame + 1] = jnp.sum(pre_grad, axis=0, keepdims=True)
            second_ref[frame : frame + 1] = jnp.sum(pre_grad * centred, axis=0, keepdims=True)


READY = ((0, 2), (2, 5), (5, 8))


def weight_kernel(h0_ref, h1_ref, c0_ref, c1_ref, out_ref, turned, sums, packed, sems):
    for half, h_ref in enumerate((h0_ref, h1_ref)):

        def turn(m, carry, h_ref=h_ref, half=half):
            values = h_ref[pl.ds(pl.multiple_of(m * 256, 256), 256)].astype(f32)
            cols = pl.ds(pl.multiple_of(half * POS + m * 256, 256), 256)
            for c, moved in enumerate((from_left(values), values, from_right(values))):
                turned[c * CHAN : (c + 1) * CHAN, cols] = moved.T.astype(bf16)
            return carry

        lax.fori_loop(0, POS // 256, turn, 0)

    upper = lax.broadcasted_iota(jnp.int32, (PIECE, LANES), 1) >= LANES // 2
    copies = []
    for a in range(3):
        right = jnp.concatenate(
            [
                jnp.concatenate(
                    [
                        ref[2 - a : 2 - a + SLOTS, 2 - b : 2 - b + ROWS].reshape(POS, TILE)
                        for ref in (c0_ref, c1_ref)
                    ],
                    axis=0,
                )
                for b in range(3)
            ],
            axis=1,
        )
        product = jnp.dot(turned[...], right, preferred_element_type=f32)
        for b in range(3):
            at = (a * 3 + b) * WIDE
            sums[at : at + WIDE] = product[:, b * TILE : (b + 1) * TILE]
        for chip in range(8 * READY[a][0], 8 * READY[a][1]):
            start = 1296 * (chip // 8) + PIECE * (chip % 8)
            first, second = sums[start : start + PIECE], sums[start + 648 : start + 648 + PIECE]
            block = jnp.concatenate(
                [
                    first[:, :LANES],
                    second[:, :LANES],
                    jnp.where(upper, second[:, LANES:], first[:, LANES:]),
                ],
                axis=0,
            )
            packed[chip] = block.astype(bf16)
        chips = pl.ds(8 * READY[a][0], 8 * (READY[a][1] - READY[a][0]))
        copies.append(pltpu.make_async_copy(packed.at[chips], out_ref.at[chips], sems.at[a]))
        copies[-1].start()
    for copy in copies:
        copy.wait()


def whole(shape):
    return pl.BlockSpec(shape, lambda step: (0,) * len(shape))


def cost(flops, moved):
    return pl.CostEstimate(flops=flops, bytes_accessed=moved, transcendentals=0)


FLOPS = 2 * POS * 27 * CHAN * CHAN
TAPS_SPEC = pl.BlockSpec((3 * WIDE, CHAN), lambda step: (step, 0))


def forward_conv(count, extended, weights, act):
    return pl.pallas_call(
        forward_kernel,
        out_shape=jax.ShapeDtypeStruct((POS, CHAN), bf16),
        grid=(3,),
        in_specs=[
            pl.BlockSpec(memory_space=pltpu.SMEM),
            whole(extended.shape),
            TAPS_SPEC,
            whole(act.shape),
        ],
        out_specs=whole((POS, CHAN)),
        scratch_shapes=[pltpu.VMEM((POS, WIDE), f32)],
        compiler_params=VMEM_LIMIT,
        cost_estimate=cost(FLOPS, 12 << 20),
        name="forward_conv",
    )(count, extended, weights, act)


def backward_conv(extended, weights, act, mean, inv, gain, bias):
    return pl.pallas_call(
        backward_kernel,
        out_shape=(
            jax.ShapeDtypeStruct((POS, CHAN), f32),
            jax.ShapeDtypeStruct((SLOTS, CHAN), f32),
            jax.ShapeDtypeStruct((SLOTS, CHAN), f32),
        ),
        grid=(3,),
        in_specs=[
            whole(extended.shape),
            TAPS_SPEC,
            whole(act.shape),
            whole(mean.shape),
            whole(inv.shape),
            whole(gain.shape),
            whole(bias.shape),
        ],
        out_specs=(whole((POS, CHAN)), whole((SLOTS, CHAN)), whole((SLOTS, CHAN))),
        scratch_shapes=[pltpu.VMEM((POS, WIDE), f32)],
        compiler_params=VMEM_LIMIT,
        cost_estimate=cost(FLOPS, 12 << 20),
        name="backward_conv",
    )(extended, weights, act, mean, inv, gain, bias)


def weight_terms(hidden, other_hidden, cots, other_cots):
    return pl.pallas_call(
        weight_kernel,
        out_shape=jax.ShapeDtypeStruct((CHIPS, 3 * PIECE, LANES), bf16),
        in_specs=[pl.BlockSpec(memory_space=pltpu.VMEM)] * 4,
        out_specs=pl.BlockSpec(memory_space=pl.ANY),
        scratch_shapes=[
            pltpu.VMEM((WIDE, 2 * POS), bf16),
            pltpu.VMEM((9 * WIDE, TILE), f32),
            pltpu.VMEM((CHIPS, 3 * PIECE, LANES), bf16),
            pltpu.SemaphoreType.DMA((3,)),
        ],
        compiler_params=VMEM_LIMIT,
        cost_estimate=cost(FLOPS, 12 << 20),
        name="weight_terms",
    )(hidden, other_hidden, cots, other_cots)


def shift(values, axes, count, step):
    pairs = [(i, i + step) for i in range(count) if 0 <= i + step < count]
    return lax.ppermute(values, axes, pairs)


def swap_cores(values):
    return lax.ppermute(values, "core", [(0, 1), (1, 0)])


def diagonal(values, step):
    pairs = [
        (tm * 8 + row, (tm - 1) * 8 + row + step)
        for tm in range(1, 16)
        for row in range(8)
        if 0 <= row + step < 8
    ]
    return lax.ppermute(values, ALL_AXES, pairs)


def edge_rows(block):
    low = shift(block[:, ROWS - 1 :], ROW_AXES, 8, 1)
    high = shift(block[:, :1], ROW_AXES, 8, -1)
    return low, high


def half_columns(cots, second):
    halves = [
        jnp.concatenate([cots[..., at : at + HALF], cots[..., at + LANES : at + HALF]], axis=3)
        for at in (0, HALF)
    ]
    return jnp.where(second, halves[1], halves[0])


def per_group(first, second):
    grouped = jnp.concatenate([first, second], axis=0).reshape(2 * SLOTS, GROUPS, CHAN // GROUPS)
    return jnp.sum(grouped, axis=2)


def over_rows(sums):
    spread = jnp.broadcast_to(sums[None], (8,) + sums.shape)
    return jnp.sum(lax.all_to_all(spread, ROW_AXES, 0, 0), axis=0)


def add_pairs(sums, axis, pairs):
    return sums + lax.ppermute(sums, axis, pairs + [(b, a) for a, b in pairs])


def per_channel(grouped):
    return jnp.repeat(grouped, CHAN // GROUPS, axis=1)


def on_device(activations, frame_counts, norm_gain, norm_bias, conv_weight, cotangent):
    core = lax.axis_index("core")
    cell_count = 8 * CELLS * (CHAN // GROUPS)
    act = activations.reshape(POS, CHAN)

    values = activations.astype(f32)
    sums = per_group(jnp.sum(values, axis=(1, 2)), jnp.sum(values * values, axis=(1, 2)))
    sums = over_rows(sums)
    low, high = edge_rows(jnp.concatenate([activations, cotangent], 0))
    head = cotangent[:2]
    next_head = [
        diagonal(head[:, ROWS - 1 :], 1),
        shift(head, TM, 16, -1),
        diagonal(head[:, :1], -1),
    ]
    sums, low, high, next_head, cotangent = lax.optimization_barrier(
        (sums, low, high, next_head, cotangent)
    )

    count = frame_counts[lax.axis_index(TM)]
    live = (jnp.arange(SLOTS) < count)[:, None, None, None]
    row_place = lax.axis_index(ROW_AXES)

    group_mean = sums[:SLOTS] / cell_count
    inv_std = lax.rsqrt(sums[SLOTS:] / cell_count - group_mean * group_mean + EPS)
    mean = per_channel(group_mean)
    inv = per_channel(inv_std)

    def normed(rows):
        return (rows.astype(f32) - mean[:, None, None, :]) * inv[:, None, None, :]

    def activated(rows, keep):
        pre_act = normed(rows) * norm_gain + norm_bias
        return jnp.where(keep, jax.nn.silu(pre_act), 0.0).astype(bf16)

    hidden = activated(activations, live)
    hidden_there = swap_cores(hidden)
    grads = jnp.where(live, cotangent, jnp.zeros_like(cotangent))
    wide_grads = jnp.concatenate(
        [
            jnp.where(live, low[SLOTS:], jnp.zeros_like(low[SLOTS:])),
            grads,
            jnp.where(live, high[SLOTS:], jnp.zeros_like(high[SLOTS:])),
        ],
        axis=1,
    )
    pair = jnp.zeros((2, ROWS + 2, COLS, CHAN), bf16)
    cots = lax.dynamic_update_slice_in_dim(
        jnp.concatenate([wide_grads, pair], 0), jnp.concatenate(next_head, axis=1), count, 0
    )
    cots_here = half_columns(cots, core == 1)
    cots_there = swap_cores(half_columns(cots, core == 0))
    wide_hidden = jnp.concatenate(
        [
            activated(low[:SLOTS], live & (row_place > 0)),
            hidden,
            activated(high[:SLOTS], live & (row_place < 7)),
        ],
        axis=1,
    )
    last_pair = lax.dynamic_slice_in_dim(jnp.concatenate([pair, wide_hidden], 0), count, 2, 0)
    before = shift(last_pair, TM, 16, 1)

    terms = weight_terms(
        hidden.reshape(POS, CHAN), hidden_there.reshape(POS, CHAN), cots_here, cots_there
    )
    terms, before = lax.optimization_barrier((terms, before))
    arrived = lax.all_to_all(terms, CHIP_AXES, 0, 0)

    cots, _ = lax.optimization_barrier((cots, terms))
    pre_grad, first_grad, second_grad = backward_conv(
        cots, conv_weight, act, mean, inv, norm_gain[None], norm_bias[None]
    )
    sums = per_group(first_grad, second_grad)
    parts = [lax.ppermute(sums, "x", [(i, (i + k) % 4) for i in range(4)]) for k in range(1, 4)]

    extended = jnp.concatenate([before, wide_hidden], axis=0)
    block_out = forward_conv(count[None], extended, conv_weight, act)
    block_out, parts, arrived = lax.optimization_barrier((block_out, parts, arrived))
    block_out = block_out.reshape(activations.shape)

    sums = add_pairs(sums + parts[0] + parts[1] + parts[2], "yhi", [(0, 1)])
    first_avg = per_channel(sums[:SLOTS] / cell_count)[:, None, None, :]
    second_avg = per_channel(sums[SLOTS:] / cell_count)[:, None, None, :]
    norm_part = inv[:, None, None, :] * (
        pre_grad.reshape(activations.shape) - first_avg - normed(activations) * second_avg
    )
    input_grad = jnp.where(live, grads.astype(f32) + norm_part, 0.0)

    frame_total = 1 + 4 * ((16 - 1) * 3 // 2)
    grad_scale = 1.0 / math.sqrt(frame_total * 8 * ROWS * COLS)
    total = jnp.sum(arrived.astype(f32), axis=0) * grad_scale
    shared = total[2 * PIECE :]
    parts = [
        jnp.concatenate(
            [total[k * PIECE : (k + 1) * PIECE], shared[:, k * 64 : (k + 1) * 64]], axis=1
        )
        for k in range(2)
    ]
    kept = jnp.where(core == 0, parts[0], parts[1])
    got = swap_cores(jnp.where(core == 0, parts[1], parts[0]))
    weight_grad = jnp.where(
        core == 0, jnp.concatenate([kept, got], 1), jnp.concatenate([got, kept], 1)
    )
    return block_out, input_grad, weight_grad


def solution(mesh):
    fine = Mesh(mesh.devices.reshape(2, 4, 2, 2, 4), ALL_AXES)
    placed = P(TM, ROW_AXES, None, None)
    return jax.shard_map(
        on_device,
        mesh=fine,
        in_specs=(placed, P(), P(), P(), P(), placed),
        out_specs=(placed, placed, P(ALL_AXES, None)),
        check_vma=False,
    )
```

```python
import functools
import math

import jax
import jax.numpy as jnp
import numpy as np
from jax import lax
from jax.experimental import pallas as pl
from jax.experimental.pallas import tpu as pltpu
from jax.sharding import Mesh
from jax.sharding import PartitionSpec as P

GROUPS = 32
EPS = 1e-05
CHAN = 384
HALF = CHAN // 2
SLOTS = 8
ROWS = 4
COLS = 32
CELLS = ROWS * COLS
POS = SLOTS * CELLS
WIDE = 3 * CHAN
PIECE = 81
CHIPS = 64
LANES = 128
WIDE_CELLS = (ROWS + 2) * COLS
CELL_COUNT = 8 * CELLS * (CHAN // GROUPS)
TILE = 256

TM = ("ylo", "z", "core")
ROW_AXES = ("yhi", "x")
CHIP_AXES = ("ylo", "z", "yhi", "x")
ALL_AXES = TM + ROW_AXES

bf16 = jnp.bfloat16
f32 = jnp.float32
VMEM_LIMIT = pltpu.CompilerParams(vmem_limit_bytes=60 * 1024 * 1024)


def from_left(values):
    col = lax.broadcasted_iota(jnp.int32, values.shape, 0) % COLS
    return jnp.where(col == 0, 0.0, pltpu.roll(values, 1, 0))


def from_right(values):
    col = lax.broadcasted_iota(jnp.int32, values.shape, 0) % COLS
    return jnp.where(col == COLS - 1, 0.0, pltpu.roll(values, values.shape[0] - 1, 0))


def tap_products(x_ref, w_ref, acc, back):
    step = pl.program_id(0)
    weights = w_ref[...]
    pieces = []
    for b in range(3):
        at = (2 - step, 2 - b) if back else (step, b)
        pieces.append(x_ref[pl.ds(at[0], SLOTS), pl.ds(at[1], ROWS)].reshape(POS, CHAN))
    left = jnp.concatenate(pieces, axis=1)
    if back:
        right = jnp.concatenate([weights[b * WIDE : (b + 1) * WIDE] for b in range(3)], axis=1)
        dims = (((1,), (1,)), ((), ()))
    else:
        right = jnp.concatenate(
            [
                jnp.concatenate(
                    [weights[(b * 3 + c) * CHAN : (b * 3 + c + 1) * CHAN] for c in range(3)], axis=1
                )
                for b in range(3)
            ],
            axis=0,
        )
        dims = (((1,), (0,)), ((), ()))
    product = lax.dot_general(left, right, dims, preferred_element_type=f32)

    @pl.when(step == 0)
    def _():
        acc[...] = product

    @pl.when(step > 0)
    def _():
        acc[...] += product


def forward_kernel(count_ref, x_ref, w_ref, act_ref, out_ref, acc):
    tap_products(x_ref, w_ref, acc, False)

    @pl.when(pl.program_id(0) == 2)
    def _():
        for frame in range(SLOTS):
            rows = slice(frame * CELLS, (frame + 1) * CELLS)
            conv = (
                acc[rows, CHAN : 2 * CHAN]
                + from_left(acc[rows, :CHAN])
                + from_right(acc[rows, 2 * CHAN :])
            )
            total = act_ref[rows].astype(f32) + conv
            out_ref[rows] = jnp.where(frame < count_ref[0], total, 0.0).astype(bf16)


def backward_kernel(
    x_ref, w_ref, act_ref, mean_ref, inv_ref, gain_ref, bias_ref, out_ref, first_ref, second_ref, acc
):
    tap_products(x_ref, w_ref, acc, True)

    @pl.when(pl.program_id(0) == 2)
    def _():
        gain = gain_ref[...]
        bias = bias_ref[...]
        for frame in range(SLOTS):
            rows = slice(frame * CELLS, (frame + 1) * CELLS)
            grad = (
                acc[rows, CHAN : 2 * CHAN]
                + from_right(acc[rows, :CHAN])
                + from_left(acc[rows, 2 * CHAN :])
            )
            centred = (act_ref[rows].astype(f32) - mean_ref[frame : frame + 1]) * inv_ref[
                frame : frame + 1
            ]
            pre_act = centred * gain + bias
            gate = jax.nn.sigmoid(pre_act)
            pre_grad = grad * gate * (1.0 + pre_act * (1.0 - gate)) * gain
            out_ref[rows] = pre_grad
            first_ref[frame : frame + 1] = jnp.sum(pre_grad, axis=0, keepdims=True)
            second_ref[frame : frame + 1] = jnp.sum(pre_grad * centred, axis=0, keepdims=True)


READY = ((0, 2), (2, 5), (5, 8))


def weight_kernel(hidden_ref, kept_ref, got_ref, out_ref, turned, sums, packed, sems):
    def turn(f, carry):
        theirs = [got_ref[pl.ds(pl.multiple_of((f * 3 + g) * CELLS, CELLS), CELLS)] for g in range(3)]
        for half, values in enumerate(
            (
                hidden_ref[f, 1 : 1 + ROWS].reshape(CELLS, CHAN),
                jnp.concatenate(theirs, axis=1),
            )
        ):
            values = values.astype(f32)
            cols = pl.ds(pl.multiple_of(half * POS + f * CELLS, CELLS), CELLS)
            for c, moved in enumerate((from_left(values), values, from_right(values))):
                turned[c * CHAN : (c + 1) * CHAN, cols] = moved.T.astype(bf16)
        return carry

    lax.fori_loop(0, SLOTS, turn, 0)

    upper = lax.broadcasted_iota(jnp.int32, (PIECE, LANES), 1) >= LANES // 2
    copies = []
    for a in range(3):
        right = jnp.concatenate(
            [
                jnp.concatenate(
                    [
                        ref[start : start + CELLS]
                        for ref, base in ((kept_ref, 0), (got_ref, 3 * POS))
                        for f in range(SLOTS)
                        for start in [base + ((2 - a + f) * 2 + g) * WIDE_CELLS + (2 - b) * COLS]
                    ],
                    axis=0,
                )
                for b in range(3)
                for g in range(2)
            ],
            axis=1,
        )
        product = jnp.dot(turned[...], right, preferred_element_type=f32)
        for b in range(3):
            at = (a * 3 + b) * WIDE
            sums[at : at + WIDE] = product[:, b * TILE : (b + 1) * TILE]
        for chip in range(8 * READY[a][0], 8 * READY[a][1]):
            start = 1296 * (chip // 8) + PIECE * (chip % 8)
            first, second = sums[start : start + PIECE], sums[start + 648 : start + 648 + PIECE]
            block = jnp.concatenate(
                [
                    first[:, :LANES],
                    second[:, :LANES],
                    jnp.where(upper, second[:, LANES:], first[:, LANES:]),
                ],
                axis=0,
            )
            packed[chip] = block.astype(bf16)
        chips = pl.ds(8 * READY[a][0], 8 * (READY[a][1] - READY[a][0]))
        copies.append(pltpu.make_async_copy(packed.at[chips], out_ref.at[chips], sems.at[a]))
        copies[-1].start()
    for copy in copies:
        copy.wait()


def sums_kernel(act_ref, out_ref):
    firsts, seconds = [], []
    for frame in range(SLOTS):
        values = act_ref[frame].reshape(CELLS, CHAN).astype(f32)
        firsts.append(jnp.sum(values, axis=0, keepdims=True))
        seconds.append(jnp.sum(values * values, axis=0, keepdims=True))
    both = jnp.concatenate(firsts + seconds, axis=0)
    for peer in range(8):
        out_ref[peer] = both


def prepare_kernel(
    place_ref,
    peers_ref,
    same_ref,
    act_ref,
    cot_ref,
    low_ref,
    high_ref,
    head_ref,
    gain_ref,
    bias_ref,
    hidden_ref,
    cots_ref,
    kept_ref,
    sent_ref,
    pair_ref,
    mean_ref,
    inv_ref,
):
    count, core, row_place = place_ref[0], place_ref[1], place_ref[2]
    total = peers_ref[0]
    for peer in range(1, 8):
        total = total + peers_ref[peer]
    stats = jnp.dot(
        total, same_ref[...], precision=lax.Precision.HIGHEST, preferred_element_type=f32
    ) * (1.0 / CELL_COUNT)
    mean = stats[:SLOTS]
    inv = lax.rsqrt(stats[SLOTS:] - mean * mean + EPS)
    mean_ref[...] = mean
    inv_ref[...] = inv
    gain = gain_ref[...]
    bias = bias_ref[...]

    for frame in range(SLOTS):
        live = frame < count

        def activated(values, keep, frame=frame):
            centred = (values.astype(f32) - mean[frame : frame + 1]) * inv[frame : frame + 1]
            pre_act = centred * gain + bias
            return jnp.where(keep, pre_act * jax.nn.sigmoid(pre_act), 0.0).astype(bf16)

        def masked(values, live=live):
            return jnp.where(live, values.astype(f32), 0.0).astype(bf16)

        hidden = activated(act_ref[frame].reshape(CELLS, CHAN), live)
        hidden_ref[frame, 1 : 1 + ROWS] = hidden.reshape(ROWS, COLS, CHAN)
        for g in range(3):
            start = (frame * 3 + g) * CELLS
            sent_ref[start : start + CELLS] = hidden[:, g * LANES : (g + 1) * LANES]
        hidden_ref[frame, 0] = activated(low_ref[frame, 0], live & (row_place > 0))
        hidden_ref[frame, 1 + ROWS] = activated(high_ref[frame, 0], live & (row_place < 7))
        cots_ref[frame, 0] = masked(low_ref[SLOTS + frame, 0])
        cots_ref[frame, 1 : 1 + ROWS] = masked(cot_ref[frame])
        cots_ref[frame, 1 + ROWS] = masked(high_ref[SLOTS + frame, 0])
    cots_ref[SLOTS:] = jnp.zeros((2, ROWS + 2, COLS, CHAN), bf16)
    cots_ref[pl.ds(count, 2)] = head_ref[...]

    @pl.when(count >= 2)
    def _():
        pair_ref[...] = hidden_ref[pl.ds(jnp.maximum(count - 2, 0), 2)]

    @pl.when(count < 2)
    def _():
        pair_ref[0] = jnp.zeros((ROWS + 2, COLS, CHAN), bf16)
        pair_ref[1] = hidden_ref[0]

    left = lax.broadcasted_iota(jnp.int32, (WIDE_CELLS, LANES), 1) < LANES // 2
    for frame in range(SLOTS + 2):
        values = cots_ref[frame].reshape(WIDE_CELLS, CHAN)
        outer = values[:, :LANES], values[:, 2 * LANES :]
        middle = values[:, LANES : 2 * LANES].astype(f32)
        turned = pltpu.roll(middle, LANES // 2, 1)
        inner = (
            jnp.where(left, middle, turned).astype(bf16),
            jnp.where(left, turned, middle).astype(bf16),
        )
        for place in range(2):

            @pl.when(core == place)
            def _(frame=frame, place=place, outer=outer, inner=inner):
                at = frame * 2 * WIDE_CELLS
                for ref, base, k in ((kept_ref, 0, place), (sent_ref, 3 * POS, 1 - place)):
                    ref[base + at : base + at + WIDE_CELLS] = outer[k]
                    ref[base + at + WIDE_CELLS : base + at + 2 * WIDE_CELLS] = inner[k]


def whole(shape):
    return pl.BlockSpec(shape, lambda step: (0,) * len(shape))


def cost(flops, moved):
    return pl.CostEstimate(flops=flops, bytes_accessed=moved, transcendentals=0)


FLOPS = 2 * POS * 27 * CHAN * CHAN
TAPS_SPEC = pl.BlockSpec((3 * WIDE, CHAN), lambda step: (step, 0))


def forward_conv(count, extended, weights, act):
    return pl.pallas_call(
        forward_kernel,
        out_shape=jax.ShapeDtypeStruct((POS, CHAN), bf16),
        grid=(3,),
        in_specs=[
            pl.BlockSpec(memory_space=pltpu.SMEM),
            whole(extended.shape),
            TAPS_SPEC,
            whole(act.shape),
        ],
        out_specs=whole((POS, CHAN)),
        scratch_shapes=[pltpu.VMEM((POS, WIDE), f32)],
        compiler_params=VMEM_LIMIT,
        cost_estimate=cost(FLOPS, 12 << 20),
        name="forward_conv",
    )(count, extended, weights, act)


def backward_conv(extended, weights, act, mean, inv, gain, bias):
    return pl.pallas_call(
        backward_kernel,
        out_shape=(
            jax.ShapeDtypeStruct((POS, CHAN), f32),
            jax.ShapeDtypeStruct((SLOTS, CHAN), f32),
            jax.ShapeDtypeStruct((SLOTS, CHAN), f32),
        ),
        grid=(3,),
        in_specs=[
            whole(extended.shape),
            TAPS_SPEC,
            whole(act.shape),
            whole(mean.shape),
            whole(inv.shape),
            whole(gain.shape),
            whole(bias.shape),
        ],
        out_specs=(whole((POS, CHAN)), whole((SLOTS, CHAN)), whole((SLOTS, CHAN))),
        scratch_shapes=[pltpu.VMEM((POS, WIDE), f32)],
        compiler_params=VMEM_LIMIT,
        cost_estimate=cost(FLOPS, 12 << 20),
        name="backward_conv",
    )(extended, weights, act, mean, inv, gain, bias)


def local_sums(act):
    return pl.pallas_call(
        sums_kernel,
        out_shape=jax.ShapeDtypeStruct((8, 2 * SLOTS, CHAN), f32),
        compiler_params=VMEM_LIMIT,
        cost_estimate=cost(4 * POS * CHAN, 1 << 20),
        name="local_sums",
    )(act)


def prepare(place, peers, act, cot, low, high, head, gain, bias):
    group = np.arange(CHAN) // (CHAN // GROUPS)
    same = jnp.asarray((group[:, None] == group[None, :]).astype(np.float32))
    in_vmem = pl.BlockSpec(memory_space=pltpu.VMEM)
    wide = (ROWS + 2, COLS, CHAN)
    halves = 2 * (SLOTS + 2) * WIDE_CELLS
    return pl.pallas_call(
        prepare_kernel,
        out_shape=(
            jax.ShapeDtypeStruct((SLOTS,) + wide, bf16),
            jax.ShapeDtypeStruct((SLOTS + 2,) + wide, bf16),
            jax.ShapeDtypeStruct((halves, LANES), bf16),
            jax.ShapeDtypeStruct((3 * POS + halves, LANES), bf16),
            jax.ShapeDtypeStruct((2,) + wide, bf16),
            jax.ShapeDtypeStruct((SLOTS, CHAN), f32),
            jax.ShapeDtypeStruct((SLOTS, CHAN), f32),
        ),
        in_specs=[pl.BlockSpec(memory_space=pltpu.SMEM)] + [in_vmem] * 9,
        compiler_params=VMEM_LIMIT,
        cost_estimate=cost(40 * POS * CHAN, 10 << 20),
        name="prepare",
    )(place, peers, same, act, cot, low, high, head, gain, bias)


def weight_terms(hidden, kept, got):
    return pl.pallas_call(
        weight_kernel,
        out_shape=jax.ShapeDtypeStruct((CHIPS, 3 * PIECE, LANES), bf16),
        in_specs=[pl.BlockSpec(memory_space=pltpu.VMEM)] * 3,
        out_specs=pl.BlockSpec(memory_space=pl.ANY),
        scratch_shapes=[
            pltpu.VMEM((WIDE, 2 * POS), bf16),
            pltpu.VMEM((9 * WIDE, TILE), f32),
            pltpu.VMEM((CHIPS, 3 * PIECE, LANES), bf16),
            pltpu.SemaphoreType.DMA((3,)),
        ],
        compiler_params=VMEM_LIMIT,
        cost_estimate=cost(FLOPS, 12 << 20),
        name="weight_terms",
    )(hidden, kept, got)


def shift(values, axes, count, step):
    pairs = [(i, i + step) for i in range(count) if 0 <= i + step < count]
    return lax.ppermute(values, axes, pairs)


def swap_cores(values):
    return lax.ppermute(values, "core", [(0, 1), (1, 0)])


def edge_rows(block):
    low = shift(block[:, ROWS - 1 :], ROW_AXES, 8, 1)
    high = shift(block[:, :1], ROW_AXES, 8, -1)
    return low, high


def per_group(first, second):
    grouped = jnp.concatenate([first, second], axis=0).reshape(2 * SLOTS, GROUPS, CHAN // GROUPS)
    return jnp.sum(grouped, axis=2)


def add_pairs(sums, axis, pairs):
    return sums + lax.ppermute(sums, axis, pairs + [(b, a) for a, b in pairs])


def per_channel(grouped):
    return jnp.repeat(grouped, CHAN // GROUPS, axis=1)


def on_device(activations, frame_counts, norm_gain, norm_bias, conv_weight, cotangent):
    core = lax.axis_index("core")
    act = activations.reshape(POS, CHAN)
    gain, bias = norm_gain[None], norm_bias[None]

    sums = local_sums(activations)
    peers = lax.all_to_all(sums, ROW_AXES, 0, 0)
    source, rows_at_once, _ = lax.optimization_barrier((activations, cotangent, sums))
    low, high = edge_rows(jnp.concatenate([source, rows_at_once], 0))
    head = jnp.concatenate(
        [low[SLOTS : SLOTS + 2], cotangent[:2], high[SLOTS : SLOTS + 2]], axis=1
    )
    head = shift(head, TM, 16, -1)

    count = frame_counts[lax.axis_index(TM)]
    live = (jnp.arange(SLOTS) < count)[:, None, None, None]
    place = jnp.stack([count, core, lax.axis_index(ROW_AXES)])
    wide_hidden, cots, kept, sent, last_pair, mean, inv = prepare(
        place, peers, activations, cotangent, low, high, head, gain, bias
    )
    before = shift(last_pair, TM, 16, 1)
    terms = weight_terms(wide_hidden, kept, swap_cores(sent))
    terms, before = lax.optimization_barrier((terms, before))
    arrived = lax.all_to_all(terms, CHIP_AXES, 0, 0)

    cots, _ = lax.optimization_barrier((cots, terms))
    pre_grad, first_grad, second_grad = backward_conv(
        cots, conv_weight, act, mean, inv, gain, bias
    )
    sums = per_group(first_grad, second_grad)
    parts = [lax.ppermute(sums, "x", [(i, (i + k) % 4) for i in range(4)]) for k in range(1, 4)]

    extended = jnp.concatenate([before, wide_hidden], axis=0)
    block_out = forward_conv(count[None], extended, conv_weight, act)
    block_out, parts, arrived = lax.optimization_barrier((block_out, parts, arrived))
    block_out = block_out.reshape(activations.shape)

    sums = add_pairs(sums + parts[0] + parts[1] + parts[2], "yhi", [(0, 1)])
    first_avg = per_channel(sums[:SLOTS] / CELL_COUNT)[:, None, None, :]
    second_avg = per_channel(sums[SLOTS:] / CELL_COUNT)[:, None, None, :]
    wide_inv = inv[:, None, None, :]
    centred = (activations.astype(f32) - mean[:, None, None, :]) * wide_inv
    norm_part = wide_inv * (
        pre_grad.reshape(activations.shape) - first_avg - centred * second_avg
    )
    input_grad = jnp.where(live, cotangent.astype(f32) + norm_part, 0.0)

    frame_total = 1 + 4 * ((16 - 1) * 3 // 2)
    grad_scale = 1.0 / math.sqrt(frame_total * 8 * ROWS * COLS)
    total = jnp.sum(arrived.astype(f32), axis=0) * grad_scale
    shared = total[2 * PIECE :]
    parts = [
        jnp.concatenate(
            [total[k * PIECE : (k + 1) * PIECE], shared[:, k * 64 : (k + 1) * 64]], axis=1
        )
        for k in range(2)
    ]
    mine = jnp.where(core == 0, parts[0], parts[1])
    theirs = swap_cores(jnp.where(core == 0, parts[1], parts[0]))
    first = jnp.where(core == 0, mine, theirs)
    second = jnp.where(core == 0, theirs, mine)
    weight_grad = jnp.concatenate([first, second[:, LANES:], second[:, :LANES]], axis=1)
    return block_out, input_grad, weight_grad


def solution(mesh):
    fine = Mesh(mesh.devices.reshape(2, 4, 2, 2, 4), ALL_AXES)
    placed = P(TM, ROW_AXES, None, None)
    return jax.shard_map(
        on_device,
        mesh=fine,
        in_specs=(placed, P(), P(), P(), P(), placed),
        out_specs=(placed, placed, P(ALL_AXES, None)),
        check_vma=False,
    )
```

```python
import functools
import math

import jax
import jax.numpy as jnp
import numpy as np
from jax import lax
from jax.experimental import pallas as pl
from jax.experimental.pallas import tpu as pltpu
from jax.sharding import Mesh
from jax.sharding import PartitionSpec as P

GROUPS = 32
EPS = 1e-05
CHAN = 384
HALF = CHAN // 2
SLOTS = 8
ROWS = 4
COLS = 32
CELLS = ROWS * COLS
POS = SLOTS * CELLS
WIDE = 3 * CHAN
PIECE = 81
CHIPS = 64
LANES = 128
WIDE_CELLS = (ROWS + 2) * COLS
CELL_COUNT = 8 * CELLS * (CHAN // GROUPS)
TILE = 256

TM = ("ylo", "z", "core")
ROW_AXES = ("yhi", "x")
CHIP_AXES = ("ylo", "z", "yhi", "x")
ALL_AXES = TM + ROW_AXES

bf16 = jnp.bfloat16
f32 = jnp.float32
VMEM_LIMIT = pltpu.CompilerParams(vmem_limit_bytes=60 * 1024 * 1024)


def from_left(values):
    col = lax.broadcasted_iota(jnp.int32, values.shape, 0) % COLS
    return jnp.where(col == 0, 0.0, pltpu.roll(values, 1, 0))


def from_right(values):
    col = lax.broadcasted_iota(jnp.int32, values.shape, 0) % COLS
    return jnp.where(col == COLS - 1, 0.0, pltpu.roll(values, values.shape[0] - 1, 0))


def tap_products(x_ref, w_ref, acc, back):
    step = pl.program_id(0)
    weights = w_ref[...]
    pieces = []
    for b in range(3):
        at = (2 - step, 2 - b) if back else (step, b)
        pieces.append(x_ref[pl.ds(at[0], SLOTS), pl.ds(at[1], ROWS)].reshape(POS, CHAN))
    left = jnp.concatenate(pieces, axis=1)
    if back:
        right = jnp.concatenate([weights[b * WIDE : (b + 1) * WIDE] for b in range(3)], axis=1)
        dims = (((1,), (1,)), ((), ()))
    else:
        right = jnp.concatenate(
            [
                jnp.concatenate(
                    [weights[(b * 3 + c) * CHAN : (b * 3 + c + 1) * CHAN] for c in range(3)], axis=1
                )
                for b in range(3)
            ],
            axis=0,
        )
        dims = (((1,), (0,)), ((), ()))
    product = lax.dot_general(left, right, dims, preferred_element_type=f32)

    @pl.when(step == 0)
    def _():
        acc[...] = product

    @pl.when(step > 0)
    def _():
        acc[...] += product


def forward_kernel(count_ref, x_ref, w_ref, act_ref, out_ref, acc):
    tap_products(x_ref, w_ref, acc, False)

    @pl.when(pl.program_id(0) == 2)
    def _():
        for frame in range(SLOTS):
            rows = slice(frame * CELLS, (frame + 1) * CELLS)
            conv = (
                acc[rows, CHAN : 2 * CHAN]
                + from_left(acc[rows, :CHAN])
                + from_right(acc[rows, 2 * CHAN :])
            )
            total = act_ref[rows].astype(f32) + conv
            out_ref[rows] = jnp.where(frame < count_ref[0], total, 0.0).astype(bf16)


def backward_kernel(
    x_ref, w_ref, act_ref, mean_ref, inv_ref, gain_ref, bias_ref, out_ref, first_ref, second_ref, acc
):
    tap_products(x_ref, w_ref, acc, True)

    @pl.when(pl.program_id(0) == 2)
    def _():
        gain = gain_ref[...]
        bias = bias_ref[...]
        for frame in range(SLOTS):
            rows = slice(frame * CELLS, (frame + 1) * CELLS)
            grad = (
                acc[rows, CHAN : 2 * CHAN]
                + from_right(acc[rows, :CHAN])
                + from_left(acc[rows, 2 * CHAN :])
            )
            centred = (act_ref[rows].astype(f32) - mean_ref[frame : frame + 1]) * inv_ref[
                frame : frame + 1
            ]
            pre_act = centred * gain + bias
            gate = jax.nn.sigmoid(pre_act)
            pre_grad = grad * gate * (1.0 + pre_act * (1.0 - gate)) * gain
            out_ref[rows] = pre_grad
            first_ref[frame : frame + 1] = jnp.sum(pre_grad, axis=0, keepdims=True)
            second_ref[frame : frame + 1] = jnp.sum(pre_grad * centred, axis=0, keepdims=True)


READY = ((0, 2), (2, 5), (5, 8))


def weight_kernel(
    hidden_ref, other_ref, kept_ref, got_ref, out_ref, turned, sums, packed, sems
):
    def turn(f, carry):
        own = hidden_ref[f, 1 : 1 + ROWS].reshape(CELLS, CHAN)
        for half, values in enumerate((own, other_ref[f])):
            values = values.astype(f32)
            cols = pl.ds(pl.multiple_of(half * POS + f * CELLS, CELLS), CELLS)
            for c, moved in enumerate((from_left(values), values, from_right(values))):
                turned[c * CHAN : (c + 1) * CHAN, cols] = moved.T.astype(bf16)
        return carry

    lax.fori_loop(0, SLOTS, turn, 0)

    upper = lax.broadcasted_iota(jnp.int32, (PIECE, LANES), 1) >= LANES // 2
    copies = []
    for a in range(3):
        right = jnp.concatenate(
            [
                jnp.concatenate(
                    [
                        ref[2 - a + f, start : start + CELLS]
                        for ref in (kept_ref, got_ref)
                        for f in range(SLOTS)
                        for start in [g * WIDE_CELLS + (2 - b) * COLS]
                    ],
                    axis=0,
                )
                for b in range(3)
                for g in range(2)
            ],
            axis=1,
        )
        product = jnp.dot(turned[...], right, preferred_element_type=f32)
        for b in range(3):
            at = (a * 3 + b) * WIDE
            sums[at : at + WIDE] = product[:, b * TILE : (b + 1) * TILE]
        for chip in range(8 * READY[a][0], 8 * READY[a][1]):
            start = 1296 * (chip // 8) + PIECE * (chip % 8)
            first, second = sums[start : start + PIECE], sums[start + 648 : start + 648 + PIECE]
            block = jnp.concatenate(
                [
                    first[:, :LANES],
                    second[:, :LANES],
                    jnp.where(upper, second[:, LANES:], first[:, LANES:]),
                ],
                axis=0,
            )
            packed[chip] = block.astype(bf16)
        chips = pl.ds(8 * READY[a][0], 8 * (READY[a][1] - READY[a][0]))
        copies.append(pltpu.make_async_copy(packed.at[chips], out_ref.at[chips], sems.at[a]))
        copies[-1].start()
    for copy in copies:
        copy.wait()


def sums_kernel(act_ref, out_ref):
    firsts, seconds = [], []
    for frame in range(SLOTS):
        values = act_ref[frame].reshape(CELLS, CHAN).astype(f32)
        firsts.append(jnp.sum(values, axis=0, keepdims=True))
        seconds.append(jnp.sum(values * values, axis=0, keepdims=True))
    both = jnp.concatenate(firsts + seconds, axis=0)
    for peer in range(8):
        out_ref[peer] = both


def group_means(sums, same_ref):
    return jnp.dot(
        sums, same_ref[...], precision=lax.Precision.HIGHEST, preferred_element_type=f32
    ) * (1.0 / CELL_COUNT)


def hidden_kernel(
    place_ref,
    peers_ref,
    same_ref,
    act_ref,
    low_ref,
    high_ref,
    gain_ref,
    bias_ref,
    hidden_ref,
    sent_ref,
    pair_ref,
    mean_ref,
    inv_ref,
):
    step = pl.program_id(0)
    count, row_place = place_ref[0], place_ref[2]

    @pl.when(step == 0)
    def _():
        total = peers_ref[0]
        for peer in range(1, 8):
            total = total + peers_ref[peer]
        stats = group_means(total, same_ref)
        mean_ref[...] = stats[:SLOTS]
        inv_ref[...] = lax.rsqrt(stats[SLOTS:] - stats[:SLOTS] * stats[:SLOTS] + EPS)
        pair_ref[0] = jnp.zeros((ROWS + 2, COLS, CHAN), bf16)

    gain = gain_ref[...]
    bias = bias_ref[...]
    for k in range(2):
        frame = step * 2 + k
        live = frame < count
        mean = mean_ref[pl.ds(frame, 1)]
        inv = inv_ref[pl.ds(frame, 1)]

        def activated(values, keep, mean=mean, inv=inv):
            pre_act = (values.astype(f32) - mean) * inv * gain + bias
            return jnp.where(keep, pre_act * jax.nn.sigmoid(pre_act), 0.0).astype(bf16)

        hidden = activated(act_ref[k].reshape(CELLS, CHAN), live)
        hidden_ref[k, 1 : 1 + ROWS] = hidden.reshape(ROWS, COLS, CHAN)
        sent_ref[k] = hidden
        hidden_ref[k, 0] = activated(low_ref[k, 0], live & (row_place > 0))
        hidden_ref[k, 1 + ROWS] = activated(high_ref[k, 0], live & (row_place < 7))
        for late in range(2):

            @pl.when(frame == count - 2 + late)
            def _(k=k, late=late):
                pair_ref[late] = hidden_ref[k]


def cots_kernel(
    place_ref, cot_ref, low_ref, high_ref, head_ref, cots_ref, kept_ref, sent_ref
):
    step = pl.program_id(0)
    count, core = place_ref[0], place_ref[1]
    left = lax.broadcasted_iota(jnp.int32, (WIDE_CELLS, LANES), 1) < LANES // 2
    for k in range(2):
        frame = step * 2 + k

        @pl.when(frame < count)
        def _(k=k):
            cots_ref[k, 0] = low_ref[k, 0]
            cots_ref[k, 1 : 1 + ROWS] = cot_ref[k]
            cots_ref[k, 1 + ROWS] = high_ref[k, 0]

        @pl.when(frame >= count)
        def _(k=k):
            cots_ref[k] = jnp.zeros((ROWS + 2, COLS, CHAN), bf16)

        for late in range(2):

            @pl.when(frame == count + late)
            def _(k=k, late=late):
                cots_ref[k] = head_ref[late]

        values = cots_ref[k].reshape(WIDE_CELLS, CHAN)
        outer = values[:, :LANES], values[:, 2 * LANES :]
        middle = values[:, LANES : 2 * LANES].astype(f32)
        turned = pltpu.roll(middle, LANES // 2, 1)
        inner = (
            jnp.where(left, middle, turned).astype(bf16),
            jnp.where(left, turned, middle).astype(bf16),
        )
        for place in range(2):

            @pl.when(core == place)
            def _(k=k, place=place, outer=outer, inner=inner):
                for ref, half in ((kept_ref, place), (sent_ref, 1 - place)):
                    ref[k, :WIDE_CELLS] = outer[half]
                    ref[k, WIDE_CELLS:] = inner[half]


def finish_kernel(
    count_ref, sums_ref, other_ref, same_ref, pre_ref, act_ref, cot_ref, mean_ref, inv_ref, out_ref, avg
):
    step = pl.program_id(0)

    @pl.when(step == 0)
    def _():
        avg[...] = group_means(sums_ref[...] + other_ref[...], same_ref)

    for k in range(2):
        frame = step * 2 + k
        inv = inv_ref[pl.ds(frame, 1)]
        centred = (act_ref[k].astype(f32) - mean_ref[pl.ds(frame, 1)]) * inv
        spread = pre_ref[k] - avg[pl.ds(frame, 1)] - centred * avg[pl.ds(frame + SLOTS, 1)]
        total = cot_ref[k].astype(f32) + inv * spread
        out_ref[k] = jnp.where(frame < count_ref[0], total, 0.0)


def whole(shape):
    return pl.BlockSpec(shape, lambda step: (0,) * len(shape))


def cost(flops, moved):
    return pl.CostEstimate(flops=flops, bytes_accessed=moved, transcendentals=0)


FLOPS = 2 * POS * 27 * CHAN * CHAN
TAPS_SPEC = pl.BlockSpec((3 * WIDE, CHAN), lambda step: (step, 0))


def forward_conv(count, extended, weights, act):
    return pl.pallas_call(
        forward_kernel,
        out_shape=jax.ShapeDtypeStruct((POS, CHAN), bf16),
        grid=(3,),
        in_specs=[
            pl.BlockSpec(memory_space=pltpu.SMEM),
            whole(extended.shape),
            TAPS_SPEC,
            whole(act.shape),
        ],
        out_specs=whole((POS, CHAN)),
        scratch_shapes=[pltpu.VMEM((POS, WIDE), f32)],
        compiler_params=VMEM_LIMIT,
        cost_estimate=cost(FLOPS, 12 << 20),
        name="forward_conv",
    )(count, extended, weights, act)


def backward_conv(extended, weights, act, mean, inv, gain, bias):
    return pl.pallas_call(
        backward_kernel,
        out_shape=(
            jax.ShapeDtypeStruct((POS, CHAN), f32),
            jax.ShapeDtypeStruct((SLOTS, CHAN), f32),
            jax.ShapeDtypeStruct((SLOTS, CHAN), f32),
        ),
        grid=(3,),
        in_specs=[
            whole(extended.shape),
            TAPS_SPEC,
            whole(act.shape),
            whole(mean.shape),
            whole(inv.shape),
            whole(gain.shape),
            whole(bias.shape),
        ],
        out_specs=(whole((POS, CHAN)), whole((SLOTS, CHAN)), whole((SLOTS, CHAN))),
        scratch_shapes=[pltpu.VMEM((POS, WIDE), f32)],
        compiler_params=VMEM_LIMIT,
        cost_estimate=cost(FLOPS, 12 << 20),
        name="backward_conv",
    )(extended, weights, act, mean, inv, gain, bias)


def local_sums(act):
    return pl.pallas_call(
        sums_kernel,
        out_shape=jax.ShapeDtypeStruct((8, 2 * SLOTS, CHAN), f32),
        compiler_params=VMEM_LIMIT,
        cost_estimate=cost(4 * POS * CHAN, 1 << 20),
        name="local_sums",
    )(act)


SMEM_SPEC = pl.BlockSpec(memory_space=pltpu.SMEM)


def same_group():
    group = np.arange(CHAN) // (CHAN // GROUPS)
    return jnp.asarray((group[:, None] == group[None, :]).astype(np.float32))


def frames_spec(*rest, first=0, last=SLOTS // 2 - 1):
    return pl.BlockSpec(
        (2,) + rest,
        lambda step: (first // 2 + jnp.minimum(step, last),) + (0,) * len(rest),
    )


def make_hidden(place, peers, act, low, high, gain, bias):
    wide = (ROWS + 2, COLS, CHAN)
    return pl.pallas_call(
        hidden_kernel,
        out_shape=(
            jax.ShapeDtypeStruct((SLOTS,) + wide, bf16),
            jax.ShapeDtypeStruct((SLOTS, CELLS, CHAN), bf16),
            jax.ShapeDtypeStruct((2,) + wide, bf16),
            jax.ShapeDtypeStruct((SLOTS, CHAN), f32),
            jax.ShapeDtypeStruct((SLOTS, CHAN), f32),
        ),
        grid=(SLOTS // 2,),
        in_specs=[
            SMEM_SPEC,
            whole(peers.shape),
            whole((CHAN, CHAN)),
            frames_spec(ROWS, COLS, CHAN),
            frames_spec(1, COLS, CHAN),
            frames_spec(1, COLS, CHAN),
            whole((1, CHAN)),
            whole((1, CHAN)),
        ],
        out_specs=(
            frames_spec(*wide),
            frames_spec(CELLS, CHAN),
            whole((2,) + wide),
            whole((SLOTS, CHAN)),
            whole((SLOTS, CHAN)),
        ),
        compiler_params=VMEM_LIMIT,
        cost_estimate=cost(40 * POS * CHAN, 5 << 20),
        name="make_hidden",
    )(place, peers, same_group(), act, low, high, gain, bias)


def make_cots(place, cot, low, high, head):
    wide = (ROWS + 2, COLS, CHAN)
    half = (2 * WIDE_CELLS, LANES)
    return pl.pallas_call(
        cots_kernel,
        out_shape=(
            jax.ShapeDtypeStruct((SLOTS + 2,) + wide, bf16),
            jax.ShapeDtypeStruct((SLOTS + 2,) + half, bf16),
            jax.ShapeDtypeStruct((SLOTS + 2,) + half, bf16),
        ),
        grid=(SLOTS // 2 + 1,),
        in_specs=[
            SMEM_SPEC,
            frames_spec(ROWS, COLS, CHAN),
            frames_spec(1, COLS, CHAN, first=SLOTS),
            frames_spec(1, COLS, CHAN, first=SLOTS),
            whole((2,) + wide),
        ],
        out_specs=tuple(frames_spec(*shape, last=SLOTS // 2) for shape in (wide, half, half)),
        compiler_params=VMEM_LIMIT,
        cost_estimate=cost(10 * POS * CHAN, 6 << 20),
        name="make_cots",
    )(place, cot, low, high, head)


def finish(place, sums, other, pre_grad, act, cot, mean, inv):
    cells = frames_spec(CELLS, CHAN)
    small = whole((2 * SLOTS, CHAN))
    return pl.pallas_call(
        finish_kernel,
        out_shape=jax.ShapeDtypeStruct((SLOTS, CELLS, CHAN), f32),
        grid=(SLOTS // 2,),
        in_specs=[SMEM_SPEC, small, small, whole((CHAN, CHAN)), cells, cells, cells]
        + [whole((SLOTS, CHAN))] * 2,
        out_specs=cells,
        scratch_shapes=[pltpu.VMEM((2 * SLOTS, CHAN), f32)],
        compiler_params=VMEM_LIMIT,
        cost_estimate=cost(12 * POS * CHAN, 5 << 20),
        name="finish",
    )(place, sums, other, same_group(), pre_grad, act, cot, mean, inv)


def weight_terms(hidden, other, kept, got):
    return pl.pallas_call(
        weight_kernel,
        out_shape=jax.ShapeDtypeStruct((CHIPS, 3 * PIECE, LANES), bf16),
        in_specs=[pl.BlockSpec(memory_space=pltpu.VMEM)] * 4,
        out_specs=pl.BlockSpec(memory_space=pl.ANY),
        scratch_shapes=[
            pltpu.VMEM((WIDE, 2 * POS), bf16),
            pltpu.VMEM((9 * WIDE, TILE), f32),
            pltpu.VMEM((CHIPS, 3 * PIECE, LANES), bf16),
            pltpu.SemaphoreType.DMA((3,)),
        ],
        compiler_params=VMEM_LIMIT,
        cost_estimate=cost(FLOPS, 12 << 20),
        name="weight_terms",
    )(hidden, other, kept, got)


def shift(values, axes, count, step):
    pairs = [(i, i + step) for i in range(count) if 0 <= i + step < count]
    return lax.ppermute(values, axes, pairs)


def swap_cores(values):
    return lax.ppermute(values, "core", [(0, 1), (1, 0)])


def edge_rows(block):
    low = shift(block[:, ROWS - 1 :], ROW_AXES, 8, 1)
    high = shift(block[:, :1], ROW_AXES, 8, -1)
    return low, high


def on_device(activations, frame_counts, norm_gain, norm_bias, conv_weight, cotangent):
    core = lax.axis_index("core")
    act = activations.reshape(POS, CHAN)
    gain, bias = norm_gain[None], norm_bias[None]

    sums = local_sums(activations)
    peers = lax.all_to_all(sums, ROW_AXES, 0, 0)
    source, rows_at_once, _ = lax.optimization_barrier((activations, cotangent, sums))
    low, high = edge_rows(jnp.concatenate([source, rows_at_once], 0))
    low, high, peers = lax.optimization_barrier((low, high, peers))
    head = jnp.concatenate(
        [low[SLOTS : SLOTS + 2], cotangent[:2], high[SLOTS : SLOTS + 2]], axis=1
    )
    head = shift(head, TM, 16, -1)

    count = frame_counts[lax.axis_index(TM)]
    place = jnp.stack([count, core, lax.axis_index(ROW_AXES)])
    wide_hidden, hidden, last_pair, mean, inv = make_hidden(
        place, peers, activations, low, high, gain, bias
    )
    other_hidden = swap_cores(hidden)
    head, other_hidden = lax.optimization_barrier((head, other_hidden))
    before = shift(last_pair, TM, 16, 1)
    cots, kept, sent = make_cots(place, cotangent, low, high, head)
    terms = weight_terms(wide_hidden, other_hidden, kept, swap_cores(sent))
    terms, before = lax.optimization_barrier((terms, before))
    arrived = lax.all_to_all(terms, CHIP_AXES, 0, 0)

    cots, _ = lax.optimization_barrier((cots, terms))
    pre_grad, first_grad, second_grad = backward_conv(
        cots, conv_weight, act, mean, inv, gain, bias
    )
    sums = jnp.concatenate([first_grad, second_grad], axis=0)
    parts = [lax.ppermute(sums, "x", [(i, (i + k) % 4) for i in range(4)]) for k in range(1, 4)]

    extended = jnp.concatenate([before, wide_hidden], axis=0)
    block_out = forward_conv(count[None], extended, conv_weight, act)
    block_out, parts, arrived = lax.optimization_barrier((block_out, parts, arrived))
    block_out = block_out.reshape(activations.shape)

    sums = sums + parts[0] + parts[1] + parts[2]
    other = lax.ppermute(sums, "yhi", [(0, 1), (1, 0)])
    blocks = [v.reshape(SLOTS, CELLS, CHAN) for v in (pre_grad, act, cotangent)]
    input_grad = finish(place, sums, other, *blocks, mean, inv).reshape(activations.shape)

    frame_total = 1 + 4 * ((16 - 1) * 3 // 2)
    grad_scale = 1.0 / math.sqrt(frame_total * 8 * ROWS * COLS)
    total = jnp.sum(arrived.astype(f32), axis=0) * grad_scale
    shared = total[2 * PIECE :]
    parts = [
        jnp.concatenate(
            [total[k * PIECE : (k + 1) * PIECE], shared[:, k * 64 : (k + 1) * 64]], axis=1
        )
        for k in range(2)
    ]
    mine = jnp.where(core == 0, parts[0], parts[1])
    theirs = swap_cores(jnp.where(core == 0, parts[1], parts[0]))
    first = jnp.where(core == 0, mine, theirs)
    second = jnp.where(core == 0, theirs, mine)
    weight_grad = jnp.concatenate([first, second[:, LANES:], second[:, :LANES]], axis=1)
    return block_out, input_grad, weight_grad


def solution(mesh):
    fine = Mesh(mesh.devices.reshape(2, 4, 2, 2, 4), ALL_AXES)
    placed = P(TM, ROW_AXES, None, None)
    return jax.shard_map(
        on_device,
        mesh=fine,
        in_specs=(placed, P(), P(), P(), P(), placed),
        out_specs=(placed, placed, P(ALL_AXES, None)),
        check_vma=False,
    )
```

```python
import functools
import math

import jax
import jax.numpy as jnp
import numpy as np
from jax import lax
from jax.experimental import pallas as pl
from jax.experimental.pallas import tpu as pltpu
from jax.sharding import Mesh
from jax.sharding import PartitionSpec as P

GROUPS = 32
EPS = 1e-05
CHAN = 384
HALF = CHAN // 2
SLOTS = 8
ROWS = 4
COLS = 32
CELLS = ROWS * COLS
POS = SLOTS * CELLS
WIDE = 3 * CHAN
PIECE = 81
CHIPS = 64
LANES = 128
WIDE_CELLS = (ROWS + 2) * COLS
CELL_COUNT = 8 * CELLS * (CHAN // GROUPS)
TILE = 256

TM = ("ylo", "z", "core")
ROW_AXES = ("yhi", "x")
CHIP_AXES = ("ylo", "z", "yhi", "x")
ALL_AXES = TM + ROW_AXES

bf16 = jnp.bfloat16
f32 = jnp.float32
VMEM_LIMIT = pltpu.CompilerParams(vmem_limit_bytes=60 * 1024 * 1024)


def from_left(values):
    col = lax.broadcasted_iota(jnp.int32, values.shape, 0) % COLS
    return jnp.where(col == 0, 0.0, pltpu.roll(values, 1, 0))


def from_right(values):
    col = lax.broadcasted_iota(jnp.int32, values.shape, 0) % COLS
    return jnp.where(col == COLS - 1, 0.0, pltpu.roll(values, values.shape[0] - 1, 0))


def tap_products(x_ref, w_ref, acc, back):
    step = pl.program_id(0)
    weights = w_ref[...]
    pieces = []
    for b in range(3):
        at = (2 - step, 2 - b) if back else (step, b)
        pieces.append(x_ref[pl.ds(at[0], SLOTS), pl.ds(at[1], ROWS)].reshape(POS, CHAN))
    left = jnp.concatenate(pieces, axis=1)
    if back:
        right = jnp.concatenate([weights[b * WIDE : (b + 1) * WIDE] for b in range(3)], axis=1)
        dims = (((1,), (1,)), ((), ()))
    else:
        right = jnp.concatenate(
            [
                jnp.concatenate(
                    [weights[(b * 3 + c) * CHAN : (b * 3 + c + 1) * CHAN] for c in range(3)], axis=1
                )
                for b in range(3)
            ],
            axis=0,
        )
        dims = (((1,), (0,)), ((), ()))
    product = lax.dot_general(left, right, dims, preferred_element_type=f32)

    @pl.when(step == 0)
    def _():
        acc[...] = product

    @pl.when(step > 0)
    def _():
        acc[...] += product


def forward_kernel(count_ref, x_ref, w_ref, act_ref, out_ref, acc):
    tap_products(x_ref, w_ref, acc, False)

    @pl.when(pl.program_id(0) == 2)
    def _():
        for frame in range(SLOTS):
            rows = slice(frame * CELLS, (frame + 1) * CELLS)
            conv = (
                acc[rows, CHAN : 2 * CHAN]
                + from_left(acc[rows, :CHAN])
                + from_right(acc[rows, 2 * CHAN :])
            )
            total = act_ref[rows].astype(f32) + conv
            out_ref[rows] = jnp.where(frame < count_ref[0], total, 0.0).astype(bf16)


def backward_kernel(
    x_ref, w_ref, act_ref, mean_ref, inv_ref, gain_ref, bias_ref, out_ref, first_ref, second_ref, acc
):
    tap_products(x_ref, w_ref, acc, True)

    @pl.when(pl.program_id(0) == 2)
    def _():
        gain = gain_ref[...]
        bias = bias_ref[...]
        for frame in range(SLOTS):
            rows = slice(frame * CELLS, (frame + 1) * CELLS)
            grad = (
                acc[rows, CHAN : 2 * CHAN]
                + from_right(acc[rows, :CHAN])
                + from_left(acc[rows, 2 * CHAN :])
            )
            centred = (act_ref[rows].astype(f32) - mean_ref[frame : frame + 1]) * inv_ref[
                frame : frame + 1
            ]
            pre_act = centred * gain + bias
            gate = jax.nn.sigmoid(pre_act)
            pre_grad = grad * gate * (1.0 + pre_act * (1.0 - gate)) * gain
            out_ref[rows] = pre_grad
            first_ref[frame : frame + 1] = jnp.sum(pre_grad, axis=0, keepdims=True)
            second_ref[frame : frame + 1] = jnp.sum(pre_grad * centred, axis=0, keepdims=True)


READY = ((0, 2), (2, 5), (5, 8))


def weight_kernel(
    place_ref,
    hidden_ref,
    other_ref,
    even_ref,
    odd_ref,
    cot_ref,
    other_cot_ref,
    out_ref,
    before_ref,
    other_before,
    turned,
    right,
    sums,
    packed,
    sems,
):
    core = place_ref[1]

    def last_two(ref, count, to_ref):
        @pl.when(count >= 2)
        def _():
            to_ref[...] = ref[pl.ds(jnp.maximum(count - 2, 0), 2)]

        @pl.when(count < 2)
        def _():
            to_ref[0] = jnp.zeros((ROWS + 2, COLS, CHAN), bf16)
            to_ref[1] = ref[0]

    @pl.when(core == 0)
    def _():
        before_ref[...] = even_ref[...]
        last_two(hidden_ref, place_ref[0], other_before)

    @pl.when(core == 1)
    def _():
        other_before[...] = odd_ref[...]
        last_two(other_ref, place_ref[3], before_ref)

    def turn(ref, f, column):
        for b in range(3):
            values = ref[f, b : b + ROWS].reshape(CELLS, CHAN).astype(f32)
            turned[b * CHAN : (b + 1) * CHAN, pl.ds(pl.multiple_of(column, CELLS), CELLS)] = (
                values.T.astype(bf16)
            )

    for block, (early, late) in enumerate(((before_ref, hidden_ref), (other_before, other_ref))):
        base = block * (SLOTS + 2) * CELLS
        for f in range(2):
            turn(early, f, base + f * CELLS)

        def turn_late(f, carry, late=late, base=base):
            turn(late, f, base + (f + 2) * CELLS)
            return carry

        lax.fori_loop(0, SLOTS, turn_late, 0)

    left_lanes = lax.broadcasted_iota(jnp.int32, (CELLS, LANES), 1) < LANES // 2

    def move(f, carry):
        for block, ref in enumerate((cot_ref, other_cot_ref)):
            values = ref[f].reshape(CELLS, CHAN).astype(f32)
            values = jnp.where(f < place_ref[3 * block], values, 0.0)
            middle = values[:, LANES : 2 * LANES]
            swapped = pltpu.roll(middle, LANES // 2, 1)
            first = core == 0
            outer = jnp.where(first, values[:, :LANES], values[:, 2 * LANES :])
            inner = jnp.where(left_lanes == first, middle, swapped)
            chosen = jnp.concatenate([outer, inner], axis=1)
            rows = pl.ds(pl.multiple_of(block * POS + f * CELLS, CELLS), CELLS)
            for c, moved in enumerate((from_right(chosen), chosen, from_left(chosen))):
                right[rows, c * TILE : (c + 1) * TILE] = moved.astype(bf16)
        return carry

    lax.fori_loop(0, SLOTS, move, 0)

    upper = lax.broadcasted_iota(jnp.int32, (PIECE, LANES), 1) >= LANES // 2
    copies = []
    for a in range(3):
        window = jnp.concatenate(
            [
                turned[:, start : start + POS]
                for block in range(2)
                for start in [(block * (SLOTS + 2) + a) * CELLS]
            ],
            axis=1,
        )
        product = jnp.dot(window, right[...], preferred_element_type=f32)
        for b in range(3):
            for c in range(3):
                at = ((a * 3 + b) * 3 + c) * CHAN
                sums[at : at + CHAN] = product[
                    b * CHAN : (b + 1) * CHAN, c * TILE : (c + 1) * TILE
                ]
        for chip in range(8 * READY[a][0], 8 * READY[a][1]):
            start = 1296 * (chip // 8) + PIECE * (chip % 8)
            first, second = sums[start : start + PIECE], sums[start + 648 : start + 648 + PIECE]
            block = jnp.concatenate(
                [
                    first[:, :LANES],
                    second[:, :LANES],
                    jnp.where(upper, second[:, LANES:], first[:, LANES:]),
                ],
                axis=0,
            )
            packed[chip] = block.astype(bf16)
        chips = pl.ds(8 * READY[a][0], 8 * (READY[a][1] - READY[a][0]))
        copies.append(pltpu.make_async_copy(packed.at[chips], out_ref.at[chips], sems.at[a]))
        copies[-1].start()
    for copy in copies:
        copy.wait()


def sums_kernel(act_ref, out_ref):
    firsts, seconds = [], []
    for frame in range(SLOTS):
        values = act_ref[frame].reshape(CELLS, CHAN).astype(f32)
        firsts.append(jnp.sum(values, axis=0, keepdims=True))
        seconds.append(jnp.sum(values * values, axis=0, keepdims=True))
    both = jnp.concatenate(firsts + seconds, axis=0)
    for peer in range(8):
        out_ref[peer] = both


def group_means(sums, same_ref):
    return jnp.dot(
        sums, same_ref[...], precision=lax.Precision.HIGHEST, preferred_element_type=f32
    ) * (1.0 / CELL_COUNT)


def hidden_kernel(
    place_ref,
    peers_ref,
    same_ref,
    act_ref,
    low_ref,
    high_ref,
    gain_ref,
    bias_ref,
    hidden_ref,
    pair_ref,
    mean_ref,
    inv_ref,
):
    step = pl.program_id(0)
    count, row_place = place_ref[0], place_ref[2]

    @pl.when(step == 0)
    def _():
        total = peers_ref[0]
        for peer in range(1, 8):
            total = total + peers_ref[peer]
        stats = group_means(total, same_ref)
        mean_ref[...] = stats[:SLOTS]
        inv_ref[...] = lax.rsqrt(stats[SLOTS:] - stats[:SLOTS] * stats[:SLOTS] + EPS)
        pair_ref[0] = jnp.zeros((ROWS + 2, COLS, CHAN), bf16)

    gain = gain_ref[...]
    bias = bias_ref[...]
    for k in range(2):
        frame = step * 2 + k
        live = frame < count
        mean = mean_ref[pl.ds(frame, 1)]
        inv = inv_ref[pl.ds(frame, 1)]

        def activated(values, keep, mean=mean, inv=inv):
            pre_act = (values.astype(f32) - mean) * inv * gain + bias
            return jnp.where(keep, pre_act * jax.nn.sigmoid(pre_act), 0.0).astype(bf16)

        hidden = activated(act_ref[k].reshape(CELLS, CHAN), live)
        hidden_ref[k, 1 : 1 + ROWS] = hidden.reshape(ROWS, COLS, CHAN)
        hidden_ref[k, 0] = activated(low_ref[k, 0], live & (row_place > 0))
        hidden_ref[k, 1 + ROWS] = activated(high_ref[k, 0], live & (row_place < 7))
        for late in range(2):

            @pl.when(frame == count - 2 + late)
            def _(k=k, late=late):
                pair_ref[late] = hidden_ref[k]


def cots_kernel(place_ref, cot_ref, low_ref, high_ref, head_ref, cots_ref):
    step = pl.program_id(0)
    count = place_ref[0]
    for k in range(2):
        frame = step * 2 + k

        @pl.when(frame < count)
        def _(k=k):
            cots_ref[k, 0] = low_ref[k, 0]
            cots_ref[k, 1 : 1 + ROWS] = cot_ref[k]
            cots_ref[k, 1 + ROWS] = high_ref[k, 0]

        @pl.when(frame >= count)
        def _(k=k):
            cots_ref[k] = jnp.zeros((ROWS + 2, COLS, CHAN), bf16)

        for late in range(2):

            @pl.when(frame == count + late)
            def _(k=k, late=late):
                cots_ref[k] = head_ref[late]


def whole(shape):
    return pl.BlockSpec(shape, lambda step: (0,) * len(shape))


def cost(flops, moved):
    return pl.CostEstimate(flops=flops, bytes_accessed=moved, transcendentals=0)


FLOPS = 2 * POS * 27 * CHAN * CHAN
TAPS_SPEC = pl.BlockSpec((3 * WIDE, CHAN), lambda step: (step, 0))


def forward_conv(count, extended, weights, act):
    return pl.pallas_call(
        forward_kernel,
        out_shape=jax.ShapeDtypeStruct((POS, CHAN), bf16),
        grid=(3,),
        in_specs=[
            pl.BlockSpec(memory_space=pltpu.SMEM),
            whole(extended.shape),
            TAPS_SPEC,
            whole(act.shape),
        ],
        out_specs=whole((POS, CHAN)),
        scratch_shapes=[pltpu.VMEM((POS, WIDE), f32)],
        compiler_params=VMEM_LIMIT,
        cost_estimate=cost(FLOPS, 12 << 20),
        name="forward_conv",
    )(count, extended, weights, act)


def backward_conv(extended, weights, act, mean, inv, gain, bias):
    return pl.pallas_call(
        backward_kernel,
        out_shape=(
            jax.ShapeDtypeStruct((POS, CHAN), f32),
            jax.ShapeDtypeStruct((SLOTS, CHAN), f32),
            jax.ShapeDtypeStruct((SLOTS, CHAN), f32),
        ),
        grid=(3,),
        in_specs=[
            whole(extended.shape),
            TAPS_SPEC,
            whole(act.shape),
            whole(mean.shape),
            whole(inv.shape),
            whole(gain.shape),
            whole(bias.shape),
        ],
        out_specs=(whole((POS, CHAN)), whole((SLOTS, CHAN)), whole((SLOTS, CHAN))),
        scratch_shapes=[pltpu.VMEM((POS, WIDE), f32)],
        compiler_params=VMEM_LIMIT,
        cost_estimate=cost(FLOPS, 12 << 20),
        name="backward_conv",
    )(extended, weights, act, mean, inv, gain, bias)


def local_sums(act):
    return pl.pallas_call(
        sums_kernel,
        out_shape=jax.ShapeDtypeStruct((8, 2 * SLOTS, CHAN), f32),
        compiler_params=VMEM_LIMIT,
        cost_estimate=cost(4 * POS * CHAN, 1 << 20),
        name="local_sums",
    )(act)


SMEM_SPEC = pl.BlockSpec(memory_space=pltpu.SMEM)


def same_group():
    group = np.arange(CHAN) // (CHAN // GROUPS)
    return jnp.asarray((group[:, None] == group[None, :]).astype(np.float32))


def frames_spec(*rest, first=0, last=SLOTS // 2 - 1):
    return pl.BlockSpec(
        (2,) + rest,
        lambda step: (first // 2 + jnp.minimum(step, last),) + (0,) * len(rest),
    )


def make_hidden(place, peers, act, low, high, gain, bias):
    wide = (ROWS + 2, COLS, CHAN)
    return pl.pallas_call(
        hidden_kernel,
        out_shape=(
            jax.ShapeDtypeStruct((SLOTS,) + wide, bf16),
            jax.ShapeDtypeStruct((2,) + wide, bf16),
            jax.ShapeDtypeStruct((SLOTS, CHAN), f32),
            jax.ShapeDtypeStruct((SLOTS, CHAN), f32),
        ),
        grid=(SLOTS // 2,),
        in_specs=[
            SMEM_SPEC,
            whole(peers.shape),
            whole((CHAN, CHAN)),
            frames_spec(ROWS, COLS, CHAN),
            frames_spec(1, COLS, CHAN),
            frames_spec(1, COLS, CHAN),
            whole((1, CHAN)),
            whole((1, CHAN)),
        ],
        out_specs=(
            frames_spec(*wide),
            whole((2,) + wide),
            whole((SLOTS, CHAN)),
            whole((SLOTS, CHAN)),
        ),
        compiler_params=VMEM_LIMIT,
        cost_estimate=cost(40 * POS * CHAN, 5 << 20),
        name="make_hidden",
    )(place, peers, same_group(), act, low, high, gain, bias)


def make_cots(place, cot, low, high, head):
    wide = (ROWS + 2, COLS, CHAN)
    return pl.pallas_call(
        cots_kernel,
        out_shape=jax.ShapeDtypeStruct((SLOTS + 2,) + wide, bf16),
        grid=(SLOTS // 2 + 1,),
        in_specs=[
            SMEM_SPEC,
            frames_spec(ROWS, COLS, CHAN),
            frames_spec(1, COLS, CHAN, first=SLOTS),
            frames_spec(1, COLS, CHAN, first=SLOTS),
            whole((2,) + wide),
        ],
        out_specs=frames_spec(*wide, last=SLOTS // 2),
        compiler_params=VMEM_LIMIT,
        cost_estimate=cost(10 * POS * CHAN, 4 << 20),
        name="make_cots",
    )(place, cot, low, high, head)


def weight_terms(place, hidden, other, even, odd, cot, other_cot):
    in_vmem = pl.BlockSpec(memory_space=pltpu.VMEM)
    pair = (2, ROWS + 2, COLS, CHAN)
    return pl.pallas_call(
        weight_kernel,
        out_shape=(
            jax.ShapeDtypeStruct((CHIPS, 3 * PIECE, LANES), bf16),
            jax.ShapeDtypeStruct(pair, bf16),
        ),
        in_specs=[SMEM_SPEC] + [in_vmem] * 6,
        out_specs=(pl.BlockSpec(memory_space=pl.ANY), in_vmem),
        scratch_shapes=[
            pltpu.VMEM(pair, bf16),
            pltpu.VMEM((WIDE, 2 * (SLOTS + 2) * CELLS), bf16),
            pltpu.VMEM((2 * POS, 3 * TILE), bf16),
            pltpu.VMEM((9 * WIDE, TILE), f32),
            pltpu.VMEM((CHIPS, 3 * PIECE, LANES), bf16),
            pltpu.SemaphoreType.DMA((3,)),
        ],
        compiler_params=VMEM_LIMIT,
        cost_estimate=cost(FLOPS, 12 << 20),
        name="weight_terms",
    )(place, hidden, other, even, odd, cot, other_cot)


def shift(values, axes, count, step):
    pairs = [(i, i + step) for i in range(count) if 0 <= i + step < count]
    return lax.ppermute(values, axes, pairs)


def swap_cores(values):
    return lax.ppermute(values, "core", [(0, 1), (1, 0)])


def edge_rows(block):
    low = shift(block[:, ROWS - 1 :], ROW_AXES, 8, 1)
    high = shift(block[:, :1], ROW_AXES, 8, -1)
    return low, high


def add_pairs(sums, axis, pairs):
    return sums + lax.ppermute(sums, axis, pairs + [(b, a) for a, b in pairs])


def per_group(first, second):
    grouped = jnp.concatenate([first, second], axis=0).reshape(2 * SLOTS, GROUPS, CHAN // GROUPS)
    return jnp.sum(grouped, axis=2)


def per_channel(grouped):
    return jnp.repeat(grouped, CHAN // GROUPS, axis=1)


def on_device(activations, frame_counts, norm_gain, norm_bias, conv_weight, cotangent):
    core = lax.axis_index("core")
    act = activations.reshape(POS, CHAN)
    gain, bias = norm_gain[None], norm_bias[None]

    sums = local_sums(activations)
    peers = lax.all_to_all(sums, ROW_AXES, 0, 0)
    source, rows_at_once, _ = lax.optimization_barrier((activations, cotangent, sums))
    low, high = edge_rows(jnp.concatenate([source, rows_at_once], 0))
    other_cot = swap_cores(rows_at_once)
    low, high, peers, other_cot = lax.optimization_barrier((low, high, peers, other_cot))

    tm = lax.axis_index(TM)
    count = frame_counts[tm]
    place = jnp.stack(
        [count, core, lax.axis_index(ROW_AXES), frame_counts[tm + 1 - 2 * core]]
    )
    wide_hidden, last_pair, mean, inv = make_hidden(
        place, peers, activations, low, high, gain, bias
    )
    other_hidden = swap_cores(wide_hidden)
    even = lax.ppermute(last_pair, TM, [(i, i + 1) for i in range(1, 15, 2)])
    odd = lax.ppermute(last_pair, TM, [(i, i + 2) for i in range(1, 15, 2)])

    low, high, _ = lax.optimization_barrier((low, high, last_pair))
    head = jnp.concatenate(
        [low[SLOTS : SLOTS + 2], cotangent[:2], high[SLOTS : SLOTS + 2]], axis=1
    )
    head = shift(head, TM, 16, -1)

    terms, before = weight_terms(
        place, wide_hidden, other_hidden, even, odd, cotangent, other_cot
    )
    terms, head = lax.optimization_barrier((terms, head))
    arrived = lax.all_to_all(terms, CHIP_AXES, 0, 0)

    low, high, _ = lax.optimization_barrier((low, high, terms))
    cots = make_cots(place, cotangent, low, high, head)
    pre_grad, first_grad, second_grad = backward_conv(
        cots, conv_weight, act, mean, inv, gain, bias
    )
    sums = per_group(first_grad, second_grad)
    parts = [lax.ppermute(sums, "x", [(i, (i + k) % 4) for i in range(4)]) for k in range(1, 4)]

    extended = jnp.concatenate([before, wide_hidden], axis=0)
    block_out = forward_conv(count[None], extended, conv_weight, act)
    block_out, parts, arrived = lax.optimization_barrier((block_out, parts, arrived))
    block_out = block_out.reshape(activations.shape)

    sums = add_pairs(sums + parts[0] + parts[1] + parts[2], "yhi", [(0, 1)])
    first_avg = per_channel(sums[:SLOTS] / CELL_COUNT)[:, None, None, :]
    second_avg = per_channel(sums[SLOTS:] / CELL_COUNT)[:, None, None, :]
    wide_inv = inv[:, None, None, :]
    centred = (activations.astype(f32) - mean[:, None, None, :]) * wide_inv
    norm_part = wide_inv * (
        pre_grad.reshape(activations.shape) - first_avg - centred * second_avg
    )
    live = (jnp.arange(SLOTS) < count)[:, None, None, None]
    input_grad = jnp.where(live, cotangent.astype(f32) + norm_part, 0.0)

    frame_total = 1 + 4 * ((16 - 1) * 3 // 2)
    grad_scale = 1.0 / math.sqrt(frame_total * 8 * ROWS * COLS)
    total = jnp.sum(arrived.astype(f32), axis=0) * grad_scale
    shared = total[2 * PIECE :]
    parts = [
        jnp.concatenate(
            [total[k * PIECE : (k + 1) * PIECE], shared[:, k * 64 : (k + 1) * 64]], axis=1
        )
        for k in range(2)
    ]
    mine = jnp.where(core == 0, parts[0], parts[1])
    theirs = swap_cores(jnp.where(core == 0, parts[1], parts[0]))
    first = jnp.where(core == 0, mine, theirs)
    second = jnp.where(core == 0, theirs, mine)
    weight_grad = jnp.concatenate([first, second[:, LANES:], second[:, :LANES]], axis=1)
    return block_out, input_grad, weight_grad


def solution(mesh):
    fine = Mesh(mesh.devices.reshape(2, 4, 2, 2, 4), ALL_AXES)
    placed = P(TM, ROW_AXES, None, None)
    return jax.shard_map(
        on_device,
        mesh=fine,
        in_specs=(placed, P(), P(), P(), P(), placed),
        out_specs=(placed, placed, P(ALL_AXES, None)),
        check_vma=False,
    )
```

```python
import functools
import math

import jax
import jax.numpy as jnp
import numpy as np
from jax import lax
from jax.experimental import pallas as pl
from jax.experimental.pallas import tpu as pltpu
from jax.sharding import Mesh
from jax.sharding import PartitionSpec as P

GROUPS = 32
EPS = 1e-05
CHAN = 384
HALF = CHAN // 2
SLOTS = 8
ROWS = 4
COLS = 32
CELLS = ROWS * COLS
POS = SLOTS * CELLS
WIDE = 3 * CHAN
PIECE = 81
CHIPS = 64
LANES = 128
WIDE_CELLS = (ROWS + 2) * COLS
CELL_COUNT = 8 * CELLS * (CHAN // GROUPS)
TILE = 256

TM = ("ylo", "z", "core")
ROW_AXES = ("yhi", "x")
CHIP_AXES = ("ylo", "z", "yhi", "x")
ALL_AXES = TM + ROW_AXES

bf16 = jnp.bfloat16
f32 = jnp.float32
VMEM_LIMIT = pltpu.CompilerParams(vmem_limit_bytes=64 * 1024 * 1024)


def from_left(values):
    col = lax.broadcasted_iota(jnp.int32, values.shape, 0) % COLS
    return jnp.where(col == 0, 0.0, pltpu.roll(values, 1, 0))


def from_right(values):
    col = lax.broadcasted_iota(jnp.int32, values.shape, 0) % COLS
    return jnp.where(col == COLS - 1, 0.0, pltpu.roll(values, values.shape[0] - 1, 0))


def tap_products(x_ref, w_ref, acc, back):
    step = pl.program_id(0)
    weights = w_ref[...]
    pieces = []
    for b in range(3):
        at = (2 - step, 2 - b) if back else (step, b)
        pieces.append(x_ref[pl.ds(at[0], SLOTS), pl.ds(at[1], ROWS)].reshape(POS, CHAN))
    left = jnp.concatenate(pieces, axis=1)
    if back:
        right = jnp.concatenate([weights[b * WIDE : (b + 1) * WIDE] for b in range(3)], axis=1)
        dims = (((1,), (1,)), ((), ()))
    else:
        right = jnp.concatenate(
            [
                jnp.concatenate(
                    [weights[(b * 3 + c) * CHAN : (b * 3 + c + 1) * CHAN] for c in range(3)], axis=1
                )
                for b in range(3)
            ],
            axis=0,
        )
        dims = (((1,), (0,)), ((), ()))
    product = lax.dot_general(left, right, dims, preferred_element_type=f32)

    @pl.when(step == 0)
    def _():
        acc[...] = product

    @pl.when(step > 0)
    def _():
        acc[...] += product


def forward_kernel(count_ref, x_ref, w_ref, act_ref, out_ref, acc):
    tap_products(x_ref, w_ref, acc, False)

    @pl.when(pl.program_id(0) == 2)
    def _():
        for frame in range(SLOTS):
            rows = slice(frame * CELLS, (frame + 1) * CELLS)
            conv = (
                acc[rows, CHAN : 2 * CHAN]
                + from_left(acc[rows, :CHAN])
                + from_right(acc[rows, 2 * CHAN :])
            )
            total = act_ref[rows].astype(f32) + conv
            out_ref[rows] = jnp.where(frame < count_ref[0], total, 0.0).astype(bf16)


def backward_kernel(
    x_ref, w_ref, act_ref, mean_ref, inv_ref, gain_ref, bias_ref, out_ref, first_ref, second_ref, acc
):
    tap_products(x_ref, w_ref, acc, True)

    @pl.when(pl.program_id(0) == 2)
    def _():
        gain = gain_ref[...]
        bias = bias_ref[...]
        for frame in range(SLOTS):
            rows = slice(frame * CELLS, (frame + 1) * CELLS)
            grad = (
                acc[rows, CHAN : 2 * CHAN]
                + from_right(acc[rows, :CHAN])
                + from_left(acc[rows, 2 * CHAN :])
            )
            centred = (act_ref[rows].astype(f32) - mean_ref[frame : frame + 1]) * inv_ref[
                frame : frame + 1
            ]
            pre_act = centred * gain + bias
            gate = jax.nn.sigmoid(pre_act)
            pre_grad = grad * gate * (1.0 + pre_act * (1.0 - gate)) * gain
            out_ref[rows] = pre_grad
            first_ref[frame : frame + 1] = jnp.sum(pre_grad, axis=0, keepdims=True)
            second_ref[frame : frame + 1] = jnp.sum(pre_grad * centred, axis=0, keepdims=True)


READY = ((0, 2), (2, 5), (5, 8))


def weight_kernel(
    place_ref,
    hidden_ref,
    other_ref,
    even_ref,
    odd_ref,
    cot_ref,
    other_cot_ref,
    out_ref,
    before_ref,
    other_before,
    turned,
    right,
    sums,
    packed,
    sems,
):
    core = place_ref[1]

    def last_two(ref, count, to_ref):
        @pl.when(count >= 2)
        def _():
            to_ref[...] = ref[pl.ds(jnp.maximum(count - 2, 0), 2)]

        @pl.when(count < 2)
        def _():
            to_ref[0] = jnp.zeros((ROWS + 2, COLS, CHAN), bf16)
            to_ref[1] = ref[0]

    @pl.when(core == 0)
    def _():
        before_ref[...] = even_ref[...]
        last_two(hidden_ref, place_ref[0], other_before)

    @pl.when(core == 1)
    def _():
        other_before[...] = odd_ref[...]
        last_two(other_ref, place_ref[3], before_ref)

    def turn(ref, f, column):
        for b in range(3):
            values = ref[f, b : b + ROWS].reshape(CELLS, CHAN)
            turned[b * CHAN : (b + 1) * CHAN, pl.ds(pl.multiple_of(column, CELLS), CELLS)] = values.T

    for block, (early, late) in enumerate(((before_ref, hidden_ref), (other_before, other_ref))):
        base = block * (SLOTS + 2) * CELLS
        for f in range(2):
            turn(early, f, base + f * CELLS)

        def turn_late(f, carry, late=late, base=base):
            turn(late, f, base + (f + 2) * CELLS)
            return carry

        lax.fori_loop(0, SLOTS, turn_late, 0, unroll=True)

    left_lanes = lax.broadcasted_iota(jnp.int32, (CELLS, LANES), 1) < LANES // 2

    def move(f, carry):
        for block, ref in enumerate((cot_ref, other_cot_ref)):
            values = ref[f].reshape(CELLS, CHAN).astype(f32)
            values = jnp.where(f < place_ref[3 * block], values, 0.0)
            middle = values[:, LANES : 2 * LANES]
            swapped = pltpu.roll(middle, LANES // 2, 1)
            first = core == 0
            outer = jnp.where(first, values[:, :LANES], values[:, 2 * LANES :])
            inner = jnp.where(left_lanes == first, middle, swapped)
            chosen = jnp.concatenate([outer, inner], axis=1)
            rows = pl.ds(pl.multiple_of(block * POS + f * CELLS, CELLS), CELLS)
            for c, moved in enumerate((from_right(chosen), chosen, from_left(chosen))):
                right[rows, c * TILE : (c + 1) * TILE] = moved.astype(bf16)
        return carry

    lax.fori_loop(0, SLOTS, move, 0, unroll=True)

    upper = lax.broadcasted_iota(jnp.int32, (PIECE, LANES), 1) >= LANES // 2
    copies = []
    for a in range(3):
        window = jnp.concatenate(
            [
                turned[:, start : start + POS]
                for block in range(2)
                for start in [(block * (SLOTS + 2) + a) * CELLS]
            ],
            axis=1,
        )
        product = jnp.dot(window, right[...], preferred_element_type=f32)
        for b in range(3):
            for c in range(3):
                at = ((a * 3 + b) * 3 + c) * CHAN
                sums[at : at + CHAN] = product[
                    b * CHAN : (b + 1) * CHAN, c * TILE : (c + 1) * TILE
                ]
        for chip in range(8 * READY[a][0], 8 * READY[a][1]):
            start = 1296 * (chip // 8) + PIECE * (chip % 8)
            first, second = sums[start : start + PIECE], sums[start + 648 : start + 648 + PIECE]
            block = jnp.concatenate(
                [
                    first[:, :LANES],
                    second[:, :LANES],
                    jnp.where(upper, second[:, LANES:], first[:, LANES:]),
                ],
                axis=0,
            )
            packed[chip] = block.astype(bf16)
        chips = pl.ds(8 * READY[a][0], 8 * (READY[a][1] - READY[a][0]))
        copies.append(pltpu.make_async_copy(packed.at[chips], out_ref.at[chips], sems.at[a]))
        copies[-1].start()
    for copy in copies:
        copy.wait()


def sums_kernel(act_ref, out_ref):
    firsts, seconds = [], []
    for frame in range(SLOTS):
        values = act_ref[frame].reshape(CELLS, CHAN).astype(f32)
        firsts.append(jnp.sum(values, axis=0, keepdims=True))
        seconds.append(jnp.sum(values * values, axis=0, keepdims=True))
    both = jnp.concatenate(firsts + seconds, axis=0)
    for peer in range(8):
        out_ref[peer] = both


def group_means(sums, same_ref):
    return jnp.dot(
        sums, same_ref[...], precision=lax.Precision.HIGHEST, preferred_element_type=f32
    ) * (1.0 / CELL_COUNT)


def hidden_kernel(
    place_ref,
    peers_ref,
    same_ref,
    act_ref,
    low_ref,
    high_ref,
    cot_ref,
    cot_low_ref,
    cot_high_ref,
    gain_ref,
    bias_ref,
    hidden_ref,
    pair_ref,
    head_ref,
    mean_ref,
    inv_ref,
):
    step = pl.program_id(0)
    count, row_place = place_ref[0], place_ref[2]

    @pl.when(step == 0)
    def _():
        total = peers_ref[0]
        for peer in range(1, 8):
            total = total + peers_ref[peer]
        stats = group_means(total, same_ref)
        mean_ref[...] = stats[:SLOTS]
        inv_ref[...] = lax.rsqrt(stats[SLOTS:] - stats[:SLOTS] * stats[:SLOTS] + EPS)
        pair_ref[0] = jnp.zeros((ROWS + 2, COLS, CHAN), bf16)
        head_ref[:, :1] = cot_low_ref[...]
        head_ref[:, 1 : 1 + ROWS] = cot_ref[...]
        head_ref[:, 1 + ROWS :] = cot_high_ref[...]

    gain = gain_ref[...]
    bias = bias_ref[...]
    for k in range(2):
        frame = step * 2 + k
        live = frame < count
        mean = mean_ref[pl.ds(frame, 1)]
        inv = inv_ref[pl.ds(frame, 1)]

        def activated(values, keep, mean=mean, inv=inv):
            pre_act = (values.astype(f32) - mean) * inv * gain + bias
            return jnp.where(keep, pre_act * jax.nn.sigmoid(pre_act), 0.0).astype(bf16)

        hidden = activated(act_ref[k].reshape(CELLS, CHAN), live)
        hidden_ref[k, 1 : 1 + ROWS] = hidden.reshape(ROWS, COLS, CHAN)
        hidden_ref[k, 0] = activated(low_ref[k, 0], live & (row_place > 0))
        hidden_ref[k, 1 + ROWS] = activated(high_ref[k, 0], live & (row_place < 7))
        for late in range(2):

            @pl.when(frame == count - 2 + late)
            def _(k=k, late=late):
                pair_ref[late] = hidden_ref[k]


def cots_kernel(place_ref, cot_ref, low_ref, high_ref, head_ref, cots_ref):
    step = pl.program_id(0)
    count = place_ref[0]
    for k in range(2):
        frame = step * 2 + k

        @pl.when(frame < count)
        def _(k=k):
            cots_ref[k, 0] = low_ref[k, 0]
            cots_ref[k, 1 : 1 + ROWS] = cot_ref[k]
            cots_ref[k, 1 + ROWS] = high_ref[k, 0]

        @pl.when(frame >= count)
        def _(k=k):
            cots_ref[k] = jnp.zeros((ROWS + 2, COLS, CHAN), bf16)

        for late in range(2):

            @pl.when(frame == count + late)
            def _(k=k, late=late):
                cots_ref[k] = head_ref[late]


def whole(shape):
    return pl.BlockSpec(shape, lambda step: (0,) * len(shape))


def cost(flops, moved):
    return pl.CostEstimate(flops=flops, bytes_accessed=moved, transcendentals=0)


FLOPS = 2 * POS * 27 * CHAN * CHAN
TAPS_SPEC = pl.BlockSpec((3 * WIDE, CHAN), lambda step: (step, 0))


def forward_conv(count, extended, weights, act):
    return pl.pallas_call(
        forward_kernel,
        out_shape=jax.ShapeDtypeStruct((POS, CHAN), bf16),
        grid=(3,),
        in_specs=[
            pl.BlockSpec(memory_space=pltpu.SMEM),
            whole(extended.shape),
            TAPS_SPEC,
            whole(act.shape),
        ],
        out_specs=whole((POS, CHAN)),
        scratch_shapes=[pltpu.VMEM((POS, WIDE), f32)],
        compiler_params=VMEM_LIMIT,
        cost_estimate=cost(FLOPS, 12 << 20),
        name="forward_conv",
    )(count, extended, weights, act)


def backward_conv(extended, weights, act, mean, inv, gain, bias):
    return pl.pallas_call(
        backward_kernel,
        out_shape=(
            jax.ShapeDtypeStruct((POS, CHAN), f32),
            jax.ShapeDtypeStruct((SLOTS, CHAN), f32),
            jax.ShapeDtypeStruct((SLOTS, CHAN), f32),
        ),
        grid=(3,),
        in_specs=[
            whole(extended.shape),
            TAPS_SPEC,
            whole(act.shape),
            whole(mean.shape),
            whole(inv.shape),
            whole(gain.shape),
            whole(bias.shape),
        ],
        out_specs=(whole((POS, CHAN)), whole((SLOTS, CHAN)), whole((SLOTS, CHAN))),
        scratch_shapes=[pltpu.VMEM((POS, WIDE), f32)],
        compiler_params=VMEM_LIMIT,
        cost_estimate=cost(FLOPS, 12 << 20),
        name="backward_conv",
    )(extended, weights, act, mean, inv, gain, bias)


def local_sums(act):
    return pl.pallas_call(
        sums_kernel,
        out_shape=jax.ShapeDtypeStruct((8, 2 * SLOTS, CHAN), f32),
        compiler_params=VMEM_LIMIT,
        cost_estimate=cost(4 * POS * CHAN, 1 << 20),
        name="local_sums",
    )(act)


SMEM_SPEC = pl.BlockSpec(memory_space=pltpu.SMEM)


def same_group():
    group = np.arange(CHAN) // (CHAN // GROUPS)
    return jnp.asarray((group[:, None] == group[None, :]).astype(np.float32))


def frames_spec(*rest, first=0, last=SLOTS // 2 - 1):
    return pl.BlockSpec(
        (2,) + rest,
        lambda step: (first // 2 + jnp.minimum(step, last),) + (0,) * len(rest),
    )


def make_hidden(place, peers, act, cot, low, high, gain, bias):
    wide = (ROWS + 2, COLS, CHAN)
    return pl.pallas_call(
        hidden_kernel,
        out_shape=(
            jax.ShapeDtypeStruct((SLOTS,) + wide, bf16),
            jax.ShapeDtypeStruct((2,) + wide, bf16),
            jax.ShapeDtypeStruct((2,) + wide, bf16),
            jax.ShapeDtypeStruct((SLOTS, CHAN), f32),
            jax.ShapeDtypeStruct((SLOTS, CHAN), f32),
        ),
        grid=(SLOTS // 2,),
        in_specs=[
            SMEM_SPEC,
            whole(peers.shape),
            whole((CHAN, CHAN)),
            frames_spec(ROWS, COLS, CHAN),
            frames_spec(1, COLS, CHAN),
            frames_spec(1, COLS, CHAN),
            frames_spec(ROWS, COLS, CHAN, last=0),
            frames_spec(1, COLS, CHAN, first=SLOTS, last=0),
            frames_spec(1, COLS, CHAN, first=SLOTS, last=0),
            whole((1, CHAN)),
            whole((1, CHAN)),
        ],
        out_specs=(
            frames_spec(*wide),
            whole((2,) + wide),
            whole((2,) + wide),
            whole((SLOTS, CHAN)),
            whole((SLOTS, CHAN)),
        ),
        compiler_params=VMEM_LIMIT,
        cost_estimate=cost(40 * POS * CHAN, 5 << 20),
        name="make_hidden",
    )(place, peers, same_group(), act, low, high, cot, low, high, gain, bias)


def make_cots(place, cot, low, high, head):
    wide = (ROWS + 2, COLS, CHAN)
    return pl.pallas_call(
        cots_kernel,
        out_shape=jax.ShapeDtypeStruct((SLOTS + 2,) + wide, bf16),
        grid=(SLOTS // 2 + 1,),
        in_specs=[
            SMEM_SPEC,
            frames_spec(ROWS, COLS, CHAN),
            frames_spec(1, COLS, CHAN, first=SLOTS),
            frames_spec(1, COLS, CHAN, first=SLOTS),
            whole((2,) + wide),
        ],
        out_specs=frames_spec(*wide, last=SLOTS // 2),
        compiler_params=VMEM_LIMIT,
        cost_estimate=cost(10 * POS * CHAN, 4 << 20),
        name="make_cots",
    )(place, cot, low, high, head)


def weight_terms(place, hidden, other, even, odd, cot, other_cot):
    in_vmem = pl.BlockSpec(memory_space=pltpu.VMEM)
    pair = (2, ROWS + 2, COLS, CHAN)
    return pl.pallas_call(
        weight_kernel,
        out_shape=(
            jax.ShapeDtypeStruct((CHIPS, 3 * PIECE, LANES), bf16),
            jax.ShapeDtypeStruct(pair, bf16),
        ),
        in_specs=[SMEM_SPEC] + [in_vmem] * 6,
        out_specs=(pl.BlockSpec(memory_space=pl.ANY), in_vmem),
        scratch_shapes=[
            pltpu.VMEM(pair, bf16),
            pltpu.VMEM((WIDE, 2 * (SLOTS + 2) * CELLS), bf16),
            pltpu.VMEM((2 * POS, 3 * TILE), bf16),
            pltpu.VMEM((9 * WIDE, TILE), f32),
            pltpu.VMEM((CHIPS, 3 * PIECE, LANES), bf16),
            pltpu.SemaphoreType.DMA((3,)),
        ],
        compiler_params=VMEM_LIMIT,
        cost_estimate=cost(FLOPS, 12 << 20),
        name="weight_terms",
    )(place, hidden, other, even, odd, cot, other_cot)


def shift(values, axes, count, step):
    pairs = [(i, i + step) for i in range(count) if 0 <= i + step < count]
    return lax.ppermute(values, axes, pairs)


def swap_cores(values):
    return lax.ppermute(values, "core", [(0, 1), (1, 0)])


def edge_rows(block):
    low = shift(block[:, ROWS - 1 :], ROW_AXES, 8, 1)
    high = shift(block[:, :1], ROW_AXES, 8, -1)
    return low, high


def add_pairs(sums, axis, pairs):
    return sums + lax.ppermute(sums, axis, pairs + [(b, a) for a, b in pairs])


def per_group(first, second):
    grouped = jnp.concatenate([first, second], axis=0).reshape(2 * SLOTS, GROUPS, CHAN // GROUPS)
    return jnp.sum(grouped, axis=2)


def per_channel(grouped):
    return jnp.repeat(grouped, CHAN // GROUPS, axis=1)


def on_device(activations, frame_counts, norm_gain, norm_bias, conv_weight, cotangent):
    core = lax.axis_index("core")
    act = activations.reshape(POS, CHAN)
    gain, bias = norm_gain[None], norm_bias[None]

    sums = local_sums(activations)
    peers = lax.all_to_all(sums, ROW_AXES, 0, 0)
    source, rows_at_once, _ = lax.optimization_barrier((activations, cotangent, sums))
    low, high = edge_rows(jnp.concatenate([source, rows_at_once], 0))
    other_cot = swap_cores(rows_at_once)
    low, high, peers, other_cot = lax.optimization_barrier((low, high, peers, other_cot))

    tm = lax.axis_index(TM)
    count = frame_counts[tm]
    place = jnp.stack(
        [count, core, lax.axis_index(ROW_AXES), frame_counts[tm + 1 - 2 * core]]
    )
    wide_hidden, last_pair, head, mean, inv = make_hidden(
        place, peers, activations, cotangent, low, high, gain, bias
    )
    other_hidden = swap_cores(wide_hidden)
    even = lax.ppermute(last_pair, TM, [(i, i + 1) for i in range(1, 15, 2)])
    odd = lax.ppermute(last_pair, TM, [(i, i + 2) for i in range(1, 15, 2)])

    head = shift(head, TM, 16, -1)

    terms, before = weight_terms(
        place, wide_hidden, other_hidden, even, odd, cotangent, other_cot
    )
    terms, head = lax.optimization_barrier((terms, head))
    arrived = lax.all_to_all(terms, CHIP_AXES, 0, 0)

    low, high, _ = lax.optimization_barrier((low, high, terms))
    cots = make_cots(place, cotangent, low, high, head)
    pre_grad, first_grad, second_grad = backward_conv(
        cots, conv_weight, act, mean, inv, gain, bias
    )
    sums = per_group(first_grad, second_grad)
    parts = [lax.ppermute(sums, "x", [(i, (i + k) % 4) for i in range(4)]) for k in range(1, 4)]

    extended = jnp.concatenate([before, wide_hidden], axis=0)
    block_out = forward_conv(count[None], extended, conv_weight, act)
    block_out, parts, arrived = lax.optimization_barrier((block_out, parts, arrived))
    block_out = block_out.reshape(activations.shape)

    sums = add_pairs(sums + parts[0] + parts[1] + parts[2], "yhi", [(0, 1)])
    averages = per_channel(sums / CELL_COUNT)[:, None, None, :]
    first_avg, second_avg = averages[:SLOTS], averages[SLOTS:]
    wide_inv = inv[:, None, None, :]
    centred = (activations.astype(f32) - mean[:, None, None, :]) * wide_inv
    norm_part = wide_inv * (
        pre_grad.reshape(activations.shape) - first_avg - centred * second_avg
    )
    live = (jnp.arange(SLOTS) < count)[:, None, None, None]
    input_grad = jnp.where(live, cotangent.astype(f32) + norm_part, 0.0)

    frame_total = 1 + 4 * ((16 - 1) * 3 // 2)
    grad_scale = 1.0 / math.sqrt(frame_total * 8 * ROWS * COLS)
    total = jnp.sum(arrived.astype(f32), axis=0) * grad_scale
    shared = total[2 * PIECE :]
    parts = [
        jnp.concatenate(
            [total[k * PIECE : (k + 1) * PIECE], shared[:, k * 64 : (k + 1) * 64]], axis=1
        )
        for k in range(2)
    ]
    mine = jnp.where(core == 0, parts[0], parts[1])
    theirs = swap_cores(jnp.where(core == 0, parts[1], parts[0]))
    first = jnp.where(core == 0, mine, theirs)
    second = jnp.where(core == 0, theirs, mine)
    weight_grad = jnp.concatenate([first, second[:, LANES:], second[:, :LANES]], axis=1)
    return block_out, input_grad, weight_grad


def solution(mesh):
    fine = Mesh(mesh.devices.reshape(2, 4, 2, 2, 4), ALL_AXES)
    placed = P(TM, ROW_AXES, None, None)
    return jax.shard_map(
        on_device,
        mesh=fine,
        in_specs=(placed, P(), P(), P(), P(), placed),
        out_specs=(placed, placed, P(ALL_AXES, None)),
        check_vma=False,
    )
```

```python
import functools
import math

import jax
import jax.numpy as jnp
import numpy as np
from jax import lax
from jax.experimental import pallas as pl
from jax.experimental.pallas import tpu as pltpu
from jax.sharding import Mesh
from jax.sharding import PartitionSpec as P

GROUPS = 32
EPS = 1e-05
CHAN = 384
HALF = CHAN // 2
SLOTS = 8
ROWS = 4
COLS = 32
CELLS = ROWS * COLS
POS = SLOTS * CELLS
WIDE = 3 * CHAN
PIECE = 81
CHIPS = 64
LANES = 128
WIDE_CELLS = (ROWS + 2) * COLS
CELL_COUNT = 8 * CELLS * (CHAN // GROUPS)
TILE = 256

TM = ("ylo", "z", "core")
ROW_AXES = ("yhi", "x")
CHIP_AXES = ("ylo", "z", "yhi", "x")
ALL_AXES = TM + ROW_AXES

bf16 = jnp.bfloat16
f32 = jnp.float32
VMEM_LIMIT = pltpu.CompilerParams(vmem_limit_bytes=64 * 1024 * 1024)


def from_left(values):
    col = lax.broadcasted_iota(jnp.int32, values.shape, 0) % COLS
    return jnp.where(col == 0, 0.0, pltpu.roll(values, 1, 0))


def from_right(values):
    col = lax.broadcasted_iota(jnp.int32, values.shape, 0) % COLS
    return jnp.where(col == COLS - 1, 0.0, pltpu.roll(values, values.shape[0] - 1, 0))


def tap_products(x_ref, w_ref, acc, back, frames):
    step = pl.program_id(0)
    weights = w_ref[...]
    pieces = []
    for b in range(3):
        at = (2 - step, 2 - b) if back else (step, b)
        taken = x_ref[pl.ds(at[0], frames), pl.ds(at[1], ROWS)]
        pieces.append(taken.reshape(frames * CELLS, CHAN))
    left = jnp.concatenate(pieces, axis=1)
    if back:
        right = jnp.concatenate([weights[b * WIDE : (b + 1) * WIDE] for b in range(3)], axis=1)
        dims = (((1,), (1,)), ((), ()))
    else:
        right = jnp.concatenate(
            [
                jnp.concatenate(
                    [weights[(b * 3 + c) * CHAN : (b * 3 + c + 1) * CHAN] for c in range(3)], axis=1
                )
                for b in range(3)
            ],
            axis=0,
        )
        dims = (((1,), (0,)), ((), ()))
    product = lax.dot_general(left, right, dims, preferred_element_type=f32)

    @pl.when(step == 0)
    def _():
        acc[...] = product

    @pl.when(step > 0)
    def _():
        acc[...] += product


def forward_kernel(half, place_ref, before_ref, hidden_ref, w_ref, act_ref, *rest):
    out_ref, x, acc = rest[-3:]

    @pl.when(pl.program_id(0) == 0)
    def _():
        if half == 0:
            x[:2] = before_ref[...]
            x[2:] = hidden_ref[:4]
        else:
            x[...] = hidden_ref[2:]

    tap_products(x, w_ref, acc, False, SLOTS // 2)

    @pl.when(pl.program_id(0) == 2)
    def _():
        for frame in range(SLOTS // 2):
            rows = slice(frame * CELLS, (frame + 1) * CELLS)
            conv = (
                acc[rows, CHAN : 2 * CHAN]
                + from_left(acc[rows, :CHAN])
                + from_right(acc[rows, 2 * CHAN :])
            )
            total = act_ref[rows].astype(f32) + conv
            live = half * SLOTS // 2 + frame < place_ref[0]
            out_ref[rows] = jnp.where(live, total, 0.0).astype(bf16)


def backward_kernel(
    place_ref,
    cot_ref,
    low_ref,
    high_ref,
    head_ref,
    w_ref,
    act_ref,
    mean_ref,
    inv_ref,
    gain_ref,
    bias_ref,
    out_ref,
    first_ref,
    second_ref,
    x,
    acc,
):
    @pl.when(pl.program_id(0) == 0)
    def _():
        count = place_ref[0]
        for frame in range(SLOTS):

            @pl.when(frame < count)
            def _(frame=frame):
                x[frame, 0] = low_ref[SLOTS + frame, 0]
                x[frame, 1 : 1 + ROWS] = cot_ref[frame]
                x[frame, 1 + ROWS] = high_ref[SLOTS + frame, 0]

            @pl.when(frame >= count)
            def _(frame=frame):
                x[frame] = jnp.zeros((ROWS + 2, COLS, CHAN), bf16)

        x[SLOTS:] = jnp.zeros((2, ROWS + 2, COLS, CHAN), bf16)
        x[pl.ds(count, 2)] = head_ref[...]

    tap_products(x, w_ref, acc, True, SLOTS)

    @pl.when(pl.program_id(0) == 2)
    def _():
        gain = gain_ref[...]
        bias = bias_ref[...]
        for frame in range(SLOTS):
            rows = slice(frame * CELLS, (frame + 1) * CELLS)
            grad = (
                acc[rows, CHAN : 2 * CHAN]
                + from_right(acc[rows, :CHAN])
                + from_left(acc[rows, 2 * CHAN :])
            )
            centred = (act_ref[rows].astype(f32) - mean_ref[frame : frame + 1]) * inv_ref[
                frame : frame + 1
            ]
            pre_act = centred * gain + bias
            gate = jax.nn.sigmoid(pre_act)
            pre_grad = grad * gate * (1.0 + pre_act * (1.0 - gate)) * gain
            out_ref[rows] = pre_grad
            first_ref[frame : frame + 1] = jnp.sum(pre_grad, axis=0, keepdims=True)
            second_ref[frame : frame + 1] = jnp.sum(pre_grad * centred, axis=0, keepdims=True)


READY = ((0, 2), (2, 5), (5, 8))


def weight_kernel(
    place_ref,
    hidden_ref,
    other_ref,
    even_ref,
    odd_ref,
    cot_ref,
    other_cot_ref,
    out_ref,
    before_ref,
    other_before,
    turned,
    right,
    sums,
    packed,
    sems,
):
    core = place_ref[1]

    def last_two(ref, count, to_ref):
        @pl.when(count >= 2)
        def _():
            to_ref[...] = ref[pl.ds(jnp.maximum(count - 2, 0), 2)]

        @pl.when(count < 2)
        def _():
            to_ref[0] = jnp.zeros((ROWS + 2, COLS, CHAN), bf16)
            to_ref[1] = ref[0]

    @pl.when(core == 0)
    def _():
        before_ref[...] = even_ref[...]
        last_two(hidden_ref, place_ref[0], other_before)

    @pl.when(core == 1)
    def _():
        other_before[...] = odd_ref[...]
        last_two(other_ref, place_ref[3], before_ref)

    def turn(ref, f, column):
        for b in range(3):
            values = ref[f, b : b + ROWS].reshape(CELLS, CHAN)
            turned[b * CHAN : (b + 1) * CHAN, pl.ds(pl.multiple_of(column, CELLS), CELLS)] = values.T

    for block, (early, late) in enumerate(((before_ref, hidden_ref), (other_before, other_ref))):
        base = block * (SLOTS + 2) * CELLS
        for f in range(2):
            turn(early, f, base + f * CELLS)

        def turn_late(f, carry, late=late, base=base):
            turn(late, f, base + (f + 2) * CELLS)
            return carry

        lax.fori_loop(0, SLOTS, turn_late, 0, unroll=True)

    left_lanes = lax.broadcasted_iota(jnp.int32, (CELLS, LANES), 1) < LANES // 2

    def move(f, carry):
        for block, ref in enumerate((cot_ref, other_cot_ref)):
            values = ref[f].reshape(CELLS, CHAN).astype(f32)
            values = jnp.where(f < place_ref[3 * block], values, 0.0)
            middle = values[:, LANES : 2 * LANES]
            swapped = pltpu.roll(middle, LANES // 2, 1)
            first = core == 0
            outer = jnp.where(first, values[:, :LANES], values[:, 2 * LANES :])
            inner = jnp.where(left_lanes == first, middle, swapped)
            chosen = jnp.concatenate([outer, inner], axis=1)
            rows = pl.ds(pl.multiple_of(block * POS + f * CELLS, CELLS), CELLS)
            for c, moved in enumerate((from_right(chosen), chosen, from_left(chosen))):
                right[rows, c * TILE : (c + 1) * TILE] = moved.astype(bf16)
        return carry

    lax.fori_loop(0, SLOTS, move, 0, unroll=True)

    upper = lax.broadcasted_iota(jnp.int32, (PIECE, LANES), 1) >= LANES // 2
    copies = []
    for a in range(3):
        window = jnp.concatenate(
            [
                turned[:, start : start + POS]
                for block in range(2)
                for start in [(block * (SLOTS + 2) + a) * CELLS]
            ],
            axis=1,
        )
        product = jnp.dot(window, right[...], preferred_element_type=f32)
        for b in range(3):
            for c in range(3):
                at = ((a * 3 + b) * 3 + c) * CHAN
                sums[at : at + CHAN] = product[
                    b * CHAN : (b + 1) * CHAN, c * TILE : (c + 1) * TILE
                ]
        for chip in range(8 * READY[a][0], 8 * READY[a][1]):
            start = 1296 * (chip // 8) + PIECE * (chip % 8)
            first, second = sums[start : start + PIECE], sums[start + 648 : start + 648 + PIECE]
            block = jnp.concatenate(
                [
                    first[:, :LANES],
                    second[:, :LANES],
                    jnp.where(upper, second[:, LANES:], first[:, LANES:]),
                ],
                axis=0,
            )
            packed[chip] = block.astype(bf16)
        chips = pl.ds(8 * READY[a][0], 8 * (READY[a][1] - READY[a][0]))
        copies.append(pltpu.make_async_copy(packed.at[chips], out_ref.at[chips], sems.at[a]))
        copies[-1].start()
    for copy in copies:
        copy.wait()


def sums_kernel(act_ref, out_ref):
    firsts, seconds = [], []
    for frame in range(SLOTS):
        values = act_ref[frame].reshape(CELLS, CHAN).astype(f32)
        firsts.append(jnp.sum(values, axis=0, keepdims=True))
        seconds.append(jnp.sum(values * values, axis=0, keepdims=True))
    both = jnp.concatenate(firsts + seconds, axis=0)
    for peer in range(8):
        out_ref[peer] = both


def group_means(sums, same_ref):
    return jnp.dot(
        sums, same_ref[...], precision=lax.Precision.HIGHEST, preferred_element_type=f32
    ) * (1.0 / CELL_COUNT)


def hidden_kernel(
    place_ref,
    peers_ref,
    same_ref,
    act_ref,
    low_ref,
    high_ref,
    cot_ref,
    cot_low_ref,
    cot_high_ref,
    gain_ref,
    bias_ref,
    hidden_ref,
    pair_ref,
    head_ref,
    mean_ref,
    inv_ref,
):
    step = pl.program_id(0)
    count, row_place = place_ref[0], place_ref[2]

    @pl.when(step == 0)
    def _():
        total = peers_ref[0]
        for peer in range(1, 8):
            total = total + peers_ref[peer]
        stats = group_means(total, same_ref)
        mean_ref[...] = stats[:SLOTS]
        inv_ref[...] = lax.rsqrt(stats[SLOTS:] - stats[:SLOTS] * stats[:SLOTS] + EPS)
        pair_ref[0] = jnp.zeros((ROWS + 2, COLS, CHAN), bf16)
        head_ref[:, :1] = cot_low_ref[...]
        head_ref[:, 1 : 1 + ROWS] = cot_ref[...]
        head_ref[:, 1 + ROWS :] = cot_high_ref[...]

    gain = gain_ref[...]
    bias = bias_ref[...]
    for k in range(2):
        frame = step * 2 + k
        live = frame < count
        mean = mean_ref[pl.ds(frame, 1)]
        inv = inv_ref[pl.ds(frame, 1)]

        def activated(values, keep, mean=mean, inv=inv):
            pre_act = (values.astype(f32) - mean) * inv * gain + bias
            return jnp.where(keep, pre_act * jax.nn.sigmoid(pre_act), 0.0).astype(bf16)

        hidden = activated(act_ref[k].reshape(CELLS, CHAN), live)
        hidden_ref[k, 1 : 1 + ROWS] = hidden.reshape(ROWS, COLS, CHAN)
        hidden_ref[k, 0] = activated(low_ref[k, 0], live & (row_place > 0))
        hidden_ref[k, 1 + ROWS] = activated(high_ref[k, 0], live & (row_place < 7))
        for late in range(2):

            @pl.when(frame == count - 2 + late)
            def _(k=k, late=late):
                pair_ref[late] = hidden_ref[k]


def whole(shape):
    return pl.BlockSpec(shape, lambda step: (0,) * len(shape))


def cost(flops, moved):
    return pl.CostEstimate(flops=flops, bytes_accessed=moved, transcendentals=0)


FLOPS = 2 * POS * 27 * CHAN * CHAN
TAPS_SPEC = pl.BlockSpec((3 * WIDE, CHAN), lambda step: (step, 0))


def forward_conv(half, place, before, hidden, weights, act, earlier=None):
    part = pl.BlockSpec((POS // 2, CHAN), lambda step: (half, 0))
    return pl.pallas_call(
        functools.partial(forward_kernel, half),
        out_shape=jax.ShapeDtypeStruct((POS, CHAN), bf16),
        grid=(3,),
        in_specs=[SMEM_SPEC, whole(before.shape), whole(hidden.shape), TAPS_SPEC, part]
        + [pl.BlockSpec(memory_space=pl.ANY)] * half,
        out_specs=part,
        scratch_shapes=[
            pltpu.VMEM((SLOTS // 2 + 2, ROWS + 2, COLS, CHAN), bf16),
            pltpu.VMEM((POS // 2, WIDE), f32),
        ],
        input_output_aliases={5: 0} if half else {},
        compiler_params=VMEM_LIMIT,
        cost_estimate=cost(FLOPS // 2, 11 << 20),
        name="forward_conv",
    )(place, before, hidden, weights, act, *([earlier] if half else []))


def backward_conv(place, cot, low, high, head, weights, act, mean, inv, gain, bias):
    smalls = [mean, inv, gain, bias]
    return pl.pallas_call(
        backward_kernel,
        out_shape=(
            jax.ShapeDtypeStruct((POS, CHAN), f32),
            jax.ShapeDtypeStruct((SLOTS, CHAN), f32),
            jax.ShapeDtypeStruct((SLOTS, CHAN), f32),
        ),
        grid=(3,),
        in_specs=[SMEM_SPEC]
        + [whole(v.shape) for v in (cot, low, high, head)]
        + [TAPS_SPEC, whole(act.shape)]
        + [whole(v.shape) for v in smalls],
        out_specs=(whole((POS, CHAN)), whole((SLOTS, CHAN)), whole((SLOTS, CHAN))),
        scratch_shapes=[
            pltpu.VMEM((SLOTS + 2, ROWS + 2, COLS, CHAN), bf16),
            pltpu.VMEM((POS, WIDE), f32),
        ],
        compiler_params=VMEM_LIMIT,
        cost_estimate=cost(FLOPS, 12 << 20),
        name="backward_conv",
    )(place, cot, low, high, head, weights, act, *smalls)


def local_sums(act):
    return pl.pallas_call(
        sums_kernel,
        out_shape=jax.ShapeDtypeStruct((8, 2 * SLOTS, CHAN), f32),
        compiler_params=VMEM_LIMIT,
        cost_estimate=cost(4 * POS * CHAN, 1 << 20),
        name="local_sums",
    )(act)


SMEM_SPEC = pl.BlockSpec(memory_space=pltpu.SMEM)


def same_group():
    group = np.arange(CHAN) // (CHAN // GROUPS)
    return jnp.asarray((group[:, None] == group[None, :]).astype(np.float32))


def frames_spec(*rest, first=0, last=SLOTS // 2 - 1):
    return pl.BlockSpec(
        (2,) + rest,
        lambda step: (first // 2 + jnp.minimum(step, last),) + (0,) * len(rest),
    )


def make_hidden(place, peers, act, cot, low, high, gain, bias):
    wide = (ROWS + 2, COLS, CHAN)
    return pl.pallas_call(
        hidden_kernel,
        out_shape=(
            jax.ShapeDtypeStruct((SLOTS,) + wide, bf16),
            jax.ShapeDtypeStruct((2,) + wide, bf16),
            jax.ShapeDtypeStruct((2,) + wide, bf16),
            jax.ShapeDtypeStruct((SLOTS, CHAN), f32),
            jax.ShapeDtypeStruct((SLOTS, CHAN), f32),
        ),
        grid=(SLOTS // 2,),
        in_specs=[
            SMEM_SPEC,
            whole(peers.shape),
            whole((CHAN, CHAN)),
            frames_spec(ROWS, COLS, CHAN),
            frames_spec(1, COLS, CHAN),
            frames_spec(1, COLS, CHAN),
            frames_spec(ROWS, COLS, CHAN, last=0),
            frames_spec(1, COLS, CHAN, first=SLOTS, last=0),
            frames_spec(1, COLS, CHAN, first=SLOTS, last=0),
            whole((1, CHAN)),
            whole((1, CHAN)),
        ],
        out_specs=(
            frames_spec(*wide),
            whole((2,) + wide),
            whole((2,) + wide),
            whole((SLOTS, CHAN)),
            whole((SLOTS, CHAN)),
        ),
        compiler_params=VMEM_LIMIT,
        cost_estimate=cost(40 * POS * CHAN, 5 << 20),
        name="make_hidden",
    )(place, peers, same_group(), act, low, high, cot, low, high, gain, bias)


def weight_terms(place, hidden, other, even, odd, cot, other_cot):
    in_vmem = pl.BlockSpec(memory_space=pltpu.VMEM)
    pair = (2, ROWS + 2, COLS, CHAN)
    return pl.pallas_call(
        weight_kernel,
        out_shape=(
            jax.ShapeDtypeStruct((CHIPS, 3 * PIECE, LANES), bf16),
            jax.ShapeDtypeStruct(pair, bf16),
        ),
        in_specs=[SMEM_SPEC] + [in_vmem] * 6,
        out_specs=(pl.BlockSpec(memory_space=pl.ANY), in_vmem),
        scratch_shapes=[
            pltpu.VMEM(pair, bf16),
            pltpu.VMEM((WIDE, 2 * (SLOTS + 2) * CELLS), bf16),
            pltpu.VMEM((2 * POS, 3 * TILE), bf16),
            pltpu.VMEM((9 * WIDE, TILE), f32),
            pltpu.VMEM((CHIPS, 3 * PIECE, LANES), bf16),
            pltpu.SemaphoreType.DMA((3,)),
        ],
        compiler_params=VMEM_LIMIT,
        cost_estimate=cost(FLOPS, 12 << 20),
        name="weight_terms",
    )(place, hidden, other, even, odd, cot, other_cot)


def shift(values, axes, count, step):
    pairs = [(i, i + step) for i in range(count) if 0 <= i + step < count]
    return lax.ppermute(values, axes, pairs)


def swap_cores(values):
    return lax.ppermute(values, "core", [(0, 1), (1, 0)])


def edge_rows(block):
    low = shift(block[:, ROWS - 1 :], ROW_AXES, 8, 1)
    high = shift(block[:, :1], ROW_AXES, 8, -1)
    return low, high


def per_group(first, second):
    grouped = jnp.concatenate([first, second], axis=0).reshape(2 * SLOTS, GROUPS, CHAN // GROUPS)
    return jnp.sum(grouped, axis=2)


def per_channel(grouped):
    return jnp.repeat(grouped, CHAN // GROUPS, axis=1)


def on_device(activations, frame_counts, norm_gain, norm_bias, conv_weight, cotangent):
    core = lax.axis_index("core")
    act = activations.reshape(POS, CHAN)
    gain, bias = norm_gain[None], norm_bias[None]

    sums = local_sums(activations)
    peers = lax.all_to_all(sums, ROW_AXES, 0, 0)
    source, rows_at_once, _ = lax.optimization_barrier((activations, cotangent, sums))
    low, high = edge_rows(jnp.concatenate([source, rows_at_once], 0))
    other_cot = swap_cores(rows_at_once)
    low, high, peers, other_cot = lax.optimization_barrier((low, high, peers, other_cot))

    tm = lax.axis_index(TM)
    count = frame_counts[tm]
    place = jnp.stack(
        [count, core, lax.axis_index(ROW_AXES), frame_counts[tm + 1 - 2 * core]]
    )
    wide_hidden, last_pair, head, mean, inv = make_hidden(
        place, peers, activations, cotangent, low, high, gain, bias
    )
    other_hidden = swap_cores(wide_hidden)
    even = lax.ppermute(last_pair, TM, [(i, i + 1) for i in range(1, 15, 2)])
    odd = lax.ppermute(last_pair, TM, [(i, i + 2) for i in range(1, 15, 2)])

    head = shift(head, TM, 16, -1)

    terms, before = weight_terms(
        place, wide_hidden, other_hidden, even, odd, cotangent, other_cot
    )
    terms, head = lax.optimization_barrier((terms, head))
    arrived = lax.all_to_all(terms, CHIP_AXES, 0, 0)

    low, high, _ = lax.optimization_barrier((low, high, terms))
    pre_grad, first_grad, second_grad = backward_conv(
        place, cotangent, low, high, head, conv_weight, act, mean, inv, gain, bias
    )
    sums = per_group(first_grad, second_grad)
    parts = [lax.ppermute(sums, "x", [(i, (i + k) % 4) for i in range(4)]) for k in range(1, 4)]

    block_out = forward_conv(0, place, before, wide_hidden, conv_weight, act)
    block_out, parts = lax.optimization_barrier((block_out, parts))
    sums = sums + parts[0] + parts[1] + parts[2]
    other = lax.ppermute(sums, "yhi", [(0, 1), (1, 0)])
    block_out = forward_conv(1, place, before, wide_hidden, conv_weight, act, block_out)
    block_out, other = lax.optimization_barrier((block_out, other))
    block_out = block_out.reshape(activations.shape)
    sums = sums + other

    averages = per_channel(sums / CELL_COUNT)[:, None, None, :]
    first_avg, second_avg = averages[:SLOTS], averages[SLOTS:]
    wide_inv = inv[:, None, None, :]
    centred = (activations.astype(f32) - mean[:, None, None, :]) * wide_inv
    norm_part = wide_inv * (
        pre_grad.reshape(activations.shape) - first_avg - centred * second_avg
    )
    live = (jnp.arange(SLOTS) < count)[:, None, None, None]
    input_grad = jnp.where(live, cotangent.astype(f32) + norm_part, 0.0)
    arrived, input_grad = lax.optimization_barrier((arrived, input_grad))

    frame_total = 1 + 4 * ((16 - 1) * 3 // 2)
    grad_scale = 1.0 / math.sqrt(frame_total * 8 * ROWS * COLS)
    total = jnp.sum(arrived.astype(f32), axis=0) * grad_scale
    shared = total[2 * PIECE :]
    parts = [
        jnp.concatenate(
            [total[k * PIECE : (k + 1) * PIECE], shared[:, k * 64 : (k + 1) * 64]], axis=1
        )
        for k in range(2)
    ]
    mine = jnp.where(core == 0, parts[0], parts[1])
    theirs = swap_cores(jnp.where(core == 0, parts[1], parts[0]))
    first = jnp.where(core == 0, mine, theirs)
    second = jnp.where(core == 0, theirs, mine)
    weight_grad = jnp.concatenate([first, second[:, LANES:], second[:, :LANES]], axis=1)
    return block_out, input_grad, weight_grad


def solution(mesh):
    fine = Mesh(mesh.devices.reshape(2, 4, 2, 2, 4), ALL_AXES)
    placed = P(TM, ROW_AXES, None, None)
    return jax.shard_map(
        on_device,
        mesh=fine,
        in_specs=(placed, P(), P(), P(), P(), placed),
        out_specs=(placed, placed, P(ALL_AXES, None)),
        check_vma=False,
    )
```

```python
import math

import jax
import jax.numpy as jnp
import numpy as np
from jax import lax
from jax.experimental import pallas as pl
from jax.experimental.pallas import tpu as pltpu
from jax.sharding import Mesh
from jax.sharding import PartitionSpec as P

GROUPS = 32
EPS = 1e-05
CHAN = 384
HALF = CHAN // 2
SLOTS = 8
ROWS = 4
COLS = 32
CELLS = ROWS * COLS
POS = SLOTS * CELLS
WIDE = 3 * CHAN
PIECE = 81
CHIPS = 64
LANES = 128
WIDE_CELLS = (ROWS + 2) * COLS
CELL_COUNT = 8 * CELLS * (CHAN // GROUPS)
TILE = 256

TM = ("ylo", "z", "core")
ROW_AXES = ("yhi", "x")
CHIP_AXES = ("ylo", "z", "yhi", "x")
ALL_AXES = TM + ROW_AXES

bf16 = jnp.bfloat16
f32 = jnp.float32
VMEM_LIMIT = pltpu.CompilerParams(vmem_limit_bytes=64 * 1024 * 1024)


def from_left(values):
    col = lax.broadcasted_iota(jnp.int32, values.shape, 0) % COLS
    return jnp.where(col == 0, 0.0, pltpu.roll(values, 1, 0))


def from_right(values):
    col = lax.broadcasted_iota(jnp.int32, values.shape, 0) % COLS
    return jnp.where(col == COLS - 1, 0.0, pltpu.roll(values, values.shape[0] - 1, 0))


def tap_products(x_ref, w_ref, acc, back):
    step = pl.program_id(0)
    weights = w_ref[...]
    pieces = []
    for b in range(3):
        at = (2 - step, 2 - b) if back else (step, b)
        pieces.append(x_ref[pl.ds(at[0], SLOTS), pl.ds(at[1], ROWS)].reshape(POS, CHAN))
    left = jnp.concatenate(pieces, axis=1)
    if back:
        right = jnp.concatenate([weights[b * WIDE : (b + 1) * WIDE] for b in range(3)], axis=1)
        dims = (((1,), (1,)), ((), ()))
    else:
        right = jnp.concatenate(
            [
                jnp.concatenate(
                    [weights[(b * 3 + c) * CHAN : (b * 3 + c + 1) * CHAN] for c in range(3)], axis=1
                )
                for b in range(3)
            ],
            axis=0,
        )
        dims = (((1,), (0,)), ((), ()))
    product = lax.dot_general(left, right, dims, preferred_element_type=f32)

    @pl.when(step == 0)
    def _():
        acc[...] = product

    @pl.when(step > 0)
    def _():
        acc[...] += product


def forward_kernel(place_ref, before_ref, hidden_ref, w_ref, act_ref, out_ref, x, acc):
    @pl.when(pl.program_id(0) == 0)
    def _():
        x[:2] = before_ref[...]
        x[2:] = hidden_ref[...]

    tap_products(x, w_ref, acc, False)

    @pl.when(pl.program_id(0) == 2)
    def _():
        for frame in range(SLOTS):
            rows = slice(frame * CELLS, (frame + 1) * CELLS)
            conv = (
                acc[rows, CHAN : 2 * CHAN]
                + from_left(acc[rows, :CHAN])
                + from_right(acc[rows, 2 * CHAN :])
            )
            total = act_ref[rows].astype(f32) + conv
            out_ref[rows] = jnp.where(frame < place_ref[0], total, 0.0).astype(bf16)


def backward_kernel(
    place_ref,
    cot_ref,
    low_ref,
    high_ref,
    head_ref,
    w_ref,
    act_ref,
    mean_ref,
    inv_ref,
    gain_ref,
    bias_ref,
    out_ref,
    first_ref,
    second_ref,
    x,
    acc,
):
    @pl.when(pl.program_id(0) == 0)
    def _():
        count = place_ref[0]
        for frame in range(SLOTS):

            @pl.when(frame < count)
            def _(frame=frame):
                x[frame, 0] = low_ref[SLOTS + frame, 0]
                x[frame, 1 : 1 + ROWS] = cot_ref[frame]
                x[frame, 1 + ROWS] = high_ref[SLOTS + frame, 0]

            @pl.when(frame >= count)
            def _(frame=frame):
                x[frame] = jnp.zeros((ROWS + 2, COLS, CHAN), bf16)

        x[SLOTS:] = jnp.zeros((2, ROWS + 2, COLS, CHAN), bf16)
        x[pl.ds(count, 2)] = head_ref[...]

    tap_products(x, w_ref, acc, True)

    @pl.when(pl.program_id(0) == 2)
    def _():
        gain = gain_ref[...]
        bias = bias_ref[...]
        for frame in range(SLOTS):
            rows = slice(frame * CELLS, (frame + 1) * CELLS)
            grad = (
                acc[rows, CHAN : 2 * CHAN]
                + from_right(acc[rows, :CHAN])
                + from_left(acc[rows, 2 * CHAN :])
            )
            centred = (act_ref[rows].astype(f32) - mean_ref[frame : frame + 1]) * inv_ref[
                frame : frame + 1
            ]
            pre_act = centred * gain + bias
            gate = jax.nn.sigmoid(pre_act)
            pre_grad = grad * gate * (1.0 + pre_act * (1.0 - gate)) * gain
            out_ref[rows] = pre_grad
            first_ref[frame : frame + 1] = jnp.sum(pre_grad, axis=0, keepdims=True)
            second_ref[frame : frame + 1] = jnp.sum(pre_grad * centred, axis=0, keepdims=True)


READY = ((0, 2), (2, 5), (5, 8))


def weight_kernel(
    place_ref,
    hidden_ref,
    other_ref,
    even_ref,
    odd_ref,
    cot_ref,
    other_cot_ref,
    out_ref,
    before_ref,
    other_before,
    turned,
    right,
    sums,
    packed,
    sems,
):
    core = place_ref[1]

    def last_two(ref, count, to_ref):
        @pl.when(count >= 2)
        def _():
            to_ref[...] = ref[pl.ds(jnp.maximum(count - 2, 0), 2)]

        @pl.when(count < 2)
        def _():
            to_ref[0] = jnp.zeros((ROWS + 2, COLS, CHAN), bf16)
            to_ref[1] = ref[0]

    @pl.when(core == 0)
    def _():
        before_ref[...] = even_ref[...]
        last_two(hidden_ref, place_ref[0], other_before)

    @pl.when(core == 1)
    def _():
        other_before[...] = odd_ref[...]
        last_two(other_ref, place_ref[3], before_ref)

    def turn(ref, f, column):
        for b in range(3):
            values = ref[f, b : b + ROWS].reshape(CELLS, CHAN)
            turned[b * CHAN : (b + 1) * CHAN, pl.ds(pl.multiple_of(column, CELLS), CELLS)] = values.T

    for block, (early, late) in enumerate(((before_ref, hidden_ref), (other_before, other_ref))):
        base = block * (SLOTS + 2) * CELLS
        for f in range(2):
            turn(early, f, base + f * CELLS)

        def turn_late(f, carry, late=late, base=base):
            turn(late, f, base + (f + 2) * CELLS)
            return carry

        lax.fori_loop(0, SLOTS, turn_late, 0, unroll=True)

    left_lanes = lax.broadcasted_iota(jnp.int32, (CELLS, LANES), 1) < LANES // 2

    def move(f, carry):
        for block, ref in enumerate((cot_ref, other_cot_ref)):
            values = ref[f].reshape(CELLS, CHAN).astype(f32)
            values = jnp.where(f < place_ref[3 * block], values, 0.0)
            middle = values[:, LANES : 2 * LANES]
            swapped = pltpu.roll(middle, LANES // 2, 1)
            first = core == 0
            outer = jnp.where(first, values[:, :LANES], values[:, 2 * LANES :])
            inner = jnp.where(left_lanes == first, middle, swapped)
            chosen = jnp.concatenate([outer, inner], axis=1)
            rows = pl.ds(pl.multiple_of(block * POS + f * CELLS, CELLS), CELLS)
            for c, moved in enumerate((from_right(chosen), chosen, from_left(chosen))):
                right[rows, c * TILE : (c + 1) * TILE] = moved.astype(bf16)
        return carry

    lax.fori_loop(0, SLOTS, move, 0, unroll=True)

    upper = lax.broadcasted_iota(jnp.int32, (PIECE, LANES), 1) >= LANES // 2
    copies = []
    for a in range(3):
        window = jnp.concatenate(
            [
                turned[:, start : start + POS]
                for block in range(2)
                for start in [(block * (SLOTS + 2) + a) * CELLS]
            ],
            axis=1,
        )
        product = jnp.dot(window, right[...], preferred_element_type=f32)
        for b in range(3):
            for c in range(3):
                at = ((a * 3 + b) * 3 + c) * CHAN
                sums[at : at + CHAN] = product[
                    b * CHAN : (b + 1) * CHAN, c * TILE : (c + 1) * TILE
                ]
        for chip in range(8 * READY[a][0], 8 * READY[a][1]):
            start = 1296 * (chip // 8) + PIECE * (chip % 8)
            first, second = sums[start : start + PIECE], sums[start + 648 : start + 648 + PIECE]
            block = jnp.concatenate(
                [
                    first[:, :LANES],
                    second[:, :LANES],
                    jnp.where(upper, second[:, LANES:], first[:, LANES:]),
                ],
                axis=0,
            )
            packed[chip] = block.astype(bf16)
        chips = pl.ds(8 * READY[a][0], 8 * (READY[a][1] - READY[a][0]))
        copies.append(pltpu.make_async_copy(packed.at[chips], out_ref.at[chips], sems.at[a]))
        copies[-1].start()
    for copy in copies:
        copy.wait()


def sums_kernel(act_ref, out_ref):
    firsts, seconds = [], []
    for frame in range(SLOTS):
        values = act_ref[frame].reshape(CELLS, CHAN).astype(f32)
        firsts.append(jnp.sum(values, axis=0, keepdims=True))
        seconds.append(jnp.sum(values * values, axis=0, keepdims=True))
    both = jnp.concatenate(firsts + seconds, axis=0)
    for peer in range(8):
        out_ref[peer] = both


def group_means(sums, same_ref):
    return jnp.dot(
        sums, same_ref[...], precision=lax.Precision.HIGHEST, preferred_element_type=f32
    ) * (1.0 / CELL_COUNT)


def hidden_kernel(
    place_ref,
    peers_ref,
    same_ref,
    act_ref,
    low_ref,
    high_ref,
    cot_ref,
    cot_low_ref,
    cot_high_ref,
    gain_ref,
    bias_ref,
    hidden_ref,
    pair_ref,
    head_ref,
    mean_ref,
    inv_ref,
):
    step = pl.program_id(0)
    count, row_place = place_ref[0], place_ref[2]

    @pl.when(step == 0)
    def _():
        total = peers_ref[0]
        for peer in range(1, 8):
            total = total + peers_ref[peer]
        stats = group_means(total, same_ref)
        mean_ref[...] = stats[:SLOTS]
        inv_ref[...] = lax.rsqrt(stats[SLOTS:] - stats[:SLOTS] * stats[:SLOTS] + EPS)
        pair_ref[0] = jnp.zeros((ROWS + 2, COLS, CHAN), bf16)
        head_ref[:, :1] = cot_low_ref[...]
        head_ref[:, 1 : 1 + ROWS] = cot_ref[...]
        head_ref[:, 1 + ROWS :] = cot_high_ref[...]

    gain = gain_ref[...]
    bias = bias_ref[...]
    for k in range(2):
        frame = step * 2 + k
        live = frame < count
        mean = mean_ref[pl.ds(frame, 1)]
        inv = inv_ref[pl.ds(frame, 1)]

        def activated(values, keep, mean=mean, inv=inv):
            pre_act = (values.astype(f32) - mean) * inv * gain + bias
            return jnp.where(keep, pre_act * jax.nn.sigmoid(pre_act), 0.0).astype(bf16)

        hidden = activated(act_ref[k].reshape(CELLS, CHAN), live)
        hidden_ref[k, 1 : 1 + ROWS] = hidden.reshape(ROWS, COLS, CHAN)
        hidden_ref[k, 0] = activated(low_ref[k, 0], live & (row_place > 0))
        hidden_ref[k, 1 + ROWS] = activated(high_ref[k, 0], live & (row_place < 7))
        for late in range(2):

            @pl.when(frame == count - 2 + late)
            def _(k=k, late=late):
                pair_ref[late] = hidden_ref[k]


def whole(shape):
    return pl.BlockSpec(shape, lambda step: (0,) * len(shape))


def cost(flops, moved):
    return pl.CostEstimate(flops=flops, bytes_accessed=moved, transcendentals=0)


FLOPS = 2 * POS * 27 * CHAN * CHAN
TAPS_SPEC = pl.BlockSpec((3 * WIDE, CHAN), lambda step: (step, 0))


def forward_conv(place, before, hidden, weights, act):
    return pl.pallas_call(
        forward_kernel,
        out_shape=jax.ShapeDtypeStruct((POS, CHAN), bf16),
        grid=(3,),
        in_specs=[
            SMEM_SPEC,
            whole(before.shape),
            whole(hidden.shape),
            TAPS_SPEC,
            whole(act.shape),
        ],
        out_specs=whole((POS, CHAN)),
        scratch_shapes=[
            pltpu.VMEM((SLOTS + 2, ROWS + 2, COLS, CHAN), bf16),
            pltpu.VMEM((POS, WIDE), f32),
        ],
        compiler_params=VMEM_LIMIT,
        cost_estimate=cost(FLOPS, 12 << 20),
        name="forward_conv",
    )(place, before, hidden, weights, act)


def backward_conv(place, cot, low, high, head, weights, act, mean, inv, gain, bias):
    smalls = [mean, inv, gain, bias]
    return pl.pallas_call(
        backward_kernel,
        out_shape=(
            jax.ShapeDtypeStruct((POS, CHAN), f32),
            jax.ShapeDtypeStruct((SLOTS, CHAN), f32),
            jax.ShapeDtypeStruct((SLOTS, CHAN), f32),
        ),
        grid=(3,),
        in_specs=[SMEM_SPEC]
        + [whole(v.shape) for v in (cot, low, high, head)]
        + [TAPS_SPEC, whole(act.shape)]
        + [whole(v.shape) for v in smalls],
        out_specs=(whole((POS, CHAN)), whole((SLOTS, CHAN)), whole((SLOTS, CHAN))),
        scratch_shapes=[
            pltpu.VMEM((SLOTS + 2, ROWS + 2, COLS, CHAN), bf16),
            pltpu.VMEM((POS, WIDE), f32),
        ],
        compiler_params=VMEM_LIMIT,
        cost_estimate=cost(FLOPS, 12 << 20),
        name="backward_conv",
    )(place, cot, low, high, head, weights, act, *smalls)


def local_sums(act):
    return pl.pallas_call(
        sums_kernel,
        out_shape=jax.ShapeDtypeStruct((8, 2 * SLOTS, CHAN), f32),
        compiler_params=VMEM_LIMIT,
        cost_estimate=cost(4 * POS * CHAN, 1 << 20),
        name="local_sums",
    )(act)


SMEM_SPEC = pl.BlockSpec(memory_space=pltpu.SMEM)


def same_group():
    group = np.arange(CHAN) // (CHAN // GROUPS)
    return jnp.asarray((group[:, None] == group[None, :]).astype(np.float32))


def frames_spec(*rest, first=0, last=SLOTS // 2 - 1):
    return pl.BlockSpec(
        (2,) + rest,
        lambda step: (first // 2 + jnp.minimum(step, last),) + (0,) * len(rest),
    )


def make_hidden(place, peers, act, cot, low, high, gain, bias):
    wide = (ROWS + 2, COLS, CHAN)
    return pl.pallas_call(
        hidden_kernel,
        out_shape=(
            jax.ShapeDtypeStruct((SLOTS,) + wide, bf16),
            jax.ShapeDtypeStruct((2,) + wide, bf16),
            jax.ShapeDtypeStruct((2,) + wide, bf16),
            jax.ShapeDtypeStruct((SLOTS, CHAN), f32),
            jax.ShapeDtypeStruct((SLOTS, CHAN), f32),
        ),
        grid=(SLOTS // 2,),
        in_specs=[
            SMEM_SPEC,
            whole(peers.shape),
            whole((CHAN, CHAN)),
            frames_spec(ROWS, COLS, CHAN),
            frames_spec(1, COLS, CHAN),
            frames_spec(1, COLS, CHAN),
            frames_spec(ROWS, COLS, CHAN, last=0),
            frames_spec(1, COLS, CHAN, first=SLOTS, last=0),
            frames_spec(1, COLS, CHAN, first=SLOTS, last=0),
            whole((1, CHAN)),
            whole((1, CHAN)),
        ],
        out_specs=(
            frames_spec(*wide),
            whole((2,) + wide),
            whole((2,) + wide),
            whole((SLOTS, CHAN)),
            whole((SLOTS, CHAN)),
        ),
        compiler_params=VMEM_LIMIT,
        cost_estimate=cost(40 * POS * CHAN, 5 << 20),
        name="make_hidden",
    )(place, peers, same_group(), act, low, high, cot, low, high, gain, bias)


def weight_terms(place, hidden, other, even, odd, cot, other_cot):
    in_vmem = pl.BlockSpec(memory_space=pltpu.VMEM)
    pair = (2, ROWS + 2, COLS, CHAN)
    return pl.pallas_call(
        weight_kernel,
        out_shape=(
            jax.ShapeDtypeStruct((CHIPS, 3 * PIECE, LANES), bf16),
            jax.ShapeDtypeStruct(pair, bf16),
        ),
        in_specs=[SMEM_SPEC] + [in_vmem] * 6,
        out_specs=(pl.BlockSpec(memory_space=pl.ANY), in_vmem),
        scratch_shapes=[
            pltpu.VMEM(pair, bf16),
            pltpu.VMEM((WIDE, 2 * (SLOTS + 2) * CELLS), bf16),
            pltpu.VMEM((2 * POS, 3 * TILE), bf16),
            pltpu.VMEM((9 * WIDE, TILE), f32),
            pltpu.VMEM((CHIPS, 3 * PIECE, LANES), bf16),
            pltpu.SemaphoreType.DMA((3,)),
        ],
        compiler_params=VMEM_LIMIT,
        cost_estimate=cost(FLOPS, 12 << 20),
        name="weight_terms",
    )(place, hidden, other, even, odd, cot, other_cot)


def shift(values, axes, count, step):
    pairs = [(i, i + step) for i in range(count) if 0 <= i + step < count]
    return lax.ppermute(values, axes, pairs)


def swap_cores(values):
    return lax.ppermute(values, "core", [(0, 1), (1, 0)])


def edge_rows(block):
    low = shift(block[:, ROWS - 1 :], ROW_AXES, 8, 1)
    high = shift(block[:, :1], ROW_AXES, 8, -1)
    return low, high


def per_group(first, second):
    grouped = jnp.concatenate([first, second], axis=0).reshape(2 * SLOTS, GROUPS, CHAN // GROUPS)
    return jnp.sum(grouped, axis=2)


def per_channel(grouped):
    return jnp.repeat(grouped, CHAN // GROUPS, axis=1)


def on_device(activations, frame_counts, norm_gain, norm_bias, conv_weight, cotangent):
    core = lax.axis_index("core")
    act = activations.reshape(POS, CHAN)
    gain, bias = norm_gain[None], norm_bias[None]

    sums = local_sums(activations)
    peers = lax.all_to_all(sums, ROW_AXES, 0, 0)
    source, rows_at_once, _ = lax.optimization_barrier((activations, cotangent, sums))
    low, high = edge_rows(jnp.concatenate([source, rows_at_once], 0))
    other_cot = swap_cores(rows_at_once)
    low, high, peers, other_cot = lax.optimization_barrier((low, high, peers, other_cot))

    tm = lax.axis_index(TM)
    count = frame_counts[tm]
    place = jnp.stack(
        [count, core, lax.axis_index(ROW_AXES), frame_counts[tm + 1 - 2 * core]]
    )
    wide_hidden, last_pair, head, mean, inv = make_hidden(
        place, peers, activations, cotangent, low, high, gain, bias
    )
    other_hidden = swap_cores(wide_hidden)
    even = lax.ppermute(last_pair, TM, [(i, i + 1) for i in range(1, 15, 2)])
    odd = lax.ppermute(last_pair, TM, [(i, i + 2) for i in range(1, 15, 2)])

    head = shift(head, TM, 16, -1)

    terms, before = weight_terms(
        place, wide_hidden, other_hidden, even, odd, cotangent, other_cot
    )
    terms, head = lax.optimization_barrier((terms, head))
    arrived = lax.all_to_all(terms, CHIP_AXES, 0, 0)

    low, high, _ = lax.optimization_barrier((low, high, terms))
    pre_grad, first_grad, second_grad = backward_conv(
        place, cotangent, low, high, head, conv_weight, act, mean, inv, gain, bias
    )
    sums = per_group(first_grad, second_grad)
    parts = [lax.ppermute(sums, "x", [(i, (i + k) % 4) for i in range(4)]) for k in range(1, 4)]

    block_out = forward_conv(place, before, wide_hidden, conv_weight, act)
    block_out, parts = lax.optimization_barrier((block_out, parts))
    block_out = block_out.reshape(activations.shape)
    sums = sums + parts[0] + parts[1] + parts[2]
    sums = sums + lax.ppermute(sums, "yhi", [(0, 1), (1, 0)])
    averages = per_channel(sums / CELL_COUNT)[:, None, None, :]
    first_avg, second_avg = averages[:SLOTS], averages[SLOTS:]
    wide_inv = inv[:, None, None, :]
    centred = (activations.astype(f32) - mean[:, None, None, :]) * wide_inv
    norm_part = wide_inv * (
        pre_grad.reshape(activations.shape) - first_avg - centred * second_avg
    )
    live = (jnp.arange(SLOTS) < count)[:, None, None, None]
    input_grad = jnp.where(live, cotangent.astype(f32) + norm_part, 0.0)
    arrived, input_grad = lax.optimization_barrier((arrived, input_grad))

    frame_total = 1 + 4 * ((16 - 1) * 3 // 2)
    grad_scale = 1.0 / math.sqrt(frame_total * 8 * ROWS * COLS)
    total = jnp.sum(arrived.astype(f32), axis=0) * grad_scale
    shared = total[2 * PIECE :]
    parts = [
        jnp.concatenate(
            [total[k * PIECE : (k + 1) * PIECE], shared[:, k * 64 : (k + 1) * 64]], axis=1
        )
        for k in range(2)
    ]
    mine = jnp.where(core == 0, parts[0], parts[1])
    theirs = swap_cores(jnp.where(core == 0, parts[1], parts[0]))
    first = jnp.where(core == 0, mine, theirs)
    second = jnp.where(core == 0, theirs, mine)
    weight_grad = jnp.concatenate([first, second[:, LANES:], second[:, :LANES]], axis=1)
    return block_out, input_grad, weight_grad


def solution(mesh):
    fine = Mesh(mesh.devices.reshape(2, 4, 2, 2, 4), ALL_AXES)
    placed = P(TM, ROW_AXES, None, None)
    return jax.shard_map(
        on_device,
        mesh=fine,
        in_specs=(placed, P(), P(), P(), P(), placed),
        out_specs=(placed, placed, P(ALL_AXES, None)),
        check_vma=False,
    )
```

```python
import math

import jax
import jax.numpy as jnp
import numpy as np
from jax import lax
from jax.experimental import pallas as pl
from jax.experimental.pallas import tpu as pltpu
from jax.sharding import Mesh
from jax.sharding import PartitionSpec as P

GROUPS = 32
EPS = 1e-05
CHAN = 384
HALF = CHAN // 2
SLOTS = 8
ROWS = 4
COLS = 32
CELLS = ROWS * COLS
POS = SLOTS * CELLS
WIDE = 3 * CHAN
PIECE = 81
CHIPS = 64
LANES = 128
WIDE_CELLS = (ROWS + 2) * COLS
CELL_COUNT = 8 * CELLS * (CHAN // GROUPS)
TILE = 256

TM = ("ylo", "z", "core")
ROW_AXES = ("yhi", "x")
CHIP_AXES = ("ylo", "z", "yhi", "x")
ALL_AXES = TM + ROW_AXES

bf16 = jnp.bfloat16
f32 = jnp.float32
VMEM_LIMIT = pltpu.CompilerParams(vmem_limit_bytes=64 * 1024 * 1024)


def from_left(values):
    col = lax.broadcasted_iota(jnp.int32, values.shape, 0) % COLS
    return jnp.where(col == 0, 0.0, pltpu.roll(values, 1, 0))


def from_right(values):
    col = lax.broadcasted_iota(jnp.int32, values.shape, 0) % COLS
    return jnp.where(col == COLS - 1, 0.0, pltpu.roll(values, values.shape[0] - 1, 0))


def tap_products(x_ref, w_ref, acc, back):
    step = pl.program_id(0)
    weights = w_ref[...]
    pieces = []
    for b in range(3):
        at = (2 - step, 2 - b) if back else (step, b)
        pieces.append(x_ref[pl.ds(at[0], SLOTS), pl.ds(at[1], ROWS)].reshape(POS, CHAN))
    left = jnp.concatenate(pieces, axis=1)
    if back:
        right = jnp.concatenate([weights[b * WIDE : (b + 1) * WIDE] for b in range(3)], axis=1)
        dims = (((1,), (1,)), ((), ()))
    else:
        right = jnp.concatenate(
            [
                jnp.concatenate(
                    [weights[(b * 3 + c) * CHAN : (b * 3 + c + 1) * CHAN] for c in range(3)], axis=1
                )
                for b in range(3)
            ],
            axis=0,
        )
        dims = (((1,), (0,)), ((), ()))
    product = lax.dot_general(left, right, dims, preferred_element_type=f32)

    @pl.when(step == 0)
    def _():
        acc[...] = product

    @pl.when(step > 0)
    def _():
        acc[...] += product


def forward_kernel(place_ref, before_ref, hidden_ref, w_ref, act_ref, out_ref, x, acc):
    @pl.when(pl.program_id(0) == 0)
    def _():
        x[:2] = before_ref[...]
        x[2:] = hidden_ref[...]

    tap_products(x, w_ref, acc, False)

    @pl.when(pl.program_id(0) == 2)
    def _():
        for frame in range(SLOTS):
            rows = slice(frame * CELLS, (frame + 1) * CELLS)
            conv = (
                acc[rows, CHAN : 2 * CHAN]
                + from_left(acc[rows, :CHAN])
                + from_right(acc[rows, 2 * CHAN :])
            )
            total = act_ref[rows].astype(f32) + conv
            out_ref[rows] = jnp.where(frame < place_ref[0], total, 0.0).astype(bf16)


def backward_kernel(
    place_ref,
    cot_ref,
    low_ref,
    high_ref,
    head_ref,
    w_ref,
    act_ref,
    mean_ref,
    inv_ref,
    gain_ref,
    bias_ref,
    out_ref,
    first_ref,
    second_ref,
    x,
    acc,
):
    @pl.when(pl.program_id(0) == 0)
    def _():
        count = place_ref[0]
        for frame in range(SLOTS):

            @pl.when(frame < count)
            def _(frame=frame):
                x[frame, 0] = low_ref[SLOTS + frame, 0]
                x[frame, 1 : 1 + ROWS] = cot_ref[frame]
                x[frame, 1 + ROWS] = high_ref[SLOTS + frame, 0]

            @pl.when(frame >= count)
            def _(frame=frame):
                x[frame] = jnp.zeros((ROWS + 2, COLS, CHAN), bf16)

        x[SLOTS:] = jnp.zeros((2, ROWS + 2, COLS, CHAN), bf16)
        x[pl.ds(count, 2)] = head_ref[...]

    tap_products(x, w_ref, acc, True)

    @pl.when(pl.program_id(0) == 2)
    def _():
        gain = gain_ref[...]
        bias = bias_ref[...]
        for frame in range(SLOTS):
            rows = slice(frame * CELLS, (frame + 1) * CELLS)
            grad = (
                acc[rows, CHAN : 2 * CHAN]
                + from_right(acc[rows, :CHAN])
                + from_left(acc[rows, 2 * CHAN :])
            )
            centred = (act_ref[rows].astype(f32) - mean_ref[frame : frame + 1]) * inv_ref[
                frame : frame + 1
            ]
            pre_act = centred * gain + bias
            gate = jax.nn.sigmoid(pre_act)
            pre_grad = grad * gate * (1.0 + pre_act * (1.0 - gate)) * gain
            out_ref[rows] = pre_grad
            first_ref[frame : frame + 1] = jnp.sum(pre_grad, axis=0, keepdims=True)
            second_ref[frame : frame + 1] = jnp.sum(pre_grad * centred, axis=0, keepdims=True)


READY = ((0, 2), (2, 5), (5, 8))


def weight_kernel(
    place_ref,
    hidden_ref,
    other_ref,
    even_ref,
    odd_ref,
    cot_ref,
    other_cot_ref,
    out_ref,
    before_ref,
    other_before,
    turned,
    right,
    sums,
    packed,
    sems,
):
    core = place_ref[1]

    def last_two(ref, count, to_ref):
        @pl.when(count >= 2)
        def _():
            to_ref[...] = ref[pl.ds(jnp.maximum(count - 2, 0), 2)]

        @pl.when(count < 2)
        def _():
            to_ref[0] = jnp.zeros((ROWS + 2, COLS, CHAN), bf16)
            to_ref[1] = ref[0]

    @pl.when(core == 0)
    def _():
        before_ref[...] = even_ref[...]
        last_two(hidden_ref, place_ref[0], other_before)

    @pl.when(core == 1)
    def _():
        other_before[...] = odd_ref[...]
        last_two(other_ref, place_ref[3], before_ref)

    def turn(ref, f, column):
        for b in range(3):
            values = ref[f, b : b + ROWS].reshape(CELLS, CHAN)
            turned[b * CHAN : (b + 1) * CHAN, pl.ds(pl.multiple_of(column, CELLS), CELLS)] = values.T

    for block, (early, late) in enumerate(((before_ref, hidden_ref), (other_before, other_ref))):
        base = block * (SLOTS + 2) * CELLS
        for f in range(2):
            turn(early, f, base + f * CELLS)

        def turn_late(f, carry, late=late, base=base):
            turn(late, f, base + (f + 2) * CELLS)
            return carry

        lax.fori_loop(0, SLOTS, turn_late, 0, unroll=True)

    left_lanes = lax.broadcasted_iota(jnp.int32, (CELLS, LANES), 1) < LANES // 2

    def move(f, carry):
        for block, ref in enumerate((cot_ref, other_cot_ref)):
            values = ref[f].reshape(CELLS, CHAN).astype(f32)
            values = jnp.where(f < place_ref[3 * block], values, 0.0)
            middle = values[:, LANES : 2 * LANES]
            swapped = pltpu.roll(middle, LANES // 2, 1)
            first = core == 0
            outer = jnp.where(first, values[:, :LANES], values[:, 2 * LANES :])
            inner = jnp.where(left_lanes == first, middle, swapped)
            chosen = jnp.concatenate([outer, inner], axis=1)
            rows = pl.ds(pl.multiple_of(block * POS + f * CELLS, CELLS), CELLS)
            for c, moved in enumerate((from_right(chosen), chosen, from_left(chosen))):
                right[rows, c * TILE : (c + 1) * TILE] = moved.astype(bf16)
        return carry

    lax.fori_loop(0, SLOTS, move, 0, unroll=True)

    upper = lax.broadcasted_iota(jnp.int32, (PIECE, LANES), 1) >= LANES // 2
    copies = []
    for a in range(3):
        window = jnp.concatenate(
            [
                turned[:, start : start + POS]
                for block in range(2)
                for start in [(block * (SLOTS + 2) + a) * CELLS]
            ],
            axis=1,
        )
        product = jnp.dot(window, right[...], preferred_element_type=f32)
        for b in range(3):
            for c in range(3):
                at = ((a * 3 + b) * 3 + c) * CHAN
                sums[at : at + CHAN] = product[
                    b * CHAN : (b + 1) * CHAN, c * TILE : (c + 1) * TILE
                ]
        for chip in range(8 * READY[a][0], 8 * READY[a][1]):
            start = 1296 * (chip // 8) + PIECE * (chip % 8)
            first, second = sums[start : start + PIECE], sums[start + 648 : start + 648 + PIECE]
            block = jnp.concatenate(
                [
                    first[:, :LANES],
                    second[:, :LANES],
                    jnp.where(upper, second[:, LANES:], first[:, LANES:]),
                ],
                axis=0,
            )
            packed[chip] = block.astype(bf16)
        chips = pl.ds(8 * READY[a][0], 8 * (READY[a][1] - READY[a][0]))
        copies.append(pltpu.make_async_copy(packed.at[chips], out_ref.at[chips], sems.at[a]))
        copies[-1].start()
    for copy in copies:
        copy.wait()


def sums_kernel(act_ref, out_ref):
    firsts, seconds = [], []
    for frame in range(SLOTS):
        values = act_ref[frame].reshape(CELLS, CHAN).astype(f32)
        firsts.append(jnp.sum(values, axis=0, keepdims=True))
        seconds.append(jnp.sum(values * values, axis=0, keepdims=True))
    both = jnp.concatenate(firsts + seconds, axis=0)
    for peer in range(8):
        out_ref[peer] = both


def group_means(sums, same_ref):
    return jnp.dot(
        sums, same_ref[...], precision=lax.Precision.HIGHEST, preferred_element_type=f32
    ) * (1.0 / CELL_COUNT)


def hidden_kernel(
    place_ref,
    peers_ref,
    same_ref,
    act_ref,
    low_ref,
    high_ref,
    cot_ref,
    cot_low_ref,
    cot_high_ref,
    gain_ref,
    bias_ref,
    hidden_ref,
    pair_ref,
    head_ref,
    mean_ref,
    inv_ref,
):
    step = pl.program_id(0)
    count, row_place = place_ref[0], place_ref[2]

    @pl.when(step == 0)
    def _():
        total = peers_ref[0]
        for peer in range(1, 8):
            total = total + peers_ref[peer]
        stats = group_means(total, same_ref)
        mean_ref[...] = stats[:SLOTS]
        inv_ref[...] = lax.rsqrt(stats[SLOTS:] - stats[:SLOTS] * stats[:SLOTS] + EPS)
        pair_ref[0] = jnp.zeros((ROWS + 2, COLS, CHAN), bf16)
        head_ref[:, :1] = cot_low_ref[...]
        head_ref[:, 1 : 1 + ROWS] = cot_ref[...]
        head_ref[:, 1 + ROWS :] = cot_high_ref[...]

    gain = gain_ref[...]
    bias = bias_ref[...]
    for k in range(4):
        frame = step * 4 + k
        live = frame < count
        mean = mean_ref[pl.ds(frame, 1)]
        inv = inv_ref[pl.ds(frame, 1)]

        def activated(values, keep, mean=mean, inv=inv):
            pre_act = (values.astype(f32) - mean) * inv * gain + bias
            return jnp.where(keep, pre_act * jax.nn.sigmoid(pre_act), 0.0).astype(bf16)

        hidden = activated(act_ref[k].reshape(CELLS, CHAN), live)
        hidden_ref[k, 1 : 1 + ROWS] = hidden.reshape(ROWS, COLS, CHAN)
        hidden_ref[k, 0] = activated(low_ref[k, 0], live & (row_place > 0))
        hidden_ref[k, 1 + ROWS] = activated(high_ref[k, 0], live & (row_place < 7))
        for late in range(2):

            @pl.when(frame == count - 2 + late)
            def _(k=k, late=late):
                pair_ref[late] = hidden_ref[k]


def whole(shape):
    return pl.BlockSpec(shape, lambda step: (0,) * len(shape))


def cost(flops, moved):
    return pl.CostEstimate(flops=flops, bytes_accessed=moved, transcendentals=0)


FLOPS = 2 * POS * 27 * CHAN * CHAN
TAPS_SPEC = pl.BlockSpec((3 * WIDE, CHAN), lambda step: (step, 0))


def forward_conv(place, before, hidden, weights, act):
    return pl.pallas_call(
        forward_kernel,
        out_shape=jax.ShapeDtypeStruct((POS, CHAN), bf16),
        grid=(3,),
        in_specs=[
            SMEM_SPEC,
            whole(before.shape),
            whole(hidden.shape),
            TAPS_SPEC,
            whole(act.shape),
        ],
        out_specs=whole((POS, CHAN)),
        scratch_shapes=[
            pltpu.VMEM((SLOTS + 2, ROWS + 2, COLS, CHAN), bf16),
            pltpu.VMEM((POS, WIDE), f32),
        ],
        compiler_params=VMEM_LIMIT,
        cost_estimate=cost(FLOPS, 12 << 20),
        name="forward_conv",
    )(place, before, hidden, weights, act)


def backward_conv(place, cot, low, high, head, weights, act, mean, inv, gain, bias):
    smalls = [mean, inv, gain, bias]
    return pl.pallas_call(
        backward_kernel,
        out_shape=(
            jax.ShapeDtypeStruct((POS, CHAN), f32),
            jax.ShapeDtypeStruct((SLOTS, CHAN), f32),
            jax.ShapeDtypeStruct((SLOTS, CHAN), f32),
        ),
        grid=(3,),
        in_specs=[SMEM_SPEC]
        + [whole(v.shape) for v in (cot, low, high, head)]
        + [TAPS_SPEC, whole(act.shape)]
        + [whole(v.shape) for v in smalls],
        out_specs=(whole((POS, CHAN)), whole((SLOTS, CHAN)), whole((SLOTS, CHAN))),
        scratch_shapes=[
            pltpu.VMEM((SLOTS + 2, ROWS + 2, COLS, CHAN), bf16),
            pltpu.VMEM((POS, WIDE), f32),
        ],
        compiler_params=VMEM_LIMIT,
        cost_estimate=cost(FLOPS, 12 << 20),
        name="backward_conv",
    )(place, cot, low, high, head, weights, act, *smalls)


def local_sums(act):
    return pl.pallas_call(
        sums_kernel,
        out_shape=jax.ShapeDtypeStruct((8, 2 * SLOTS, CHAN), f32),
        compiler_params=VMEM_LIMIT,
        cost_estimate=cost(4 * POS * CHAN, 1 << 20),
        name="local_sums",
    )(act)


SMEM_SPEC = pl.BlockSpec(memory_space=pltpu.SMEM)


def same_group():
    group = np.arange(CHAN) // (CHAN // GROUPS)
    return jnp.asarray((group[:, None] == group[None, :]).astype(np.float32))


def frames_spec(*rest, first=0, count=4, last=1):
    return pl.BlockSpec(
        (count,) + rest,
        lambda step: (first // count + jnp.minimum(step, last),) + (0,) * len(rest),
    )


def make_hidden(place, peers, act, cot, low, high, gain, bias):
    wide = (ROWS + 2, COLS, CHAN)
    return pl.pallas_call(
        hidden_kernel,
        out_shape=(
            jax.ShapeDtypeStruct((SLOTS,) + wide, bf16),
            jax.ShapeDtypeStruct((2,) + wide, bf16),
            jax.ShapeDtypeStruct((2,) + wide, bf16),
            jax.ShapeDtypeStruct((SLOTS, CHAN), f32),
            jax.ShapeDtypeStruct((SLOTS, CHAN), f32),
        ),
        grid=(2,),
        in_specs=[
            SMEM_SPEC,
            whole(peers.shape),
            whole((CHAN, CHAN)),
            frames_spec(ROWS, COLS, CHAN),
            frames_spec(1, COLS, CHAN),
            frames_spec(1, COLS, CHAN),
            frames_spec(ROWS, COLS, CHAN, count=2, last=0),
            frames_spec(1, COLS, CHAN, first=SLOTS, count=2, last=0),
            frames_spec(1, COLS, CHAN, first=SLOTS, count=2, last=0),
            whole((1, CHAN)),
            whole((1, CHAN)),
        ],
        out_specs=(
            frames_spec(*wide),
            whole((2,) + wide),
            whole((2,) + wide),
            whole((SLOTS, CHAN)),
            whole((SLOTS, CHAN)),
        ),
        compiler_params=VMEM_LIMIT,
        cost_estimate=cost(40 * POS * CHAN, 5 << 20),
        name="make_hidden",
    )(place, peers, same_group(), act, low, high, cot, low, high, gain, bias)


def weight_terms(place, hidden, other, even, odd, cot, other_cot):
    in_vmem = pl.BlockSpec(memory_space=pltpu.VMEM)
    pair = (2, ROWS + 2, COLS, CHAN)
    return pl.pallas_call(
        weight_kernel,
        out_shape=(
            jax.ShapeDtypeStruct((CHIPS, 3 * PIECE, LANES), bf16),
            jax.ShapeDtypeStruct(pair, bf16),
        ),
        in_specs=[SMEM_SPEC] + [in_vmem] * 6,
        out_specs=(pl.BlockSpec(memory_space=pl.ANY), in_vmem),
        scratch_shapes=[
            pltpu.VMEM(pair, bf16),
            pltpu.VMEM((WIDE, 2 * (SLOTS + 2) * CELLS), bf16),
            pltpu.VMEM((2 * POS, 3 * TILE), bf16),
            pltpu.VMEM((9 * WIDE, TILE), f32),
            pltpu.VMEM((CHIPS, 3 * PIECE, LANES), bf16),
            pltpu.SemaphoreType.DMA((3,)),
        ],
        compiler_params=VMEM_LIMIT,
        cost_estimate=cost(FLOPS, 12 << 20),
        name="weight_terms",
    )(place, hidden, other, even, odd, cot, other_cot)


def shift(values, axes, count, step):
    pairs = [(i, i + step) for i in range(count) if 0 <= i + step < count]
    return lax.ppermute(values, axes, pairs)


def swap_cores(values):
    return lax.ppermute(values, "core", [(0, 1), (1, 0)])


def edge_rows(block):
    low = shift(block[:, ROWS - 1 :], ROW_AXES, 8, 1)
    high = shift(block[:, :1], ROW_AXES, 8, -1)
    return low, high


def per_group(first, second):
    grouped = jnp.concatenate([first, second], axis=0).reshape(2 * SLOTS, GROUPS, CHAN // GROUPS)
    return jnp.sum(grouped, axis=2)


def per_channel(grouped):
    return jnp.repeat(grouped, CHAN // GROUPS, axis=1)


def on_device(activations, frame_counts, norm_gain, norm_bias, conv_weight, cotangent):
    core = lax.axis_index("core")
    act = activations.reshape(POS, CHAN)
    gain, bias = norm_gain[None], norm_bias[None]

    sums = local_sums(activations)
    peers = lax.all_to_all(sums, ROW_AXES, 0, 0)
    source, rows_at_once, _ = lax.optimization_barrier((activations, cotangent, sums))
    low, high = edge_rows(jnp.concatenate([source, rows_at_once], 0))
    other_cot = swap_cores(rows_at_once)
    low, high, peers, other_cot = lax.optimization_barrier((low, high, peers, other_cot))

    tm = lax.axis_index(TM)
    count = frame_counts[tm]
    place = jnp.stack(
        [count, core, lax.axis_index(ROW_AXES), frame_counts[tm + 1 - 2 * core]]
    )
    wide_hidden, last_pair, head, mean, inv = make_hidden(
        place, peers, activations, cotangent, low, high, gain, bias
    )
    other_hidden = swap_cores(wide_hidden)
    even = lax.ppermute(last_pair, TM, [(i, i + 1) for i in range(1, 15, 2)])
    odd = lax.ppermute(last_pair, TM, [(i, i + 2) for i in range(1, 15, 2)])

    head = shift(head, TM, 16, -1)

    terms, before = weight_terms(
        place, wide_hidden, other_hidden, even, odd, cotangent, other_cot
    )
    terms, head = lax.optimization_barrier((terms, head))
    arrived = lax.all_to_all(terms, CHIP_AXES, 0, 0)

    low, high, _ = lax.optimization_barrier((low, high, terms))
    pre_grad, first_grad, second_grad = backward_conv(
        place, cotangent, low, high, head, conv_weight, act, mean, inv, gain, bias
    )
    sums = per_group(first_grad, second_grad)
    parts = [lax.ppermute(sums, "x", [(i, (i + k) % 4) for i in range(4)]) for k in range(1, 4)]

    block_out = forward_conv(place, before, wide_hidden, conv_weight, act)
    block_out, parts, arrived = lax.optimization_barrier((block_out, parts, arrived))
    block_out = block_out.reshape(activations.shape)
    sums = sums + parts[0] + parts[1] + parts[2]
    sums, arrived = lax.optimization_barrier((sums, arrived))
    other = lax.ppermute(sums, "yhi", [(0, 1), (1, 0)])
    total = jnp.sum(arrived[: CHIPS // 2].astype(f32), axis=0)
    other, total, arrived = lax.optimization_barrier((other, total, arrived))
    total = total + jnp.sum(arrived[CHIPS // 2 :].astype(f32), axis=0)
    sums = sums + other
    averages = per_channel(sums / CELL_COUNT)[:, None, None, :]
    first_avg, second_avg = averages[:SLOTS], averages[SLOTS:]
    wide_inv = inv[:, None, None, :]
    centred = (activations.astype(f32) - mean[:, None, None, :]) * wide_inv
    norm_part = wide_inv * (
        pre_grad.reshape(activations.shape) - first_avg - centred * second_avg
    )
    live = (jnp.arange(SLOTS) < count)[:, None, None, None]
    input_grad = jnp.where(live, cotangent.astype(f32) + norm_part, 0.0)

    frame_total = 1 + 4 * ((16 - 1) * 3 // 2)
    grad_scale = 1.0 / math.sqrt(frame_total * 8 * ROWS * COLS)
    total = total * grad_scale
    shared = total[2 * PIECE :]
    parts = [
        jnp.concatenate(
            [total[k * PIECE : (k + 1) * PIECE], shared[:, k * 64 : (k + 1) * 64]], axis=1
        )
        for k in range(2)
    ]
    mine = jnp.where(core == 0, parts[0], parts[1])
    theirs = swap_cores(jnp.where(core == 0, parts[1], parts[0]))
    first = jnp.where(core == 0, mine, theirs)
    second = jnp.where(core == 0, theirs, mine)
    weight_grad = jnp.concatenate([first, second[:, LANES:], second[:, :LANES]], axis=1)
    return block_out, input_grad, weight_grad


def solution(mesh):
    fine = Mesh(mesh.devices.reshape(2, 4, 2, 2, 4), ALL_AXES)
    placed = P(TM, ROW_AXES, None, None)
    return jax.shard_map(
        on_device,
        mesh=fine,
        in_specs=(placed, P(), P(), P(), P(), placed),
        out_specs=(placed, placed, P(ALL_AXES, None)),
        check_vma=False,
    )
```

```python
import math

import jax
import jax.numpy as jnp
import numpy as np
from jax import lax
from jax.experimental import pallas as pl
from jax.experimental.pallas import tpu as pltpu
from jax.sharding import Mesh
from jax.sharding import PartitionSpec as P

GROUPS = 32
EPS = 1e-05
CHAN = 384
HALF = CHAN // 2
SLOTS = 8
ROWS = 4
COLS = 32
CELLS = ROWS * COLS
POS = SLOTS * CELLS
WIDE = 3 * CHAN
PIECE = 81
CHIPS = 64
LANES = 128
WIDE_CELLS = (ROWS + 2) * COLS
CELL_COUNT = 8 * CELLS * (CHAN // GROUPS)
TILE = 256

TM = ("ylo", "z", "core")
ROW_AXES = ("yhi", "x")
CHIP_AXES = ("ylo", "z", "yhi", "x")
ALL_AXES = TM + ROW_AXES

bf16 = jnp.bfloat16
f32 = jnp.float32
VMEM_LIMIT = pltpu.CompilerParams(vmem_limit_bytes=64 * 1024 * 1024)


def from_left(values):
    col = lax.broadcasted_iota(jnp.int32, values.shape, 0) % COLS
    return jnp.where(col == 0, 0.0, pltpu.roll(values, 1, 0))


def from_right(values):
    col = lax.broadcasted_iota(jnp.int32, values.shape, 0) % COLS
    return jnp.where(col == COLS - 1, 0.0, pltpu.roll(values, values.shape[0] - 1, 0))


def tap_products(x_ref, w_ref, acc, back):
    step = pl.program_id(0)
    weights = w_ref[...]
    pieces = []
    for b in range(3):
        at = (2 - step, 2 - b) if back else (step, b)
        pieces.append(x_ref[pl.ds(at[0], SLOTS), pl.ds(at[1], ROWS)].reshape(POS, CHAN))
    left = jnp.concatenate(pieces, axis=1)
    if back:
        right = jnp.concatenate([weights[b * WIDE : (b + 1) * WIDE] for b in range(3)], axis=1)
        dims = (((1,), (1,)), ((), ()))
    else:
        right = jnp.concatenate(
            [
                jnp.concatenate(
                    [weights[(b * 3 + c) * CHAN : (b * 3 + c + 1) * CHAN] for c in range(3)], axis=1
                )
                for b in range(3)
            ],
            axis=0,
        )
        dims = (((1,), (0,)), ((), ()))
    product = lax.dot_general(left, right, dims, preferred_element_type=f32)

    @pl.when(step == 0)
    def _():
        acc[...] = product

    @pl.when(step > 0)
    def _():
        acc[...] += product


def forward_kernel(place_ref, before_ref, hidden_ref, w_ref, act_ref, out_ref, x, acc):
    @pl.when(pl.program_id(0) == 0)
    def _():
        x[:2] = before_ref[...]
        x[2:] = hidden_ref[...]

    tap_products(x, w_ref, acc, False)

    @pl.when(pl.program_id(0) == 2)
    def _():
        for frame in range(SLOTS):
            rows = slice(frame * CELLS, (frame + 1) * CELLS)
            conv = (
                acc[rows, CHAN : 2 * CHAN]
                + from_left(acc[rows, :CHAN])
                + from_right(acc[rows, 2 * CHAN :])
            )
            total = act_ref[rows].astype(f32) + conv
            out_ref[rows] = jnp.where(frame < place_ref[0], total, 0.0).astype(bf16)


def backward_kernel(
    place_ref,
    cot_ref,
    low_ref,
    high_ref,
    head_ref,
    w_ref,
    act_ref,
    mean_ref,
    inv_ref,
    gain_ref,
    bias_ref,
    out_ref,
    first_ref,
    second_ref,
    x,
    acc,
):
    @pl.when(pl.program_id(0) == 0)
    def _():
        count = place_ref[0]
        for frame in range(SLOTS):

            @pl.when(frame < count)
            def _(frame=frame):
                x[frame, 0] = low_ref[SLOTS + frame, 0]
                x[frame, 1 : 1 + ROWS] = cot_ref[frame]
                x[frame, 1 + ROWS] = high_ref[SLOTS + frame, 0]

            @pl.when(frame >= count)
            def _(frame=frame):
                x[frame] = jnp.zeros((ROWS + 2, COLS, CHAN), bf16)

        x[SLOTS:] = jnp.zeros((2, ROWS + 2, COLS, CHAN), bf16)
        x[pl.ds(count, 2)] = head_ref[...]

    tap_products(x, w_ref, acc, True)

    @pl.when(pl.program_id(0) == 2)
    def _():
        gain = gain_ref[...]
        bias = bias_ref[...]
        for frame in range(SLOTS):
            rows = slice(frame * CELLS, (frame + 1) * CELLS)
            grad = (
                acc[rows, CHAN : 2 * CHAN]
                + from_right(acc[rows, :CHAN])
                + from_left(acc[rows, 2 * CHAN :])
            )
            centred = (act_ref[rows].astype(f32) - mean_ref[frame : frame + 1]) * inv_ref[
                frame : frame + 1
            ]
            pre_act = centred * gain + bias
            gate = jax.nn.sigmoid(pre_act)
            pre_grad = grad * gate * (1.0 + pre_act * (1.0 - gate)) * gain
            out_ref[rows] = pre_grad
            first_ref[frame : frame + 1] = jnp.sum(pre_grad, axis=0, keepdims=True)
            second_ref[frame : frame + 1] = jnp.sum(pre_grad * centred, axis=0, keepdims=True)


READY = ((0, 2), (2, 5), (5, 8))


def weight_kernel(
    place_ref,
    hidden_ref,
    other_ref,
    even_ref,
    odd_ref,
    cot_ref,
    other_cot_ref,
    out_ref,
    before_ref,
    other_before,
    turned,
    right,
    sums,
    packed,
    sems,
):
    core = place_ref[1]

    def last_two(ref, count, to_ref):
        @pl.when(count >= 2)
        def _():
            to_ref[...] = ref[pl.ds(jnp.maximum(count - 2, 0), 2)]

        @pl.when(count < 2)
        def _():
            to_ref[0] = jnp.zeros((ROWS + 2, COLS, CHAN), bf16)
            to_ref[1] = ref[0]

    @pl.when(core == 0)
    def _():
        before_ref[...] = even_ref[...]
        last_two(hidden_ref, place_ref[0], other_before)

    @pl.when(core == 1)
    def _():
        other_before[...] = odd_ref[...]
        last_two(other_ref, place_ref[3], before_ref)

    def turn(ref, f, column):
        for b in range(3):
            values = ref[f, b : b + ROWS].reshape(CELLS, CHAN)
            turned[b * CHAN : (b + 1) * CHAN, pl.ds(pl.multiple_of(column, CELLS), CELLS)] = values.T

    for block, (early, late) in enumerate(((before_ref, hidden_ref), (other_before, other_ref))):
        base = block * (SLOTS + 2) * CELLS
        for f in range(2):
            turn(early, f, base + f * CELLS)

        def turn_late(f, carry, late=late, base=base):
            turn(late, f, base + (f + 2) * CELLS)
            return carry

        lax.fori_loop(0, SLOTS, turn_late, 0, unroll=True)

    left_lanes = lax.broadcasted_iota(jnp.int32, (CELLS, LANES), 1) < LANES // 2

    def move(f, carry):
        for block, ref in enumerate((cot_ref, other_cot_ref)):
            values = ref[f].reshape(CELLS, CHAN).astype(f32)
            values = jnp.where(f < place_ref[3 * block], values, 0.0)
            middle = values[:, LANES : 2 * LANES]
            swapped = pltpu.roll(middle, LANES // 2, 1)
            first = core == 0
            outer = jnp.where(first, values[:, :LANES], values[:, 2 * LANES :])
            inner = jnp.where(left_lanes == first, middle, swapped)
            chosen = jnp.concatenate([outer, inner], axis=1)
            rows = pl.ds(pl.multiple_of(block * POS + f * CELLS, CELLS), CELLS)
            for c, moved in enumerate((from_right(chosen), chosen, from_left(chosen))):
                right[rows, c * TILE : (c + 1) * TILE] = moved.astype(bf16)
        return carry

    lax.fori_loop(0, SLOTS, move, 0, unroll=True)

    upper = lax.broadcasted_iota(jnp.int32, (PIECE, LANES), 1) >= LANES // 2
    copies = []
    for a in range(3):
        window = jnp.concatenate(
            [
                turned[:, start : start + POS]
                for block in range(2)
                for start in [(block * (SLOTS + 2) + a) * CELLS]
            ],
            axis=1,
        )
        product = jnp.dot(window, right[...], preferred_element_type=f32)
        for b in range(3):
            for c in range(3):
                at = ((a * 3 + b) * 3 + c) * CHAN
                sums[at : at + CHAN] = product[
                    b * CHAN : (b + 1) * CHAN, c * TILE : (c + 1) * TILE
                ]
        for chip in range(8 * READY[a][0], 8 * READY[a][1]):
            start = 1296 * (chip // 8) + PIECE * (chip % 8)
            first, second = sums[start : start + PIECE], sums[start + 648 : start + 648 + PIECE]
            block = jnp.concatenate(
                [
                    first[:, :LANES],
                    second[:, :LANES],
                    jnp.where(upper, second[:, LANES:], first[:, LANES:]),
                ],
                axis=0,
            )
            packed[chip] = block.astype(bf16)
        chips = pl.ds(8 * READY[a][0], 8 * (READY[a][1] - READY[a][0]))
        copies.append(pltpu.make_async_copy(packed.at[chips], out_ref.at[chips], sems.at[a]))
        copies[-1].start()
    for copy in copies:
        copy.wait()


def sums_kernel(act_ref, out_ref):
    firsts, seconds = [], []
    for frame in range(SLOTS):
        values = act_ref[frame].reshape(CELLS, CHAN).astype(f32)
        firsts.append(jnp.sum(values, axis=0, keepdims=True))
        seconds.append(jnp.sum(values * values, axis=0, keepdims=True))
    both = jnp.concatenate(firsts + seconds, axis=0)
    for peer in range(8):
        out_ref[peer] = both


def group_means(sums, same_ref):
    return jnp.dot(
        sums, same_ref[...], precision=lax.Precision.HIGHEST, preferred_element_type=f32
    ) * (1.0 / CELL_COUNT)


def hidden_kernel(
    place_ref,
    peers_ref,
    same_ref,
    act_ref,
    low_ref,
    high_ref,
    cot_ref,
    cot_low_ref,
    cot_high_ref,
    gain_ref,
    bias_ref,
    hidden_ref,
    pair_ref,
    head_ref,
    mean_ref,
    inv_ref,
):
    step = pl.program_id(0)
    count, row_place = place_ref[0], place_ref[2]

    @pl.when(step == 0)
    def _():
        total = peers_ref[0]
        for peer in range(1, 8):
            total = total + peers_ref[peer]
        stats = group_means(total, same_ref)
        mean_ref[...] = stats[:SLOTS]
        inv_ref[...] = lax.rsqrt(stats[SLOTS:] - stats[:SLOTS] * stats[:SLOTS] + EPS)
        pair_ref[0] = jnp.zeros((ROWS + 2, COLS, CHAN), bf16)
        head_ref[:, :1] = cot_low_ref[...]
        head_ref[:, 1 : 1 + ROWS] = cot_ref[...]
        head_ref[:, 1 + ROWS :] = cot_high_ref[...]

    gain = gain_ref[...]
    bias = bias_ref[...]
    for k in range(4):
        frame = step * 4 + k
        live = frame < count
        mean = mean_ref[pl.ds(frame, 1)]
        inv = inv_ref[pl.ds(frame, 1)]

        def activated(values, keep, mean=mean, inv=inv):
            pre_act = (values.astype(f32) - mean) * inv * gain + bias
            return jnp.where(keep, pre_act * jax.nn.sigmoid(pre_act), 0.0).astype(bf16)

        hidden = activated(act_ref[k].reshape(CELLS, CHAN), live)
        hidden_ref[k, 1 : 1 + ROWS] = hidden.reshape(ROWS, COLS, CHAN)
        hidden_ref[k, 0] = activated(low_ref[k, 0], live & (row_place > 0))
        hidden_ref[k, 1 + ROWS] = activated(high_ref[k, 0], live & (row_place < 7))
        for late in range(2):

            @pl.when(frame == count - 2 + late)
            def _(k=k, late=late):
                pair_ref[late] = hidden_ref[k]


def whole(shape):
    return pl.BlockSpec(shape, lambda step: (0,) * len(shape))


def cost(flops, moved):
    return pl.CostEstimate(flops=flops, bytes_accessed=moved, transcendentals=0)


FLOPS = 2 * POS * 27 * CHAN * CHAN
TAPS_SPEC = pl.BlockSpec((3 * WIDE, CHAN), lambda step: (step, 0))


def forward_conv(place, before, hidden, weights, act):
    return pl.pallas_call(
        forward_kernel,
        out_shape=jax.ShapeDtypeStruct((POS, CHAN), bf16),
        grid=(3,),
        in_specs=[
            SMEM_SPEC,
            whole(before.shape),
            whole(hidden.shape),
            TAPS_SPEC,
            whole(act.shape),
        ],
        out_specs=whole((POS, CHAN)),
        scratch_shapes=[
            pltpu.VMEM((SLOTS + 2, ROWS + 2, COLS, CHAN), bf16),
            pltpu.VMEM((POS, WIDE), f32),
        ],
        compiler_params=VMEM_LIMIT,
        cost_estimate=cost(FLOPS, 12 << 20),
        name="forward_conv",
    )(place, before, hidden, weights, act)


def backward_conv(place, cot, low, high, head, weights, act, mean, inv, gain, bias):
    smalls = [mean, inv, gain, bias]
    return pl.pallas_call(
        backward_kernel,
        out_shape=(
            jax.ShapeDtypeStruct((POS, CHAN), f32),
            jax.ShapeDtypeStruct((SLOTS, CHAN), f32),
            jax.ShapeDtypeStruct((SLOTS, CHAN), f32),
        ),
        grid=(3,),
        in_specs=[SMEM_SPEC]
        + [whole(v.shape) for v in (cot, low, high, head)]
        + [TAPS_SPEC, whole(act.shape)]
        + [whole(v.shape) for v in smalls],
        out_specs=(whole((POS, CHAN)), whole((SLOTS, CHAN)), whole((SLOTS, CHAN))),
        scratch_shapes=[
            pltpu.VMEM((SLOTS + 2, ROWS + 2, COLS, CHAN), bf16),
            pltpu.VMEM((POS, WIDE), f32),
        ],
        compiler_params=VMEM_LIMIT,
        cost_estimate=cost(FLOPS, 12 << 20),
        name="backward_conv",
    )(place, cot, low, high, head, weights, act, *smalls)


def local_sums(act):
    return pl.pallas_call(
        sums_kernel,
        out_shape=jax.ShapeDtypeStruct((8, 2 * SLOTS, CHAN), f32),
        compiler_params=VMEM_LIMIT,
        cost_estimate=cost(4 * POS * CHAN, 1 << 20),
        name="local_sums",
    )(act)


SMEM_SPEC = pl.BlockSpec(memory_space=pltpu.SMEM)


def same_group():
    group = np.arange(CHAN) // (CHAN // GROUPS)
    return jnp.asarray((group[:, None] == group[None, :]).astype(np.float32))


def frames_spec(*rest, first=0, count=4, last=1):
    return pl.BlockSpec(
        (count,) + rest,
        lambda step: (first // count + jnp.minimum(step, last),) + (0,) * len(rest),
    )


def make_hidden(place, peers, act, cot, low, high, gain, bias):
    wide = (ROWS + 2, COLS, CHAN)
    return pl.pallas_call(
        hidden_kernel,
        out_shape=(
            jax.ShapeDtypeStruct((SLOTS,) + wide, bf16),
            jax.ShapeDtypeStruct((2,) + wide, bf16),
            jax.ShapeDtypeStruct((2,) + wide, bf16),
            jax.ShapeDtypeStruct((SLOTS, CHAN), f32),
            jax.ShapeDtypeStruct((SLOTS, CHAN), f32),
        ),
        grid=(2,),
        in_specs=[
            SMEM_SPEC,
            whole(peers.shape),
            whole((CHAN, CHAN)),
            frames_spec(ROWS, COLS, CHAN),
            frames_spec(1, COLS, CHAN),
            frames_spec(1, COLS, CHAN),
            frames_spec(ROWS, COLS, CHAN, count=2, last=0),
            frames_spec(1, COLS, CHAN, first=SLOTS, count=2, last=0),
            frames_spec(1, COLS, CHAN, first=SLOTS, count=2, last=0),
            whole((1, CHAN)),
            whole((1, CHAN)),
        ],
        out_specs=(
            frames_spec(*wide),
            whole((2,) + wide),
            whole((2,) + wide),
            whole((SLOTS, CHAN)),
            whole((SLOTS, CHAN)),
        ),
        compiler_params=VMEM_LIMIT,
        cost_estimate=cost(40 * POS * CHAN, 5 << 20),
        name="make_hidden",
    )(place, peers, same_group(), act, low, high, cot, low, high, gain, bias)


def weight_terms(place, hidden, other, even, odd, cot, other_cot):
    in_vmem = pl.BlockSpec(memory_space=pltpu.VMEM)
    pair = (2, ROWS + 2, COLS, CHAN)
    return pl.pallas_call(
        weight_kernel,
        out_shape=(
            jax.ShapeDtypeStruct((CHIPS, 3 * PIECE, LANES), bf16),
            jax.ShapeDtypeStruct(pair, bf16),
        ),
        in_specs=[SMEM_SPEC] + [in_vmem] * 6,
        out_specs=(pl.BlockSpec(memory_space=pl.ANY), in_vmem),
        scratch_shapes=[
            pltpu.VMEM(pair, bf16),
            pltpu.VMEM((WIDE, 2 * (SLOTS + 2) * CELLS), bf16),
            pltpu.VMEM((2 * POS, 3 * TILE), bf16),
            pltpu.VMEM((9 * WIDE, TILE), f32),
            pltpu.VMEM((CHIPS, 3 * PIECE, LANES), bf16),
            pltpu.SemaphoreType.DMA((3,)),
        ],
        compiler_params=VMEM_LIMIT,
        cost_estimate=cost(FLOPS, 12 << 20),
        name="weight_terms",
    )(place, hidden, other, even, odd, cot, other_cot)


def shift(values, axes, count, step):
    pairs = [(i, i + step) for i in range(count) if 0 <= i + step < count]
    return lax.ppermute(values, axes, pairs)


def swap_cores(values):
    return lax.ppermute(values, "core", [(0, 1), (1, 0)])


def edge_rows(block):
    low = shift(block[:, ROWS - 1 :], ROW_AXES, 8, 1)
    high = shift(block[:, :1], ROW_AXES, 8, -1)
    return low, high


def per_group(first, second):
    grouped = jnp.concatenate([first, second], axis=0).reshape(2 * SLOTS, GROUPS, CHAN // GROUPS)
    return jnp.sum(grouped, axis=2)


def per_channel(grouped):
    return jnp.repeat(grouped, CHAN // GROUPS, axis=1)


def on_device(activations, frame_counts, norm_gain, norm_bias, conv_weight, cotangent):
    core = lax.axis_index("core")
    act = activations.reshape(POS, CHAN)
    gain, bias = norm_gain[None], norm_bias[None]

    sums = local_sums(activations)
    peers = lax.all_to_all(sums, ROW_AXES, 0, 0)
    source, rows_at_once, _ = lax.optimization_barrier((activations, cotangent, sums))
    low, high = edge_rows(jnp.concatenate([source, rows_at_once], 0))
    other_cot = swap_cores(rows_at_once)
    low, high, peers, other_cot = lax.optimization_barrier((low, high, peers, other_cot))

    tm = lax.axis_index(TM)
    count = frame_counts[tm]
    place = jnp.stack(
        [count, core, lax.axis_index(ROW_AXES), frame_counts[tm + 1 - 2 * core]]
    )
    wide_hidden, last_pair, head, mean, inv = make_hidden(
        place, peers, activations, cotangent, low, high, gain, bias
    )
    other_hidden = swap_cores(wide_hidden)
    even = lax.ppermute(last_pair, TM, [(i, i + 1) for i in range(1, 15, 2)])
    odd = lax.ppermute(last_pair, TM, [(i, i + 2) for i in range(1, 15, 2)])

    head = shift(head, TM, 16, -1)

    terms, before = weight_terms(
        place, wide_hidden, other_hidden, even, odd, cotangent, other_cot
    )
    terms, head = lax.optimization_barrier((terms, head))
    arrived = lax.all_to_all(terms, CHIP_AXES, 0, 0)

    low, high, _ = lax.optimization_barrier((low, high, terms))
    pre_grad, first_grad, second_grad = backward_conv(
        place, cotangent, low, high, head, conv_weight, act, mean, inv, gain, bias
    )
    sums = per_group(first_grad, second_grad)
    parts = [lax.ppermute(sums, "x", [(i, (i + k) % 4) for i in range(4)]) for k in range(1, 4)]

    block_out = forward_conv(place, before, wide_hidden, conv_weight, act)
    block_out, parts = lax.optimization_barrier((block_out, parts))
    block_out = block_out.reshape(activations.shape)
    sums = sums + parts[0] + parts[1] + parts[2]
    other = lax.ppermute(sums, "yhi", [(0, 1), (1, 0)])
    other, arrived = lax.optimization_barrier((other, arrived))
    total = jnp.sum(arrived.astype(f32), axis=0)
    sums = sums + other
    averages = per_channel(sums / CELL_COUNT)[:, None, None, :]
    first_avg, second_avg = averages[:SLOTS], averages[SLOTS:]
    wide_inv = inv[:, None, None, :]
    centred = (activations.astype(f32) - mean[:, None, None, :]) * wide_inv
    norm_part = wide_inv * (
        pre_grad.reshape(activations.shape) - first_avg - centred * second_avg
    )
    live = (jnp.arange(SLOTS) < count)[:, None, None, None]
    input_grad = jnp.where(live, cotangent.astype(f32) + norm_part, 0.0)

    frame_total = 1 + 4 * ((16 - 1) * 3 // 2)
    grad_scale = 1.0 / math.sqrt(frame_total * 8 * ROWS * COLS)
    total = total * grad_scale
    shared = total[2 * PIECE :]
    parts = [
        jnp.concatenate(
            [total[k * PIECE : (k + 1) * PIECE], shared[:, k * 64 : (k + 1) * 64]], axis=1
        )
        for k in range(2)
    ]
    mine = jnp.where(core == 0, parts[0], parts[1])
    theirs = swap_cores(jnp.where(core == 0, parts[1], parts[0]))
    first = jnp.where(core == 0, mine, theirs)
    second = jnp.where(core == 0, theirs, mine)
    weight_grad = jnp.concatenate([first, second[:, LANES:], second[:, :LANES]], axis=1)
    return block_out, input_grad, weight_grad


def solution(mesh):
    fine = Mesh(mesh.devices.reshape(2, 4, 2, 2, 4), ALL_AXES)
    placed = P(TM, ROW_AXES, None, None)
    return jax.shard_map(
        on_device,
        mesh=fine,
        in_specs=(placed, P(), P(), P(), P(), placed),
        out_specs=(placed, placed, P(ALL_AXES, None)),
        check_vma=False,
    )
```

```python
import math

import jax
import jax.numpy as jnp
import numpy as np
from jax import lax
from jax.experimental import pallas as pl
from jax.experimental.pallas import tpu as pltpu
from jax.sharding import Mesh
from jax.sharding import PartitionSpec as P

GROUPS = 32
EPS = 1e-05
CHAN = 384
HALF = CHAN // 2
SLOTS = 8
ROWS = 4
COLS = 32
CELLS = ROWS * COLS
POS = SLOTS * CELLS
WIDE = 3 * CHAN
PIECE = 81
CHIPS = 64
LANES = 128
WIDE_CELLS = (ROWS + 2) * COLS
CELL_COUNT = 8 * CELLS * (CHAN // GROUPS)
TILE = 256

TM = ("ylo", "z", "core")
ROW_AXES = ("yhi", "x")
CHIP_AXES = ("ylo", "z", "yhi", "x")
ALL_AXES = TM + ROW_AXES

bf16 = jnp.bfloat16
f32 = jnp.float32
VMEM_LIMIT = pltpu.CompilerParams(vmem_limit_bytes=64 * 1024 * 1024)


def from_left(values):
    col = lax.broadcasted_iota(jnp.int32, values.shape, 0) % COLS
    return jnp.where(col == 0, 0.0, pltpu.roll(values, 1, 0))


def from_right(values):
    col = lax.broadcasted_iota(jnp.int32, values.shape, 0) % COLS
    return jnp.where(col == COLS - 1, 0.0, pltpu.roll(values, values.shape[0] - 1, 0))


def tap_products(x_ref, w_ref, acc, back):
    step = pl.program_id(0)
    weights = w_ref[...]
    pieces = []
    for b in range(3):
        at = (2 - step, 2 - b) if back else (step, b)
        pieces.append(x_ref[pl.ds(at[0], SLOTS), pl.ds(at[1], ROWS)].reshape(POS, CHAN))
    left = jnp.concatenate(pieces, axis=1)
    if back:
        right = jnp.concatenate([weights[b * WIDE : (b + 1) * WIDE] for b in range(3)], axis=1)
        dims = (((1,), (1,)), ((), ()))
    else:
        right = jnp.concatenate(
            [
                jnp.concatenate(
                    [weights[(b * 3 + c) * CHAN : (b * 3 + c + 1) * CHAN] for c in range(3)], axis=1
                )
                for b in range(3)
            ],
            axis=0,
        )
        dims = (((1,), (0,)), ((), ()))
    product = lax.dot_general(left, right, dims, preferred_element_type=f32)

    @pl.when(step == 0)
    def _():
        acc[...] = product

    @pl.when(step > 0)
    def _():
        acc[...] += product


def forward_kernel(place_ref, before_ref, hidden_ref, w_ref, act_ref, out_ref, x, acc):
    @pl.when(pl.program_id(0) == 0)
    def _():
        x[:2] = before_ref[...]
        x[2:] = hidden_ref[...]

    tap_products(x, w_ref, acc, False)

    @pl.when(pl.program_id(0) == 2)
    def _():
        for frame in range(SLOTS):
            rows = slice(frame * CELLS, (frame + 1) * CELLS)
            conv = (
                acc[rows, CHAN : 2 * CHAN]
                + from_left(acc[rows, :CHAN])
                + from_right(acc[rows, 2 * CHAN :])
            )
            total = act_ref[rows].astype(f32) + conv
            out_ref[rows] = jnp.where(frame < place_ref[0], total, 0.0).astype(bf16)


def backward_kernel(
    place_ref,
    cot_ref,
    low_ref,
    high_ref,
    head_ref,
    w_ref,
    act_ref,
    mean_ref,
    inv_ref,
    gain_ref,
    bias_ref,
    out_ref,
    first_ref,
    second_ref,
    x,
    acc,
):
    @pl.when(pl.program_id(0) == 0)
    def _():
        count = place_ref[0]
        for frame in range(SLOTS):

            @pl.when(frame < count)
            def _(frame=frame):
                x[frame, 0] = low_ref[SLOTS + frame, 0]
                x[frame, 1 : 1 + ROWS] = cot_ref[frame]
                x[frame, 1 + ROWS] = high_ref[SLOTS + frame, 0]

            @pl.when(frame >= count)
            def _(frame=frame):
                x[frame] = jnp.zeros((ROWS + 2, COLS, CHAN), bf16)

        x[SLOTS:] = jnp.zeros((2, ROWS + 2, COLS, CHAN), bf16)
        x[pl.ds(count, 2)] = head_ref[...]

    tap_products(x, w_ref, acc, True)

    @pl.when(pl.program_id(0) == 2)
    def _():
        gain = gain_ref[...]
        bias = bias_ref[...]
        for frame in range(SLOTS):
            rows = slice(frame * CELLS, (frame + 1) * CELLS)
            grad = (
                acc[rows, CHAN : 2 * CHAN]
                + from_right(acc[rows, :CHAN])
                + from_left(acc[rows, 2 * CHAN :])
            )
            centred = (act_ref[rows].astype(f32) - mean_ref[frame : frame + 1]) * inv_ref[
                frame : frame + 1
            ]
            pre_act = centred * gain + bias
            gate = jax.nn.sigmoid(pre_act)
            pre_grad = grad * gate * (1.0 + pre_act * (1.0 - gate)) * gain
            out_ref[rows] = pre_grad
            first_ref[frame : frame + 1] = jnp.sum(pre_grad, axis=0, keepdims=True)
            second_ref[frame : frame + 1] = jnp.sum(pre_grad * centred, axis=0, keepdims=True)


READY = ((0, 2), (2, 5), (5, 8))


def weight_kernel(
    place_ref,
    hidden_ref,
    other_ref,
    even_ref,
    odd_ref,
    cot_ref,
    other_cot_ref,
    out_ref,
    before_ref,
    other_before,
    turned,
    right,
    sums,
    packed,
    sems,
):
    core = place_ref[1]

    def last_two(ref, count, to_ref):
        @pl.when(count >= 2)
        def _():
            to_ref[...] = ref[pl.ds(jnp.maximum(count - 2, 0), 2)]

        @pl.when(count < 2)
        def _():
            to_ref[0] = jnp.zeros((ROWS + 2, COLS, CHAN), bf16)
            to_ref[1] = ref[0]

    @pl.when(core == 0)
    def _():
        before_ref[...] = even_ref[...]
        last_two(hidden_ref, place_ref[0], other_before)

    @pl.when(core == 1)
    def _():
        other_before[...] = odd_ref[...]
        last_two(other_ref, place_ref[3], before_ref)

    def turn(ref, f, column):
        for b in range(3):
            values = ref[f, b : b + ROWS].reshape(CELLS, CHAN)
            turned[b * CHAN : (b + 1) * CHAN, pl.ds(pl.multiple_of(column, CELLS), CELLS)] = values.T

    for block, (early, late) in enumerate(((before_ref, hidden_ref), (other_before, other_ref))):
        base = block * (SLOTS + 2) * CELLS
        for f in range(2):
            turn(early, f, base + f * CELLS)

        def turn_late(f, carry, late=late, base=base):
            turn(late, f, base + (f + 2) * CELLS)
            return carry

        lax.fori_loop(0, SLOTS, turn_late, 0, unroll=True)

    left_lanes = lax.broadcasted_iota(jnp.int32, (CELLS, LANES), 1) < LANES // 2

    def move(f, carry):
        for block, ref in enumerate((cot_ref, other_cot_ref)):
            values = ref[f].reshape(CELLS, CHAN).astype(f32)
            values = jnp.where(f < place_ref[3 * block], values, 0.0)
            middle = values[:, LANES : 2 * LANES]
            swapped = pltpu.roll(middle, LANES // 2, 1)
            first = core == 0
            outer = jnp.where(first, values[:, :LANES], values[:, 2 * LANES :])
            inner = jnp.where(left_lanes == first, middle, swapped)
            chosen = jnp.concatenate([outer, inner], axis=1)
            rows = pl.ds(pl.multiple_of(block * POS + f * CELLS, CELLS), CELLS)
            for c, moved in enumerate((from_right(chosen), chosen, from_left(chosen))):
                right[rows, c * TILE : (c + 1) * TILE] = moved.astype(bf16)
        return carry

    lax.fori_loop(0, SLOTS, move, 0, unroll=True)

    upper = lax.broadcasted_iota(jnp.int32, (PIECE, LANES), 1) >= LANES // 2
    copies = []
    for a in range(3):
        window = jnp.concatenate(
            [
                turned[:, start : start + POS]
                for block in range(2)
                for start in [(block * (SLOTS + 2) + a) * CELLS]
            ],
            axis=1,
        )
        product = jnp.dot(window, right[...], preferred_element_type=f32)
        for b in range(3):
            for c in range(3):
                at = ((a * 3 + b) * 3 + c) * CHAN
                sums[at : at + CHAN] = product[
                    b * CHAN : (b + 1) * CHAN, c * TILE : (c + 1) * TILE
                ]
        for chip in range(8 * READY[a][0], 8 * READY[a][1]):
            start = 1296 * (chip // 8) + PIECE * (chip % 8)
            first, second = sums[start : start + PIECE], sums[start + 648 : start + 648 + PIECE]
            block = jnp.concatenate(
                [
                    first[:, :LANES],
                    second[:, :LANES],
                    jnp.where(upper, second[:, LANES:], first[:, LANES:]),
                ],
                axis=0,
            )
            packed[chip] = block.astype(bf16)
        chips = pl.ds(8 * READY[a][0], 8 * (READY[a][1] - READY[a][0]))
        copies.append(pltpu.make_async_copy(packed.at[chips], out_ref.at[chips], sems.at[a]))
        copies[-1].start()
    for copy in copies:
        copy.wait()


def sums_kernel(act_ref, cot_ref, out_ref, bottom_ref, top_ref):
    firsts, seconds = [], []
    for frame in range(SLOTS):
        values = act_ref[frame].reshape(CELLS, CHAN).astype(f32)
        firsts.append(jnp.sum(values, axis=0, keepdims=True))
        seconds.append(jnp.sum(values * values, axis=0, keepdims=True))
    both = jnp.concatenate(firsts + seconds, axis=0)
    for peer in range(8):
        out_ref[peer] = both
    for first, ref in ((0, act_ref), (SLOTS, cot_ref)):
        bottom_ref[first : first + SLOTS] = ref[:, ROWS - 1 :]
        top_ref[first : first + SLOTS] = ref[:, :1]


def group_means(sums, same_ref):
    return jnp.dot(
        sums, same_ref[...], precision=lax.Precision.HIGHEST, preferred_element_type=f32
    ) * (1.0 / CELL_COUNT)


def hidden_kernel(
    place_ref,
    peers_ref,
    same_ref,
    act_ref,
    low_ref,
    high_ref,
    cot_ref,
    cot_low_ref,
    cot_high_ref,
    gain_ref,
    bias_ref,
    hidden_ref,
    pair_ref,
    head_ref,
    mean_ref,
    inv_ref,
):
    step = pl.program_id(0)
    count, row_place = place_ref[0], place_ref[2]

    @pl.when(step == 0)
    def _():
        total = peers_ref[0]
        for peer in range(1, 8):
            total = total + peers_ref[peer]
        stats = group_means(total, same_ref)
        mean_ref[...] = stats[:SLOTS]
        inv_ref[...] = lax.rsqrt(stats[SLOTS:] - stats[:SLOTS] * stats[:SLOTS] + EPS)
        pair_ref[0] = jnp.zeros((ROWS + 2, COLS, CHAN), bf16)
        head_ref[:, :1] = cot_low_ref[...]
        head_ref[:, 1 : 1 + ROWS] = cot_ref[...]
        head_ref[:, 1 + ROWS :] = cot_high_ref[...]

    gain = gain_ref[...]
    bias = bias_ref[...]
    for k in range(4):
        frame = step * 4 + k
        live = frame < count
        mean = mean_ref[pl.ds(frame, 1)]
        inv = inv_ref[pl.ds(frame, 1)]

        def activated(values, keep, mean=mean, inv=inv):
            pre_act = (values.astype(f32) - mean) * inv * gain + bias
            return jnp.where(keep, pre_act * jax.nn.sigmoid(pre_act), 0.0).astype(bf16)

        hidden = activated(act_ref[k].reshape(CELLS, CHAN), live)
        hidden_ref[k, 1 : 1 + ROWS] = hidden.reshape(ROWS, COLS, CHAN)
        hidden_ref[k, 0] = activated(low_ref[k, 0], live & (row_place > 0))
        hidden_ref[k, 1 + ROWS] = activated(high_ref[k, 0], live & (row_place < 7))
        for late in range(2):

            @pl.when(frame == count - 2 + late)
            def _(k=k, late=late):
                pair_ref[late] = hidden_ref[k]


def whole(shape):
    return pl.BlockSpec(shape, lambda step: (0,) * len(shape))


def cost(flops, moved):
    return pl.CostEstimate(flops=flops, bytes_accessed=moved, transcendentals=0)


FLOPS = 2 * POS * 27 * CHAN * CHAN
TAPS_SPEC = pl.BlockSpec((3 * WIDE, CHAN), lambda step: (step, 0))


def forward_conv(place, before, hidden, weights, act):
    return pl.pallas_call(
        forward_kernel,
        out_shape=jax.ShapeDtypeStruct((POS, CHAN), bf16),
        grid=(3,),
        in_specs=[
            SMEM_SPEC,
            whole(before.shape),
            whole(hidden.shape),
            TAPS_SPEC,
            whole(act.shape),
        ],
        out_specs=whole((POS, CHAN)),
        scratch_shapes=[
            pltpu.VMEM((SLOTS + 2, ROWS + 2, COLS, CHAN), bf16),
            pltpu.VMEM((POS, WIDE), f32),
        ],
        compiler_params=VMEM_LIMIT,
        cost_estimate=cost(FLOPS, 12 << 20),
        name="forward_conv",
    )(place, before, hidden, weights, act)


def backward_conv(place, cot, low, high, head, weights, act, mean, inv, gain, bias):
    smalls = [mean, inv, gain, bias]
    return pl.pallas_call(
        backward_kernel,
        out_shape=(
            jax.ShapeDtypeStruct((POS, CHAN), f32),
            jax.ShapeDtypeStruct((SLOTS, CHAN), f32),
            jax.ShapeDtypeStruct((SLOTS, CHAN), f32),
        ),
        grid=(3,),
        in_specs=[SMEM_SPEC]
        + [whole(v.shape) for v in (cot, low, high, head)]
        + [TAPS_SPEC, whole(act.shape)]
        + [whole(v.shape) for v in smalls],
        out_specs=(whole((POS, CHAN)), whole((SLOTS, CHAN)), whole((SLOTS, CHAN))),
        scratch_shapes=[
            pltpu.VMEM((SLOTS + 2, ROWS + 2, COLS, CHAN), bf16),
            pltpu.VMEM((POS, WIDE), f32),
        ],
        compiler_params=VMEM_LIMIT,
        cost_estimate=cost(FLOPS, 12 << 20),
        name="backward_conv",
    )(place, cot, low, high, head, weights, act, *smalls)


def local_sums(act, cot):
    edge = jax.ShapeDtypeStruct((2 * SLOTS, 1, COLS, CHAN), bf16)
    return pl.pallas_call(
        sums_kernel,
        out_shape=(jax.ShapeDtypeStruct((8, 2 * SLOTS, CHAN), f32), edge, edge),
        compiler_params=VMEM_LIMIT,
        cost_estimate=cost(4 * POS * CHAN, 3 << 20),
        name="local_sums",
    )(act, cot)


SMEM_SPEC = pl.BlockSpec(memory_space=pltpu.SMEM)


def same_group():
    group = np.arange(CHAN) // (CHAN // GROUPS)
    return jnp.asarray((group[:, None] == group[None, :]).astype(np.float32))


def frames_spec(*rest, first=0, count=4, last=1):
    return pl.BlockSpec(
        (count,) + rest,
        lambda step: (first // count + jnp.minimum(step, last),) + (0,) * len(rest),
    )


def make_hidden(place, peers, act, cot, low, high, gain, bias):
    wide = (ROWS + 2, COLS, CHAN)
    return pl.pallas_call(
        hidden_kernel,
        out_shape=(
            jax.ShapeDtypeStruct((SLOTS,) + wide, bf16),
            jax.ShapeDtypeStruct((2,) + wide, bf16),
            jax.ShapeDtypeStruct((2,) + wide, bf16),
            jax.ShapeDtypeStruct((SLOTS, CHAN), f32),
            jax.ShapeDtypeStruct((SLOTS, CHAN), f32),
        ),
        grid=(2,),
        in_specs=[
            SMEM_SPEC,
            whole(peers.shape),
            whole((CHAN, CHAN)),
            frames_spec(ROWS, COLS, CHAN),
            frames_spec(1, COLS, CHAN),
            frames_spec(1, COLS, CHAN),
            frames_spec(ROWS, COLS, CHAN, count=2, last=0),
            frames_spec(1, COLS, CHAN, first=SLOTS, count=2, last=0),
            frames_spec(1, COLS, CHAN, first=SLOTS, count=2, last=0),
            whole((1, CHAN)),
            whole((1, CHAN)),
        ],
        out_specs=(
            frames_spec(*wide),
            whole((2,) + wide),
            whole((2,) + wide),
            whole((SLOTS, CHAN)),
            whole((SLOTS, CHAN)),
        ),
        compiler_params=VMEM_LIMIT,
        cost_estimate=cost(40 * POS * CHAN, 5 << 20),
        name="make_hidden",
    )(place, peers, same_group(), act, low, high, cot, low, high, gain, bias)


def weight_terms(place, hidden, other, even, odd, cot, other_cot):
    in_vmem = pl.BlockSpec(memory_space=pltpu.VMEM)
    pair = (2, ROWS + 2, COLS, CHAN)
    return pl.pallas_call(
        weight_kernel,
        out_shape=(
            jax.ShapeDtypeStruct((CHIPS, 3 * PIECE, LANES), bf16),
            jax.ShapeDtypeStruct(pair, bf16),
        ),
        in_specs=[SMEM_SPEC] + [in_vmem] * 6,
        out_specs=(pl.BlockSpec(memory_space=pl.ANY), in_vmem),
        scratch_shapes=[
            pltpu.VMEM(pair, bf16),
            pltpu.VMEM((WIDE, 2 * (SLOTS + 2) * CELLS), bf16),
            pltpu.VMEM((2 * POS, 3 * TILE), bf16),
            pltpu.VMEM((9 * WIDE, TILE), f32),
            pltpu.VMEM((CHIPS, 3 * PIECE, LANES), bf16),
            pltpu.SemaphoreType.DMA((3,)),
        ],
        compiler_params=VMEM_LIMIT,
        cost_estimate=cost(FLOPS, 12 << 20),
        name="weight_terms",
    )(place, hidden, other, even, odd, cot, other_cot)


def shift(values, axes, count, step):
    pairs = [(i, i + step) for i in range(count) if 0 <= i + step < count]
    return lax.ppermute(values, axes, pairs)


def swap_cores(values):
    return lax.ppermute(values, "core", [(0, 1), (1, 0)])


def per_group(first, second):
    grouped = jnp.concatenate([first, second], axis=0).reshape(2 * SLOTS, GROUPS, CHAN // GROUPS)
    return jnp.sum(grouped, axis=2)


def per_channel(grouped):
    return jnp.repeat(grouped, CHAN // GROUPS, axis=1)


def on_device(activations, frame_counts, norm_gain, norm_bias, conv_weight, cotangent):
    core = lax.axis_index("core")
    act = activations.reshape(POS, CHAN)
    gain, bias = norm_gain[None], norm_bias[None]

    sums, bottom, top = local_sums(activations, cotangent)
    peers = lax.all_to_all(sums, ROW_AXES, 0, 0)
    low = shift(bottom, ROW_AXES, 8, 1)
    high = shift(top, ROW_AXES, 8, -1)
    other_cot = swap_cores(cotangent)
    low, high, peers, other_cot = lax.optimization_barrier((low, high, peers, other_cot))

    tm = lax.axis_index(TM)
    count = frame_counts[tm]
    place = jnp.stack(
        [count, core, lax.axis_index(ROW_AXES), frame_counts[tm + 1 - 2 * core]]
    )
    wide_hidden, last_pair, head, mean, inv = make_hidden(
        place, peers, activations, cotangent, low, high, gain, bias
    )
    other_hidden = swap_cores(wide_hidden)
    even = lax.ppermute(last_pair, TM, [(i, i + 1) for i in range(1, 15, 2)])
    odd = lax.ppermute(last_pair, TM, [(i, i + 2) for i in range(1, 15, 2)])

    head = shift(head, TM, 16, -1)

    terms, before = weight_terms(
        place, wide_hidden, other_hidden, even, odd, cotangent, other_cot
    )
    terms, head = lax.optimization_barrier((terms, head))
    arrived = lax.all_to_all(terms, CHIP_AXES, 0, 0)

    low, high, _ = lax.optimization_barrier((low, high, terms))
    pre_grad, first_grad, second_grad = backward_conv(
        place, cotangent, low, high, head, conv_weight, act, mean, inv, gain, bias
    )
    sums = per_group(first_grad, second_grad)
    parts = [lax.ppermute(sums, "x", [(i, (i + k) % 4) for i in range(4)]) for k in range(1, 4)]

    block_out = forward_conv(place, before, wide_hidden, conv_weight, act)
    block_out, parts = lax.optimization_barrier((block_out, parts))
    block_out = block_out.reshape(activations.shape)
    sums = sums + parts[0] + parts[1] + parts[2]
    other = lax.ppermute(sums, "yhi", [(0, 1), (1, 0)])
    other, arrived = lax.optimization_barrier((other, arrived))
    total = jnp.sum(arrived.astype(f32), axis=0)
    sums = sums + other
    averages = per_channel(sums / CELL_COUNT)[:, None, None, :]
    first_avg, second_avg = averages[:SLOTS], averages[SLOTS:]
    wide_inv = inv[:, None, None, :]
    centred = (activations.astype(f32) - mean[:, None, None, :]) * wide_inv
    norm_part = wide_inv * (
        pre_grad.reshape(activations.shape) - first_avg - centred * second_avg
    )
    live = (jnp.arange(SLOTS) < count)[:, None, None, None]
    input_grad = jnp.where(live, cotangent.astype(f32) + norm_part, 0.0)

    frame_total = 1 + 4 * ((16 - 1) * 3 // 2)
    grad_scale = 1.0 / math.sqrt(frame_total * 8 * ROWS * COLS)
    total = total * grad_scale
    shared = total[2 * PIECE :]
    parts = [
        jnp.concatenate(
            [total[k * PIECE : (k + 1) * PIECE], shared[:, k * 64 : (k + 1) * 64]], axis=1
        )
        for k in range(2)
    ]
    mine = jnp.where(core == 0, parts[0], parts[1])
    theirs = swap_cores(jnp.where(core == 0, parts[1], parts[0]))
    first = jnp.where(core == 0, mine, theirs)
    second = jnp.where(core == 0, theirs, mine)
    weight_grad = jnp.concatenate([first, second[:, LANES:], second[:, :LANES]], axis=1)
    return block_out, input_grad, weight_grad


def solution(mesh):
    fine = Mesh(mesh.devices.reshape(2, 4, 2, 2, 4), ALL_AXES)
    placed = P(TM, ROW_AXES, None, None)
    return jax.shard_map(
        on_device,
        mesh=fine,
        in_specs=(placed, P(), P(), P(), P(), placed),
        out_specs=(placed, placed, P(ALL_AXES, None)),
        check_vma=False,
    )
```

```python
import math

import jax
import jax.numpy as jnp
import numpy as np
from jax import lax
from jax.experimental import pallas as pl
from jax.experimental.pallas import tpu as pltpu
from jax.sharding import Mesh
from jax.sharding import PartitionSpec as P

GROUPS = 32
EPS = 1e-05
CHAN = 384
HALF = CHAN // 2
SLOTS = 8
ROWS = 4
COLS = 32
CELLS = ROWS * COLS
POS = SLOTS * CELLS
WIDE = 3 * CHAN
PIECE = 81
CHIPS = 64
LANES = 128
WIDE_CELLS = (ROWS + 2) * COLS
CELL_COUNT = 8 * CELLS * (CHAN // GROUPS)
TILE = 256

TM = ("ylo", "z", "core")
ROW_AXES = ("yhi", "x")
CHIP_AXES = ("ylo", "z", "yhi", "x")
ALL_AXES = TM + ROW_AXES

bf16 = jnp.bfloat16
f32 = jnp.float32
VMEM_LIMIT = pltpu.CompilerParams(vmem_limit_bytes=64 * 1024 * 1024)


def from_left(values):
    col = lax.broadcasted_iota(jnp.int32, values.shape, 0) % COLS
    return jnp.where(col == 0, 0.0, pltpu.roll(values, 1, 0))


def from_right(values):
    col = lax.broadcasted_iota(jnp.int32, values.shape, 0) % COLS
    return jnp.where(col == COLS - 1, 0.0, pltpu.roll(values, values.shape[0] - 1, 0))


def tap_products(x_ref, w_ref, acc, back):
    step = pl.program_id(0)
    weights = w_ref[...]
    pieces = []
    for b in range(3):
        at = (2 - step, 2 - b) if back else (step, b)
        pieces.append(x_ref[pl.ds(at[0], SLOTS), pl.ds(at[1], ROWS)].reshape(POS, CHAN))
    left = jnp.concatenate(pieces, axis=1)
    if back:
        right = jnp.concatenate([weights[b * WIDE : (b + 1) * WIDE] for b in range(3)], axis=1)
        dims = (((1,), (1,)), ((), ()))
    else:
        right = jnp.concatenate(
            [
                jnp.concatenate(
                    [weights[(b * 3 + c) * CHAN : (b * 3 + c + 1) * CHAN] for c in range(3)], axis=1
                )
                for b in range(3)
            ],
            axis=0,
        )
        dims = (((1,), (0,)), ((), ()))
    product = lax.dot_general(left, right, dims, preferred_element_type=f32)

    @pl.when(step == 0)
    def _():
        acc[...] = product

    @pl.when(step > 0)
    def _():
        acc[...] += product


def forward_kernel(place_ref, before_ref, hidden_ref, w_ref, act_ref, out_ref, x, acc):
    @pl.when(pl.program_id(0) == 0)
    def _():
        x[:2] = before_ref[...]
        x[2:] = hidden_ref[...]

    tap_products(x, w_ref, acc, False)

    @pl.when(pl.program_id(0) == 2)
    def _():
        for frame in range(SLOTS):
            rows = slice(frame * CELLS, (frame + 1) * CELLS)
            conv = (
                acc[rows, CHAN : 2 * CHAN]
                + from_left(acc[rows, :CHAN])
                + from_right(acc[rows, 2 * CHAN :])
            )
            total = act_ref[rows].astype(f32) + conv
            out_ref[rows] = jnp.where(frame < place_ref[0], total, 0.0).astype(bf16)


def backward_kernel(
    place_ref,
    cot_ref,
    low_ref,
    high_ref,
    head_ref,
    w_ref,
    act_ref,
    mean_ref,
    inv_ref,
    gain_ref,
    bias_ref,
    out_ref,
    first_ref,
    second_ref,
    x,
    acc,
):
    @pl.when(pl.program_id(0) == 0)
    def _():
        count = place_ref[0]
        for frame in range(SLOTS):

            @pl.when(frame < count)
            def _(frame=frame):
                x[frame, 0] = low_ref[SLOTS + frame, 0]
                x[frame, 1 : 1 + ROWS] = cot_ref[frame]
                x[frame, 1 + ROWS] = high_ref[SLOTS + frame, 0]

            @pl.when(frame >= count)
            def _(frame=frame):
                x[frame] = jnp.zeros((ROWS + 2, COLS, CHAN), bf16)

        x[SLOTS:] = jnp.zeros((2, ROWS + 2, COLS, CHAN), bf16)
        x[pl.ds(count, 2)] = head_ref[...]

    tap_products(x, w_ref, acc, True)

    @pl.when(pl.program_id(0) == 2)
    def _():
        gain = gain_ref[...]
        bias = bias_ref[...]
        for frame in range(SLOTS):
            rows = slice(frame * CELLS, (frame + 1) * CELLS)
            grad = (
                acc[rows, CHAN : 2 * CHAN]
                + from_right(acc[rows, :CHAN])
                + from_left(acc[rows, 2 * CHAN :])
            )
            centred = (act_ref[rows].astype(f32) - mean_ref[frame : frame + 1]) * inv_ref[
                frame : frame + 1
            ]
            pre_act = centred * gain + bias
            gate = jax.nn.sigmoid(pre_act)
            pre_grad = grad * gate * (1.0 + pre_act * (1.0 - gate)) * gain
            out_ref[rows] = pre_grad
            first_ref[frame : frame + 1] = jnp.sum(pre_grad, axis=0, keepdims=True)
            second_ref[frame : frame + 1] = jnp.sum(pre_grad * centred, axis=0, keepdims=True)


READY = ((0, 2), (2, 5), (5, 8))


def weight_kernel(
    place_ref,
    hidden_ref,
    other_ref,
    even_ref,
    odd_ref,
    cot_ref,
    other_cot_ref,
    out_ref,
    before_ref,
    other_before,
    turned,
    right,
    sums,
    packed,
    sems,
):
    core = place_ref[1]

    def last_two(ref, count, to_ref):
        @pl.when(count >= 2)
        def _():
            to_ref[...] = ref[pl.ds(jnp.maximum(count - 2, 0), 2)]

        @pl.when(count < 2)
        def _():
            to_ref[0] = jnp.zeros((ROWS + 2, COLS, CHAN), bf16)
            to_ref[1] = ref[0]

    @pl.when(core == 0)
    def _():
        before_ref[...] = even_ref[...]
        last_two(hidden_ref, place_ref[0], other_before)

    @pl.when(core == 1)
    def _():
        other_before[...] = odd_ref[...]
        last_two(other_ref, place_ref[3], before_ref)

    def turn(ref, f, column):
        for b in range(3):
            values = ref[f, b : b + ROWS].reshape(CELLS, CHAN)
            turned[b * CHAN : (b + 1) * CHAN, pl.ds(pl.multiple_of(column, CELLS), CELLS)] = values.T

    for block, (early, late) in enumerate(((before_ref, hidden_ref), (other_before, other_ref))):
        base = block * (SLOTS + 2) * CELLS
        for f in range(2):
            turn(early, f, base + f * CELLS)

        def turn_late(f, carry, late=late, base=base):
            turn(late, f, base + (f + 2) * CELLS)
            return carry

        lax.fori_loop(0, SLOTS, turn_late, 0, unroll=True)

    left_lanes = lax.broadcasted_iota(jnp.int32, (CELLS, LANES), 1) < LANES // 2

    def move(f, carry):
        for block, ref in enumerate((cot_ref, other_cot_ref)):
            values = ref[f].reshape(CELLS, CHAN).astype(f32)
            values = jnp.where(f < place_ref[3 * block], values, 0.0)
            middle = values[:, LANES : 2 * LANES]
            swapped = pltpu.roll(middle, LANES // 2, 1)
            first = core == 0
            outer = jnp.where(first, values[:, :LANES], values[:, 2 * LANES :])
            inner = jnp.where(left_lanes == first, middle, swapped)
            chosen = jnp.concatenate([outer, inner], axis=1)
            rows = pl.ds(pl.multiple_of(block * POS + f * CELLS, CELLS), CELLS)
            for c, moved in enumerate((from_right(chosen), chosen, from_left(chosen))):
                right[rows, c * TILE : (c + 1) * TILE] = moved.astype(bf16)
        return carry

    lax.fori_loop(0, SLOTS, move, 0, unroll=True)

    upper = lax.broadcasted_iota(jnp.int32, (PIECE, LANES), 1) >= LANES // 2
    copies = []
    for a in range(3):
        window = jnp.concatenate(
            [
                turned[:, start : start + POS]
                for block in range(2)
                for start in [(block * (SLOTS + 2) + a) * CELLS]
            ],
            axis=1,
        )
        product = jnp.dot(window, right[...], preferred_element_type=f32)
        for b in range(3):
            for c in range(3):
                at = ((a * 3 + b) * 3 + c) * CHAN
                sums[at : at + CHAN] = product[
                    b * CHAN : (b + 1) * CHAN, c * TILE : (c + 1) * TILE
                ]
        for chip in range(8 * READY[a][0], 8 * READY[a][1]):
            start = 1296 * (chip // 8) + PIECE * (chip % 8)
            first, second = sums[start : start + PIECE], sums[start + 648 : start + 648 + PIECE]
            block = jnp.concatenate(
                [
                    first[:, :LANES],
                    second[:, :LANES],
                    jnp.where(upper, second[:, LANES:], first[:, LANES:]),
                ],
                axis=0,
            )
            packed[chip] = block.astype(bf16)
        chips = pl.ds(8 * READY[a][0], 8 * (READY[a][1] - READY[a][0]))
        copies.append(pltpu.make_async_copy(packed.at[chips], out_ref.at[chips], sems.at[a]))
        copies[-1].start()
    for copy in copies:
        copy.wait()


def sums_kernel(act_ref, cot_ref, out_ref, bottom_ref, top_ref):
    firsts, seconds = [], []
    for frame in range(SLOTS):
        values = act_ref[frame].reshape(CELLS, CHAN).astype(f32)
        firsts.append(jnp.sum(values, axis=0, keepdims=True))
        seconds.append(jnp.sum(values * values, axis=0, keepdims=True))
    both = jnp.concatenate(firsts + seconds, axis=0)
    for peer in range(8):
        out_ref[peer] = both
    for first, ref in ((0, act_ref), (SLOTS, cot_ref)):
        bottom_ref[first : first + SLOTS] = ref[:, ROWS - 1 :]
        top_ref[first : first + SLOTS] = ref[:, :1]


def group_means(sums, same_ref):
    return jnp.dot(
        sums, same_ref[...], precision=lax.Precision.HIGHEST, preferred_element_type=f32
    ) * (1.0 / CELL_COUNT)


def hidden_kernel(
    place_ref,
    peers_ref,
    same_ref,
    act_ref,
    low_ref,
    high_ref,
    cot_ref,
    cot_low_ref,
    cot_high_ref,
    gain_ref,
    bias_ref,
    hidden_ref,
    pair_ref,
    head_ref,
    mean_ref,
    inv_ref,
):
    step = pl.program_id(0)
    count, row_place = place_ref[0], place_ref[2]

    @pl.when(step == 0)
    def _():
        total = peers_ref[0]
        for peer in range(1, 8):
            total = total + peers_ref[peer]
        stats = group_means(total, same_ref)
        mean_ref[...] = stats[:SLOTS]
        inv_ref[...] = lax.rsqrt(stats[SLOTS:] - stats[:SLOTS] * stats[:SLOTS] + EPS)
        pair_ref[0] = jnp.zeros((ROWS + 2, COLS, CHAN), bf16)
        head_ref[:, :1] = cot_low_ref[...]
        head_ref[:, 1 : 1 + ROWS] = cot_ref[...]
        head_ref[:, 1 + ROWS :] = cot_high_ref[...]

    gain = gain_ref[...]
    bias = bias_ref[...]
    for k in range(4):
        frame = step * 4 + k
        live = frame < count
        mean = mean_ref[pl.ds(frame, 1)]
        inv = inv_ref[pl.ds(frame, 1)]

        def activated(values, keep, mean=mean, inv=inv):
            pre_act = (values.astype(f32) - mean) * inv * gain + bias
            return jnp.where(keep, pre_act * jax.nn.sigmoid(pre_act), 0.0).astype(bf16)

        hidden = activated(act_ref[k].reshape(CELLS, CHAN), live)
        hidden_ref[k, 1 : 1 + ROWS] = hidden.reshape(ROWS, COLS, CHAN)
        hidden_ref[k, 0] = activated(low_ref[k, 0], live & (row_place > 0))
        hidden_ref[k, 1 + ROWS] = activated(high_ref[k, 0], live & (row_place < 7))
        for late in range(2):

            @pl.when(frame == count - 2 + late)
            def _(k=k, late=late):
                pair_ref[late] = hidden_ref[k]


def whole(shape):
    return pl.BlockSpec(shape, lambda step: (0,) * len(shape))


def cost(flops, moved):
    return pl.CostEstimate(flops=flops, bytes_accessed=moved, transcendentals=0)


FLOPS = 2 * POS * 27 * CHAN * CHAN
TAPS_SPEC = pl.BlockSpec((3 * WIDE, CHAN), lambda step: (step, 0))


def forward_conv(place, before, hidden, weights, act):
    return pl.pallas_call(
        forward_kernel,
        out_shape=jax.ShapeDtypeStruct((POS, CHAN), bf16),
        grid=(3,),
        in_specs=[
            SMEM_SPEC,
            whole(before.shape),
            whole(hidden.shape),
            TAPS_SPEC,
            whole(act.shape),
        ],
        out_specs=whole((POS, CHAN)),
        scratch_shapes=[
            pltpu.VMEM((SLOTS + 2, ROWS + 2, COLS, CHAN), bf16),
            pltpu.VMEM((POS, WIDE), f32),
        ],
        compiler_params=VMEM_LIMIT,
        cost_estimate=cost(FLOPS, 12 << 20),
        name="forward_conv",
    )(place, before, hidden, weights, act)


def backward_conv(place, cot, low, high, head, weights, act, mean, inv, gain, bias):
    smalls = [mean, inv, gain, bias]
    return pl.pallas_call(
        backward_kernel,
        out_shape=(
            jax.ShapeDtypeStruct((POS, CHAN), f32),
            jax.ShapeDtypeStruct((SLOTS, CHAN), f32),
            jax.ShapeDtypeStruct((SLOTS, CHAN), f32),
        ),
        grid=(3,),
        in_specs=[SMEM_SPEC]
        + [whole(v.shape) for v in (cot, low, high, head)]
        + [TAPS_SPEC, whole(act.shape)]
        + [whole(v.shape) for v in smalls],
        out_specs=(whole((POS, CHAN)), whole((SLOTS, CHAN)), whole((SLOTS, CHAN))),
        scratch_shapes=[
            pltpu.VMEM((SLOTS + 2, ROWS + 2, COLS, CHAN), bf16),
            pltpu.VMEM((POS, WIDE), f32),
        ],
        compiler_params=VMEM_LIMIT,
        cost_estimate=cost(FLOPS, 12 << 20),
        name="backward_conv",
    )(place, cot, low, high, head, weights, act, *smalls)


def local_sums(act, cot):
    edge = jax.ShapeDtypeStruct((2 * SLOTS, 1, COLS, CHAN), bf16)
    return pl.pallas_call(
        sums_kernel,
        out_shape=(jax.ShapeDtypeStruct((8, 2 * SLOTS, CHAN), f32), edge, edge),
        compiler_params=VMEM_LIMIT,
        cost_estimate=cost(4 * POS * CHAN, 3 << 20),
        name="local_sums",
    )(act, cot)


SMEM_SPEC = pl.BlockSpec(memory_space=pltpu.SMEM)


def same_group():
    group = np.arange(CHAN) // (CHAN // GROUPS)
    return jnp.asarray((group[:, None] == group[None, :]).astype(np.float32))


def frames_spec(*rest, first=0, count=4, last=1):
    return pl.BlockSpec(
        (count,) + rest,
        lambda step: (first // count + jnp.minimum(step, last),) + (0,) * len(rest),
    )


def make_hidden(place, peers, act, cot, low, high, gain, bias):
    wide = (ROWS + 2, COLS, CHAN)
    return pl.pallas_call(
        hidden_kernel,
        out_shape=(
            jax.ShapeDtypeStruct((SLOTS,) + wide, bf16),
            jax.ShapeDtypeStruct((2,) + wide, bf16),
            jax.ShapeDtypeStruct((2,) + wide, bf16),
            jax.ShapeDtypeStruct((SLOTS, CHAN), f32),
            jax.ShapeDtypeStruct((SLOTS, CHAN), f32),
        ),
        grid=(2,),
        in_specs=[
            SMEM_SPEC,
            whole(peers.shape),
            whole((CHAN, CHAN)),
            frames_spec(ROWS, COLS, CHAN),
            frames_spec(1, COLS, CHAN),
            frames_spec(1, COLS, CHAN),
            frames_spec(ROWS, COLS, CHAN, count=2, last=0),
            frames_spec(1, COLS, CHAN, first=SLOTS, count=2, last=0),
            frames_spec(1, COLS, CHAN, first=SLOTS, count=2, last=0),
            whole((1, CHAN)),
            whole((1, CHAN)),
        ],
        out_specs=(
            frames_spec(*wide),
            whole((2,) + wide),
            whole((2,) + wide),
            whole((SLOTS, CHAN)),
            whole((SLOTS, CHAN)),
        ),
        compiler_params=VMEM_LIMIT,
        cost_estimate=cost(40 * POS * CHAN, 5 << 20),
        name="make_hidden",
    )(place, peers, same_group(), act, low, high, cot, low, high, gain, bias)


def weight_terms(place, hidden, other, even, odd, cot, other_cot):
    in_vmem = pl.BlockSpec(memory_space=pltpu.VMEM)
    pair = (2, ROWS + 2, COLS, CHAN)
    return pl.pallas_call(
        weight_kernel,
        out_shape=(
            jax.ShapeDtypeStruct((CHIPS, 3 * PIECE, LANES), bf16),
            jax.ShapeDtypeStruct(pair, bf16),
        ),
        in_specs=[SMEM_SPEC] + [in_vmem] * 6,
        out_specs=(pl.BlockSpec(memory_space=pl.ANY), in_vmem),
        scratch_shapes=[
            pltpu.VMEM(pair, bf16),
            pltpu.VMEM((WIDE, 2 * (SLOTS + 2) * CELLS), bf16),
            pltpu.VMEM((2 * POS, 3 * TILE), bf16),
            pltpu.VMEM((9 * WIDE, TILE), f32),
            pltpu.VMEM((CHIPS, 3 * PIECE, LANES), bf16),
            pltpu.SemaphoreType.DMA((3,)),
        ],
        compiler_params=VMEM_LIMIT,
        cost_estimate=cost(FLOPS, 12 << 20),
        name="weight_terms",
    )(place, hidden, other, even, odd, cot, other_cot)


def shift(values, axes, count, step):
    pairs = [(i, i + step) for i in range(count) if 0 <= i + step < count]
    return lax.ppermute(values, axes, pairs)


def swap_cores(values):
    return lax.ppermute(values, "core", [(0, 1), (1, 0)])


def per_group(first, second):
    grouped = jnp.concatenate([first, second], axis=0).reshape(2 * SLOTS, GROUPS, CHAN // GROUPS)
    return jnp.sum(grouped, axis=2)


def per_channel(grouped):
    return jnp.repeat(grouped, CHAN // GROUPS, axis=1)


def on_device(activations, frame_counts, norm_gain, norm_bias, conv_weight, cotangent):
    core = lax.axis_index("core")
    act = activations.reshape(POS, CHAN)
    gain, bias = norm_gain[None], norm_bias[None]

    sums, bottom, top = local_sums(activations, cotangent)
    peers = lax.all_to_all(sums, ROW_AXES, 0, 0)
    low = shift(bottom, ROW_AXES, 8, 1)
    high = shift(top, ROW_AXES, 8, -1)
    other_cot = swap_cores(cotangent)
    low, high, peers, other_cot = lax.optimization_barrier((low, high, peers, other_cot))

    tm = lax.axis_index(TM)
    count = frame_counts[tm]
    place = jnp.stack(
        [count, core, lax.axis_index(ROW_AXES), frame_counts[tm + 1 - 2 * core]]
    )
    wide_hidden, last_pair, head, mean, inv = make_hidden(
        place, peers, activations, cotangent, low, high, gain, bias
    )
    other_hidden = swap_cores(wide_hidden)
    even = lax.ppermute(last_pair, TM, [(i, i + 1) for i in range(1, 15, 2)])
    odd = lax.ppermute(last_pair, TM, [(i, i + 2) for i in range(1, 15, 2)])

    head = shift(head, TM, 16, -1)

    terms, before = weight_terms(
        place, wide_hidden, other_hidden, even, odd, cotangent, other_cot
    )
    terms, head = lax.optimization_barrier((terms, head))
    arrived = lax.all_to_all(terms, CHIP_AXES, 0, 0)

    low, high, _ = lax.optimization_barrier((low, high, terms))
    pre_grad, first_grad, second_grad = backward_conv(
        place, cotangent, low, high, head, conv_weight, act, mean, inv, gain, bias
    )
    sums = per_group(first_grad, second_grad)
    parts = [lax.ppermute(sums, "x", [(i, (i + k) % 4) for i in range(4)]) for k in range(1, 4)]

    block_out = forward_conv(place, before, wide_hidden, conv_weight, act)
    block_out, parts = lax.optimization_barrier((block_out, parts))
    block_out = block_out.reshape(activations.shape)
    sums = sums + parts[0] + parts[1] + parts[2]
    other = lax.ppermute(sums, "yhi", [(0, 1), (1, 0)])
    other, arrived = lax.optimization_barrier((other, arrived))
    total = jnp.sum(arrived.astype(f32), axis=0)
    sums = sums + other
    averages = per_channel(sums / CELL_COUNT)[:, None, None, :]
    averages = lax.optimization_barrier(averages)
    first_avg, second_avg = averages[:SLOTS], averages[SLOTS:]
    wide_inv = inv[:, None, None, :]
    centred = (activations.astype(f32) - mean[:, None, None, :]) * wide_inv
    norm_part = wide_inv * (
        pre_grad.reshape(activations.shape) - first_avg - centred * second_avg
    )
    live = (jnp.arange(SLOTS) < count)[:, None, None, None]
    input_grad = jnp.where(live, cotangent.astype(f32) + norm_part, 0.0)

    frame_total = 1 + 4 * ((16 - 1) * 3 // 2)
    grad_scale = 1.0 / math.sqrt(frame_total * 8 * ROWS * COLS)
    total = total * grad_scale
    shared = total[2 * PIECE :]
    parts = [
        jnp.concatenate(
            [total[k * PIECE : (k + 1) * PIECE], shared[:, k * 64 : (k + 1) * 64]], axis=1
        )
        for k in range(2)
    ]
    mine = jnp.where(core == 0, parts[0], parts[1])
    theirs = swap_cores(jnp.where(core == 0, parts[1], parts[0]))
    first = jnp.where(core == 0, mine, theirs)
    second = jnp.where(core == 0, theirs, mine)
    weight_grad = jnp.concatenate([first, second[:, LANES:], second[:, :LANES]], axis=1)
    return block_out, input_grad, weight_grad


def solution(mesh):
    fine = Mesh(mesh.devices.reshape(2, 4, 2, 2, 4), ALL_AXES)
    placed = P(TM, ROW_AXES, None, None)
    return jax.shard_map(
        on_device,
        mesh=fine,
        in_specs=(placed, P(), P(), P(), P(), placed),
        out_specs=(placed, placed, P(ALL_AXES, None)),
        check_vma=False,
    )
```

```python
import math

import jax
import jax.numpy as jnp
import numpy as np
from jax import lax
from jax.experimental import pallas as pl
from jax.experimental.pallas import tpu as pltpu
from jax.sharding import Mesh
from jax.sharding import PartitionSpec as P

GROUPS = 32
EPS = 1e-05
CHAN = 384
HALF = CHAN // 2
SLOTS = 8
ROWS = 4
COLS = 32
CELLS = ROWS * COLS
POS = SLOTS * CELLS
WIDE = 3 * CHAN
PIECE = 81
DEVICES = 128
SENT = PIECE + (PIECE + 1) // 2
LANES = 128
WIDE_CELLS = (ROWS + 2) * COLS
CELL_COUNT = 8 * CELLS * (CHAN // GROUPS)
TILE = 256

TM = ("ylo", "z", "core")
ROW_AXES = ("yhi", "x")
ALL_AXES = TM + ROW_AXES

bf16 = jnp.bfloat16
f32 = jnp.float32
VMEM_LIMIT = pltpu.CompilerParams(vmem_limit_bytes=64 * 1024 * 1024)


def from_left(values):
    col = lax.broadcasted_iota(jnp.int32, values.shape, 0) % COLS
    return jnp.where(col == 0, 0.0, pltpu.roll(values, 1, 0))


def from_right(values):
    col = lax.broadcasted_iota(jnp.int32, values.shape, 0) % COLS
    return jnp.where(col == COLS - 1, 0.0, pltpu.roll(values, values.shape[0] - 1, 0))


def tap_products(x_ref, w_ref, acc, back):
    step = pl.program_id(0)
    weights = w_ref[...]
    pieces = []
    for b in range(3):
        at = (2 - step, 2 - b) if back else (step, b)
        pieces.append(x_ref[pl.ds(at[0], SLOTS), pl.ds(at[1], ROWS)].reshape(POS, CHAN))
    left = jnp.concatenate(pieces, axis=1)
    if back:
        right = jnp.concatenate([weights[b * WIDE : (b + 1) * WIDE] for b in range(3)], axis=1)
        dims = (((1,), (1,)), ((), ()))
    else:
        right = jnp.concatenate(
            [
                jnp.concatenate(
                    [weights[(b * 3 + c) * CHAN : (b * 3 + c + 1) * CHAN] for c in range(3)], axis=1
                )
                for b in range(3)
            ],
            axis=0,
        )
        dims = (((1,), (0,)), ((), ()))
    product = lax.dot_general(left, right, dims, preferred_element_type=f32)

    @pl.when(step == 0)
    def _():
        acc[...] = product

    @pl.when(step > 0)
    def _():
        acc[...] += product


def forward_kernel(place_ref, before_ref, hidden_ref, w_ref, act_ref, out_ref, x, acc):
    @pl.when(pl.program_id(0) == 0)
    def _():
        x[:2] = before_ref[...]
        x[2:] = hidden_ref[...]

    tap_products(x, w_ref, acc, False)

    @pl.when(pl.program_id(0) == 2)
    def _():
        for frame in range(SLOTS):
            rows = slice(frame * CELLS, (frame + 1) * CELLS)
            conv = (
                acc[rows, CHAN : 2 * CHAN]
                + from_left(acc[rows, :CHAN])
                + from_right(acc[rows, 2 * CHAN :])
            )
            total = act_ref[rows].astype(f32) + conv
            out_ref[rows] = jnp.where(frame < place_ref[0], total, 0.0).astype(bf16)


def backward_kernel(
    place_ref,
    cot_ref,
    low_ref,
    high_ref,
    head_ref,
    w_ref,
    act_ref,
    mean_ref,
    inv_ref,
    gain_ref,
    bias_ref,
    out_ref,
    first_ref,
    second_ref,
    x,
    acc,
):
    @pl.when(pl.program_id(0) == 0)
    def _():
        count = place_ref[0]
        for frame in range(SLOTS):

            @pl.when(frame < count)
            def _(frame=frame):
                x[frame, 0] = low_ref[SLOTS + frame, 0]
                x[frame, 1 : 1 + ROWS] = cot_ref[frame]
                x[frame, 1 + ROWS] = high_ref[SLOTS + frame, 0]

            @pl.when(frame >= count)
            def _(frame=frame):
                x[frame] = jnp.zeros((ROWS + 2, COLS, CHAN), bf16)

        x[SLOTS:] = jnp.zeros((2, ROWS + 2, COLS, CHAN), bf16)
        x[pl.ds(count, 2)] = head_ref[...]

    tap_products(x, w_ref, acc, True)

    @pl.when(pl.program_id(0) == 2)
    def _():
        gain = gain_ref[...]
        bias = bias_ref[...]
        for frame in range(SLOTS):
            rows = slice(frame * CELLS, (frame + 1) * CELLS)
            grad = (
                acc[rows, CHAN : 2 * CHAN]
                + from_right(acc[rows, :CHAN])
                + from_left(acc[rows, 2 * CHAN :])
            )
            centred = (act_ref[rows].astype(f32) - mean_ref[frame : frame + 1]) * inv_ref[
                frame : frame + 1
            ]
            pre_act = centred * gain + bias
            gate = jax.nn.sigmoid(pre_act)
            pre_grad = grad * gate * (1.0 + pre_act * (1.0 - gate)) * gain
            out_ref[rows] = pre_grad
            first_ref[frame : frame + 1] = jnp.sum(pre_grad, axis=0, keepdims=True)
            second_ref[frame : frame + 1] = jnp.sum(pre_grad * centred, axis=0, keepdims=True)


READY = ((0, 42), (42, 85), (85, 128))


def weight_kernel(
    place_ref,
    hidden_ref,
    other_ref,
    even_ref,
    odd_ref,
    cot_ref,
    other_cot_ref,
    out_ref,
    before_ref,
    other_before,
    turned,
    right,
    sums,
    packed,
    sems,
):
    core = place_ref[1]

    def last_two(ref, count, to_ref):
        @pl.when(count >= 2)
        def _():
            to_ref[...] = ref[pl.ds(jnp.maximum(count - 2, 0), 2)]

        @pl.when(count < 2)
        def _():
            to_ref[0] = jnp.zeros((ROWS + 2, COLS, CHAN), bf16)
            to_ref[1] = ref[0]

    @pl.when(core == 0)
    def _():
        before_ref[...] = even_ref[...]
        last_two(hidden_ref, place_ref[0], other_before)

    @pl.when(core == 1)
    def _():
        other_before[...] = odd_ref[...]
        last_two(other_ref, place_ref[3], before_ref)

    def turn(ref, f, column):
        for b in range(3):
            values = ref[f, b : b + ROWS].reshape(CELLS, CHAN)
            turned[b * CHAN : (b + 1) * CHAN, pl.ds(pl.multiple_of(column, CELLS), CELLS)] = values.T

    for block, (early, late) in enumerate(((before_ref, hidden_ref), (other_before, other_ref))):
        base = block * (SLOTS + 2) * CELLS
        for f in range(2):
            turn(early, f, base + f * CELLS)

        def turn_late(f, carry, late=late, base=base):
            turn(late, f, base + (f + 2) * CELLS)
            return carry

        lax.fori_loop(0, SLOTS, turn_late, 0, unroll=True)

    left_lanes = lax.broadcasted_iota(jnp.int32, (CELLS, LANES), 1) < LANES // 2

    def move(f, carry):
        for block, ref in enumerate((cot_ref, other_cot_ref)):
            values = ref[f].reshape(CELLS, CHAN).astype(f32)
            values = jnp.where(f < place_ref[3 * block], values, 0.0)
            middle = values[:, LANES : 2 * LANES]
            swapped = pltpu.roll(middle, LANES // 2, 1)
            first = core == 0
            outer = jnp.where(first, values[:, :LANES], values[:, 2 * LANES :])
            inner = jnp.where(left_lanes == first, middle, swapped)
            chosen = jnp.concatenate([outer, inner], axis=1)
            rows = pl.ds(pl.multiple_of(block * POS + f * CELLS, CELLS), CELLS)
            for c, moved in enumerate((from_right(chosen), chosen, from_left(chosen))):
                right[rows, c * TILE : (c + 1) * TILE] = moved.astype(bf16)
        return carry

    lax.fori_loop(0, SLOTS, move, 0, unroll=True)

    short = SENT - PIECE
    upper = lax.broadcasted_iota(jnp.int32, (short, LANES), 1) >= LANES // 2
    copies = []
    for a in range(3):
        window = jnp.concatenate(
            [
                turned[:, start : start + POS]
                for block in range(2)
                for start in [(block * (SLOTS + 2) + a) * CELLS]
            ],
            axis=1,
        )
        product = jnp.dot(window, right[...], preferred_element_type=f32)
        for b in range(3):
            for c in range(3):
                at = ((a * 3 + b) * 3 + c) * CHAN
                sums[at : at + CHAN] = product[
                    b * CHAN : (b + 1) * CHAN, c * TILE : (c + 1) * TILE
                ]
        for device in range(*READY[a]):
            piece = sums[device * PIECE : (device + 1) * PIECE]
            inner = piece[:, LANES:]
            block = jnp.concatenate(
                [piece[:, :LANES], jnp.where(upper, inner[PIECE - short :], inner[:short])], axis=0
            )
            packed[device] = block.astype(bf16)
        chips = pl.ds(READY[a][0], READY[a][1] - READY[a][0])
        copies.append(pltpu.make_async_copy(packed.at[chips], out_ref.at[chips], sems.at[a]))
        copies[-1].start()
    for copy in copies:
        copy.wait()


def sums_kernel(act_ref, cot_ref, out_ref, bottom_ref, top_ref):
    firsts, seconds = [], []
    for frame in range(SLOTS):
        values = act_ref[frame].reshape(CELLS, CHAN).astype(f32)
        firsts.append(jnp.sum(values, axis=0, keepdims=True))
        seconds.append(jnp.sum(values * values, axis=0, keepdims=True))
    both = jnp.concatenate(firsts + seconds, axis=0)
    for peer in range(8):
        out_ref[peer] = both
    for first, ref in ((0, act_ref), (SLOTS, cot_ref)):
        bottom_ref[first : first + SLOTS] = ref[:, ROWS - 1 :]
        top_ref[first : first + SLOTS] = ref[:, :1]


def group_means(sums, same_ref):
    return jnp.dot(
        sums, same_ref[...], precision=lax.Precision.HIGHEST, preferred_element_type=f32
    ) * (1.0 / CELL_COUNT)


def hidden_kernel(
    place_ref,
    peers_ref,
    same_ref,
    act_ref,
    low_ref,
    high_ref,
    cot_ref,
    cot_low_ref,
    cot_high_ref,
    gain_ref,
    bias_ref,
    hidden_ref,
    pair_ref,
    head_ref,
    mean_ref,
    inv_ref,
):
    step = pl.program_id(0)
    count, row_place = place_ref[0], place_ref[2]

    @pl.when(step == 0)
    def _():
        total = peers_ref[0]
        for peer in range(1, 8):
            total = total + peers_ref[peer]
        stats = group_means(total, same_ref)
        mean_ref[...] = stats[:SLOTS]
        inv_ref[...] = lax.rsqrt(stats[SLOTS:] - stats[:SLOTS] * stats[:SLOTS] + EPS)
        pair_ref[0] = jnp.zeros((ROWS + 2, COLS, CHAN), bf16)
        head_ref[:, :1] = cot_low_ref[...]
        head_ref[:, 1 : 1 + ROWS] = cot_ref[...]
        head_ref[:, 1 + ROWS :] = cot_high_ref[...]

    gain = gain_ref[...]
    bias = bias_ref[...]
    for k in range(4):
        frame = step * 4 + k
        live = frame < count
        mean = mean_ref[pl.ds(frame, 1)]
        inv = inv_ref[pl.ds(frame, 1)]

        def activated(values, keep, mean=mean, inv=inv):
            pre_act = (values.astype(f32) - mean) * inv * gain + bias
            return jnp.where(keep, pre_act * jax.nn.sigmoid(pre_act), 0.0).astype(bf16)

        hidden = activated(act_ref[k].reshape(CELLS, CHAN), live)
        hidden_ref[k, 1 : 1 + ROWS] = hidden.reshape(ROWS, COLS, CHAN)
        hidden_ref[k, 0] = activated(low_ref[k, 0], live & (row_place > 0))
        hidden_ref[k, 1 + ROWS] = activated(high_ref[k, 0], live & (row_place < 7))
        for late in range(2):

            @pl.when(frame == count - 2 + late)
            def _(k=k, late=late):
                pair_ref[late] = hidden_ref[k]


def whole(shape):
    return pl.BlockSpec(shape, lambda step: (0,) * len(shape))


def cost(flops, moved):
    return pl.CostEstimate(flops=flops, bytes_accessed=moved, transcendentals=0)


FLOPS = 2 * POS * 27 * CHAN * CHAN
TAPS_SPEC = pl.BlockSpec((3 * WIDE, CHAN), lambda step: (step, 0))


def forward_conv(place, before, hidden, weights, act):
    return pl.pallas_call(
        forward_kernel,
        out_shape=jax.ShapeDtypeStruct((POS, CHAN), bf16),
        grid=(3,),
        in_specs=[
            SMEM_SPEC,
            whole(before.shape),
            whole(hidden.shape),
            TAPS_SPEC,
            whole(act.shape),
        ],
        out_specs=whole((POS, CHAN)),
        scratch_shapes=[
            pltpu.VMEM((SLOTS + 2, ROWS + 2, COLS, CHAN), bf16),
            pltpu.VMEM((POS, WIDE), f32),
        ],
        compiler_params=VMEM_LIMIT,
        cost_estimate=cost(FLOPS, 12 << 20),
        name="forward_conv",
    )(place, before, hidden, weights, act)


def backward_conv(place, cot, low, high, head, weights, act, mean, inv, gain, bias):
    smalls = [mean, inv, gain, bias]
    return pl.pallas_call(
        backward_kernel,
        out_shape=(
            jax.ShapeDtypeStruct((POS, CHAN), f32),
            jax.ShapeDtypeStruct((SLOTS, CHAN), f32),
            jax.ShapeDtypeStruct((SLOTS, CHAN), f32),
        ),
        grid=(3,),
        in_specs=[SMEM_SPEC]
        + [whole(v.shape) for v in (cot, low, high, head)]
        + [TAPS_SPEC, whole(act.shape)]
        + [whole(v.shape) for v in smalls],
        out_specs=(whole((POS, CHAN)), whole((SLOTS, CHAN)), whole((SLOTS, CHAN))),
        scratch_shapes=[
            pltpu.VMEM((SLOTS + 2, ROWS + 2, COLS, CHAN), bf16),
            pltpu.VMEM((POS, WIDE), f32),
        ],
        compiler_params=VMEM_LIMIT,
        cost_estimate=cost(FLOPS, 12 << 20),
        name="backward_conv",
    )(place, cot, low, high, head, weights, act, *smalls)


def local_sums(act, cot):
    edge = jax.ShapeDtypeStruct((2 * SLOTS, 1, COLS, CHAN), bf16)
    return pl.pallas_call(
        sums_kernel,
        out_shape=(jax.ShapeDtypeStruct((8, 2 * SLOTS, CHAN), f32), edge, edge),
        compiler_params=VMEM_LIMIT,
        cost_estimate=cost(4 * POS * CHAN, 3 << 20),
        name="local_sums",
    )(act, cot)


SMEM_SPEC = pl.BlockSpec(memory_space=pltpu.SMEM)


def same_group():
    group = np.arange(CHAN) // (CHAN // GROUPS)
    return jnp.asarray((group[:, None] == group[None, :]).astype(np.float32))


def frames_spec(*rest, first=0, count=4, last=1):
    return pl.BlockSpec(
        (count,) + rest,
        lambda step: (first // count + jnp.minimum(step, last),) + (0,) * len(rest),
    )


def make_hidden(place, peers, act, cot, low, high, gain, bias):
    wide = (ROWS + 2, COLS, CHAN)
    return pl.pallas_call(
        hidden_kernel,
        out_shape=(
            jax.ShapeDtypeStruct((SLOTS,) + wide, bf16),
            jax.ShapeDtypeStruct((2,) + wide, bf16),
            jax.ShapeDtypeStruct((2,) + wide, bf16),
            jax.ShapeDtypeStruct((SLOTS, CHAN), f32),
            jax.ShapeDtypeStruct((SLOTS, CHAN), f32),
        ),
        grid=(2,),
        in_specs=[
            SMEM_SPEC,
            whole(peers.shape),
            whole((CHAN, CHAN)),
            frames_spec(ROWS, COLS, CHAN),
            frames_spec(1, COLS, CHAN),
            frames_spec(1, COLS, CHAN),
            frames_spec(ROWS, COLS, CHAN, count=2, last=0),
            frames_spec(1, COLS, CHAN, first=SLOTS, count=2, last=0),
            frames_spec(1, COLS, CHAN, first=SLOTS, count=2, last=0),
            whole((1, CHAN)),
            whole((1, CHAN)),
        ],
        out_specs=(
            frames_spec(*wide),
            whole((2,) + wide),
            whole((2,) + wide),
            whole((SLOTS, CHAN)),
            whole((SLOTS, CHAN)),
        ),
        compiler_params=VMEM_LIMIT,
        cost_estimate=cost(40 * POS * CHAN, 5 << 20),
        name="make_hidden",
    )(place, peers, same_group(), act, low, high, cot, low, high, gain, bias)


def weight_terms(place, hidden, other, even, odd, cot, other_cot):
    in_vmem = pl.BlockSpec(memory_space=pltpu.VMEM)
    pair = (2, ROWS + 2, COLS, CHAN)
    return pl.pallas_call(
        weight_kernel,
        out_shape=(
            jax.ShapeDtypeStruct((DEVICES, SENT, LANES), bf16),
            jax.ShapeDtypeStruct(pair, bf16),
        ),
        in_specs=[SMEM_SPEC] + [in_vmem] * 6,
        out_specs=(pl.BlockSpec(memory_space=pl.ANY), in_vmem),
        scratch_shapes=[
            pltpu.VMEM(pair, bf16),
            pltpu.VMEM((WIDE, 2 * (SLOTS + 2) * CELLS), bf16),
            pltpu.VMEM((2 * POS, 3 * TILE), bf16),
            pltpu.VMEM((9 * WIDE, TILE), f32),
            pltpu.VMEM((DEVICES, SENT, LANES), bf16),
            pltpu.SemaphoreType.DMA((3,)),
        ],
        compiler_params=VMEM_LIMIT,
        cost_estimate=cost(FLOPS, 12 << 20),
        name="weight_terms",
    )(place, hidden, other, even, odd, cot, other_cot)


def shift(values, axes, count, step):
    pairs = [(i, i + step) for i in range(count) if 0 <= i + step < count]
    return lax.ppermute(values, axes, pairs)


def swap_cores(values):
    return lax.ppermute(values, "core", [(0, 1), (1, 0)])


def per_group(first, second):
    grouped = jnp.concatenate([first, second], axis=0).reshape(2 * SLOTS, GROUPS, CHAN // GROUPS)
    return jnp.sum(grouped, axis=2)


def per_channel(grouped):
    return jnp.repeat(grouped, CHAN // GROUPS, axis=1)


def on_device(activations, frame_counts, norm_gain, norm_bias, conv_weight, cotangent):
    core = lax.axis_index("core")
    act = activations.reshape(POS, CHAN)
    gain, bias = norm_gain[None], norm_bias[None]

    sums, bottom, top = local_sums(activations, cotangent)
    peers = lax.all_to_all(sums, ROW_AXES, 0, 0)
    low = shift(bottom, ROW_AXES, 8, 1)
    high = shift(top, ROW_AXES, 8, -1)
    other_cot = swap_cores(cotangent)
    low, high, peers, other_cot = lax.optimization_barrier((low, high, peers, other_cot))

    tm = lax.axis_index(TM)
    count = frame_counts[tm]
    place = jnp.stack(
        [count, core, lax.axis_index(ROW_AXES), frame_counts[tm + 1 - 2 * core]]
    )
    wide_hidden, last_pair, head, mean, inv = make_hidden(
        place, peers, activations, cotangent, low, high, gain, bias
    )
    other_hidden = swap_cores(wide_hidden)
    even = lax.ppermute(last_pair, TM, [(i, i + 1) for i in range(1, 15, 2)])
    odd = lax.ppermute(last_pair, TM, [(i, i + 2) for i in range(1, 15, 2)])

    head = shift(head, TM, 16, -1)

    terms, before = weight_terms(
        place, wide_hidden, other_hidden, even, odd, cotangent, other_cot
    )
    terms, head = lax.optimization_barrier((terms, head))
    arrived = lax.all_to_all(terms, ALL_AXES, 0, 0)

    low, high, _ = lax.optimization_barrier((low, high, terms))
    pre_grad, first_grad, second_grad = backward_conv(
        place, cotangent, low, high, head, conv_weight, act, mean, inv, gain, bias
    )
    sums = per_group(first_grad, second_grad)
    parts = [lax.ppermute(sums, "x", [(i, (i + k) % 4) for i in range(4)]) for k in range(1, 4)]

    block_out = forward_conv(place, before, wide_hidden, conv_weight, act)
    block_out, parts = lax.optimization_barrier((block_out, parts))
    block_out = block_out.reshape(activations.shape)
    sums = sums + parts[0] + parts[1] + parts[2]
    other = lax.ppermute(sums, "yhi", [(0, 1), (1, 0)])
    other, arrived = lax.optimization_barrier((other, arrived))
    by_core = arrived.reshape(8, 2, 8, SENT, LANES)
    total = jnp.sum(by_core.astype(f32), axis=(0, 2))
    sums = sums + other
    averages = per_channel(sums / CELL_COUNT)[:, None, None, :]
    first_avg, second_avg = averages[:SLOTS], averages[SLOTS:]
    wide_inv = inv[:, None, None, :]
    centred = (activations.astype(f32) - mean[:, None, None, :]) * wide_inv
    norm_part = wide_inv * (
        pre_grad.reshape(activations.shape) - first_avg - centred * second_avg
    )
    live = (jnp.arange(SLOTS) < count)[:, None, None, None]
    input_grad = jnp.where(live, cotangent.astype(f32) + norm_part, 0.0)

    frame_total = 1 + 4 * ((16 - 1) * 3 // 2)
    grad_scale = 1.0 / math.sqrt(frame_total * 8 * ROWS * COLS)
    total = total * grad_scale
    outer = total[:, :PIECE]
    inner = jnp.concatenate(
        [total[:, PIECE:, : LANES // 2], total[:, PIECE + 1 :, LANES // 2 :]], axis=1
    )
    weight_grad = jnp.concatenate([outer[0], inner[0], inner[1], outer[1]], axis=1)
    return block_out, input_grad, weight_grad


def solution(mesh):
    fine = Mesh(mesh.devices.reshape(2, 4, 2, 2, 4), ALL_AXES)
    placed = P(TM, ROW_AXES, None, None)
    return jax.shard_map(
        on_device,
        mesh=fine,
        in_specs=(placed, P(), P(), P(), P(), placed),
        out_specs=(placed, placed, P(ALL_AXES, None)),
        check_vma=False,
    )
```
